128 devices in a mesh: sec: 32 (over x, y_lo, z), ax: 4 (over y_hi, core).
Axes of the slice: x: 4, y: 4 (y_hi: 2, y_lo: 2; y = y_hi * 2 + y_lo), z: 4, core: 2. Of those that a mesh axis runs over, the one named last changes fastest.
Arguments:
- material_labels: int32 [256, 512, 256], P('ax', 'sec'), may hold values from 0 to 3
- excitation_amplitudes: float32 [2, 256, 512, 256], P(None, 'ax', 'sec'), may hold values from -6 to 6
- opening_magnetic_gauge: float32 [256, 512, 256], P('ax', 'sec'), may hold values from -6 to 6
- prior_warming_excess: float32 [256, 256, 512], P('ax', 'sec'), may hold values from -6 to 6
Outputs:
- closing_magnetic_gauge: float32 [256, 512, 256], P('ax', 'sec')
- dissipation_accumulated: float32 [256, 512, 256], P('ax', 'sec')
- temperature: float32 [256, 256, 512], P('ax', 'sec')
The draws below stay inside these ranges and needn't reach their ends.
Inputs may be any that keep to these rules, and one draw needn't show every extreme that they name: `material_labels`: 0 iron, 1 copper, 2 air, 3 magnet.
All inputs are finite; a program needn't handle non-finite values.
Results may differ from the reference program's by a relative error of at most 0.00002.
Values sent between devices are 32-bit elements; how exact they have to be, the bound alone decides.
No kernel may reach another device: no remote copies, remote signals or barrier semaphores. Data moves between devices by JAX's collectives and lax.ppermute only.
A program may use at most 128 MiB of HBM per device.

```python
import jax
import jax.numpy as jnp
from jax import lax

SPOKEWISE_COUNT = 256
SAMPLES = 16
SWEEPS = 2
ANGULAR_COUNT = 512
LENGTHWISE_COUNT = 256


def touch_ends(values, rng, low, top_value):
    longest = values.shape.index(max(values.shape))
    spots = []
    for shift in (0, 1):
        where = [jax.random.randint(jax.random.fold_in(rng, axis), (), 0, length) for axis, length in enumerate(values.shape)]
        where[longest] = (where[longest] + shift) % values.shape[longest]
        spots.append(tuple(where))
    return values.at[spots[0]].set(low).at[spots[1]].set(top_value)


def level_of(stream_key, dims, pieces, low, top_value):
    level = 1.0
    for dim, parts in pieces:
        draws = jax.random.uniform(jax.random.fold_in(jax.random.fold_in(stream_key, 6), dim), (parts,), jnp.float32, low / len(pieces), top_value / len(pieces))
        level = level * jnp.repeat(jnp.exp(draws), dims[dim] // parts).reshape((-1,) + (1,) * (len(dims) - 1 - dim))
    return level


def gaussian(key, dims, spread, reach, split=(), kind=jnp.bfloat16):
    gain = level_of(key, dims, split, -0.22, 0.18) if split else 1.0
    values = jax.random.normal(key, dims, jnp.float32) * spread * gain
    return jnp.minimum(jnp.maximum(values, -reach), reach).astype(kind)


def setup_inputs(seed: int = 0) -> dict:
    splits = jax.random.split(jax.random.key(seed), 5)
    return {
        "material_labels": touch_ends(jax.random.randint(splits[0], (LENGTHWISE_COUNT, ANGULAR_COUNT, SPOKEWISE_COUNT), 0, 4), jax.random.fold_in(splits[0], 1), 0, 3).astype(jnp.int32),
        "excitation_amplitudes": gaussian(splits[1], (2, LENGTHWISE_COUNT, ANGULAR_COUNT, SPOKEWISE_COUNT), 1.0, 6.0, ((1, 4), (2, 32)), jnp.float32),
        "opening_magnetic_gauge": gaussian(splits[2], (LENGTHWISE_COUNT, ANGULAR_COUNT, SPOKEWISE_COUNT), 1.0, 6.0, ((0, 4), (1, 32)), jnp.float32),
        "prior_warming_excess": gaussian(splits[3], (LENGTHWISE_COUNT, SPOKEWISE_COUNT, ANGULAR_COUNT), 1.0, 6.0, ((0, 4), (1, 32)), jnp.float32),
    }


electrical_period = 32.0
reluct_table = (0.05, 0.24, 0.24, 0.2)
sigma_table = (0.3, 1.0, 0.0, 0.6)
kappa_table = (1.0, 1.5, 0.1, 0.4)
capacity_table = (3.0, 3.5, 0.5, 3.0)
drive_table = (0.0, 1.0, 0.0, 1.0)


def lookup(material_labels, table):
    result = jnp.zeros(material_labels.shape, jnp.float32)
    for index, value in enumerate(table):
        result = result + jnp.where(material_labels == index, jnp.float32(value), jnp.float32(0.0))
    return result


def advance(potential, induced_dissipation, azimuth_sum, reluct, sigma, driven, cosine_part, sine_part, sample):
    padded = jnp.pad(potential, ((0, 0), (0, 0), (1, 1)))
    radial_sum = padded[:, :, 2:] + padded[:, :, :-2]
    phase = (2.0 * jnp.pi / electrical_period) * sample.astype(jnp.float32)
    source = driven * (jnp.cos(phase) * cosine_part + jnp.sin(phase) * sine_part)
    fresh = potential + reluct * (azimuth_sum + radial_sum - 4.0 * potential) + source
    change = fresh - potential
    return fresh, induced_dissipation + sigma * change * change


def damping_weight(warmth_distribution, conduction_coupling, earlier_iterate, specific_warmth_store, induced_dissipation, adjacent_couples):
    energy_stream = jnp.zeros_like(warmth_distribution)
    main_entries = specific_warmth_store
    for adjacent_warmth, other_cond in adjacent_couples:
        boundary_surface = 0.5 * (conduction_coupling + other_cond)
        energy_stream = energy_stream + boundary_surface * (adjacent_warmth - warmth_distribution)
        main_entries = main_entries + boundary_surface
    mismatch_amount = specific_warmth_store * (warmth_distribution - earlier_iterate) - energy_stream - induced_dissipation
    return warmth_distribution - mismatch_amount / main_entries


def padded_pairs(gathered_arrays, dimension_label):
    widths = [(0, 0)] * gathered_arrays.ndim
    widths[dimension_label] = (1, 1)
    padded = jnp.pad(gathered_arrays, widths)
    size = gathered_arrays.shape[dimension_label]
    lower = lax.slice_in_dim(padded, 0, size, axis=dimension_label)
    upper = lax.slice_in_dim(padded, 2, size + 2, axis=dimension_label)
    return [(lower[0], lower[1]), (upper[0], upper[1])]


def reference(material_labels, excitation_amplitudes, opening_magnetic_gauge, prior_warming_excess):
    reluct = lookup(material_labels, reluct_table)
    sigma = lookup(material_labels, sigma_table)
    driven = lookup(material_labels, drive_table)

    def turn(sample, carry):
        potential, induced_dissipation = carry
        azimuth_sum = jnp.roll(potential, 1, 1) + jnp.roll(potential, -1, 1)
        return advance(potential, induced_dissipation, azimuth_sum, reluct, sigma, driven, excitation_amplitudes[0], excitation_amplitudes[1], sample)

    closing_magnetic_gauge, dissipation_accumulated = lax.fori_loop(0, SAMPLES, turn, (opening_magnetic_gauge, jnp.zeros_like(opening_magnetic_gauge)))
    conductivity_coefficient = jnp.swapaxes(lookup(material_labels, kappa_table), 1, 2)
    specific_warmth_store = jnp.swapaxes(lookup(material_labels, capacity_table), 1, 2)
    induced_dissipation = jnp.swapaxes(dissipation_accumulated, 1, 2)
    warmth_distribution = prior_warming_excess
    for sweep_index in range(SWEEPS):
        conduction_coupling = conductivity_coefficient * (1.0 + 0.5 * jnp.tanh(warmth_distribution))
        gathered_arrays = jnp.stack([warmth_distribution, conduction_coupling])
        adjacent_couples = padded_pairs(gathered_arrays, 1) + padded_pairs(gathered_arrays, 2)
        adjacent_couples = adjacent_couples + [(jnp.roll(warmth_distribution, 1, 2), jnp.roll(conduction_coupling, 1, 2)), (jnp.roll(warmth_distribution, -1, 2), jnp.roll(conduction_coupling, -1, 2))]
        warmth_distribution = damping_weight(warmth_distribution, conduction_coupling, prior_warming_excess, specific_warmth_store, induced_dissipation, adjacent_couples)
    return closing_magnetic_gauge, dissipation_accumulated, warmth_distribution
```

```python
import functools
import math

import jax
import jax.numpy as jnp
from jax import lax
from jax.experimental import pallas as pl
from jax.experimental.pallas import tpu as pltpu
from jax.sharding import PartitionSpec as P

SAMPLES = 16
PERIOD = 32
WIDTHS = (4, 4, 4, 4)
KMAX = max(WIDTHS)
CH = KMAX - 1

F32 = jnp.float32
AX, AZ, RAD, ANG = 64, 16, 256, 512
SEC = 32
RL = RAD // SEC
G = 8
NG = AX // G
REGION = 16


def _params(mib=None):
    return pltpu.CompilerParams(vmem_limit_bytes=(mib or 24) * 2**20)


def _sds(*shape):
    return jax.ShapeDtypeStruct(shape, F32)


def _reluct(lab):
    return jnp.where(lab == 0, 0.05, jnp.where(lab == 3, 0.2, 0.24)).astype(F32)


def _sigma(lab):
    return jnp.where(lab == 0, 0.3, jnp.where(lab == 1, 1.0, jnp.where(lab == 2, 0.0, 0.6))).astype(F32)


def _driven(lab, x):
    return jnp.where((lab == 1) | (lab == 3), x, 0.0)


def _edges_kernel(lab_ref, exc_ref, a_ref, low_ref, high_ref):
    lab = jnp.swapaxes(lab_ref[...], 0, 1)
    c = jnp.swapaxes(exc_ref[0], 0, 1)
    s = jnp.swapaxes(exc_ref[1], 0, 1)
    a = jnp.swapaxes(a_ref[...], 0, 1)
    w = WIDTHS[0]
    for out, ra, rc in ((low_ref, 0, 0), (high_ref, AZ - w, AZ - CH)):
        out[0:w] = a[ra : ra + w]
        lb = lab[rc : rc + CH]
        out[w : w + CH] = _reluct(lb)
        out[w + CH : w + 2 * CH] = _driven(lb, c[rc : rc + CH])
        out[w + 2 * CH : w + 3 * CH] = _driven(lb, s[rc : rc + CH])


def _edges(labels, exc, a):
    n = WIDTHS[0] + 3 * CH
    nat = pl.BlockSpec((G, AZ, RAD), lambda i: (i, 0, 0))
    out = pl.BlockSpec((n, G, RAD), lambda i: (0, i, 0))
    return pl.pallas_call(
        _edges_kernel,
        grid=(NG,),
        in_specs=[nat, pl.BlockSpec((2, G, AZ, RAD), lambda i: (0, i, 0, 0)), nat],
        out_specs=[out, out],
        out_shape=[_sds(n, AX, RAD)] * 2,
        compiler_params=_params(),
        name="edge_layers",
    )(labels, exc, a)


def _prepare_kernel(lab_ref, exc_ref, a_ref, a_out, nu_out, oc_out, os_out, lt_out):
    lab = lab_ref[...]
    lt_out[...] = jnp.transpose(lab.astype(F32).reshape(G * AZ, RAD)).reshape(SEC, 1, RL, G * AZ)
    lab = jnp.swapaxes(lab, 0, 1)
    a_out[...] = jnp.swapaxes(a_ref[...], 0, 1)
    nu_out[...] = _reluct(lab)
    oc_out[...] = _driven(lab, jnp.swapaxes(exc_ref[0], 0, 1))
    os_out[...] = _driven(lab, jnp.swapaxes(exc_ref[1], 0, 1))


def _prepare(labels, exc, a):
    nat = pl.BlockSpec((G, AZ, RAD), lambda i: (i, 0, 0))
    tr = pl.BlockSpec((AZ, G, RAD), lambda i: (0, i, 0))
    return pl.pallas_call(
        _prepare_kernel,
        grid=(NG,),
        in_specs=[nat, pl.BlockSpec((2, G, AZ, RAD), lambda i: (0, i, 0, 0)), nat],
        out_specs=[tr] * 4 + [pl.BlockSpec((SEC, 1, RL, G * AZ), lambda i: (0, i, 0, 0))],
        out_shape=[_sds(AZ, AX, RAD)] * 4 + [_sds(SEC, NG, RL, G * AZ)],
        compiler_params=_params(),
        name="prepare",
    )(labels, exc, a)


def _advance(first, width, a_rows, nu_of, oc_of, os_of, q_ref, bufs, fresh_q):
    half = RAD // 2
    lane = lax.broadcasted_iota(jnp.int32, (G, half), 1)
    at_low, at_high = lane == 0, lane == half - 1

    def get(t, r):
        return a_rows(r) if t == 0 else bufs[(t - 1) % 2, r + KMAX]

    for t in range(width):
        phase = 2.0 * math.pi / PERIOD * (first + t)
        cc, ss = math.cos(phase), math.sin(phase)
        lo, hi = -width + 1 + t, AZ - 1 + width - 1 - t
        down, mid = get(t, lo - 1), get(t, lo)
        for r in range(lo, hi + 1):
            up = get(t, r + 1)
            m0, m1 = mid[:, :half], mid[:, half:]
            f0, f1 = pltpu.roll(m0, 1, 1), pltpu.roll(m1, 1, 1)
            b0, b1 = pltpu.roll(m0, half - 1, 1), pltpu.roll(m1, half - 1, 1)
            side0 = jnp.where(at_low, 0.0, f0) + jnp.where(at_high, b1, b0)
            side1 = jnp.where(at_low, f0, f1) + jnp.where(at_high, 0.0, b1)
            side = jnp.concatenate([side0, side1], axis=1)
            source = cc * oc_of(r) if ss == 0.0 else cc * oc_of(r) + ss * os_of(r)
            change = nu_of(r) * ((down + up) + side - 4.0 * mid) + source
            new = mid + change
            if 0 <= r < AZ:
                sq = change * change
                q_ref[r] = sq if (fresh_q and t == 0) else q_ref[r] + sq
            bufs[t % 2, r + KMAX] = new
            down, mid = mid, up


def _phase_kernel(first, width, nextw, last, *refs):
    refs = list(refs)
    a_ref, low_ref, high_ref, nu_ref, oc_ref, os_ref, clow_ref, chigh_ref = refs[:8]
    refs = refs[8:]
    fresh = first == 0
    q_in = None if fresh else refs.pop(0)
    if last:
        lab_ref, a_out, d_out, dt_out, bufs, q = refs
    else:
        a_out, q, e_low, e_high, bufs = refs
    if not fresh:
        q[...] = q_in[...]
    w0 = WIDTHS[0]

    def rows(r):
        if r < 0:
            return low_ref[width + r]
        if r >= AZ:
            return high_ref[r - AZ]
        return a_ref[r]

    def const(ref, k):
        def get(r):
            if r < 0:
                return clow_ref[w0 + k * CH + CH + r]
            if r >= AZ:
                return chigh_ref[w0 + k * CH + r - AZ]
            return ref[r]

        return get

    _advance(first, width, rows, const(nu_ref, 0), const(oc_ref, 1), const(os_ref, 2), q, bufs, fresh)
    end = (width - 1) % 2
    a = bufs[end, KMAX : KMAX + AZ]
    if last:
        a_out[...] = jnp.swapaxes(a, 0, 1)
        d = _sigma(lab_ref[...]) * jnp.swapaxes(q[...], 0, 1)
        d_out[...] = d
        dt_out[...] = jnp.transpose(d.reshape(G * AZ, RAD)).reshape(SEC, 1, RL, G * AZ)
    else:
        a_out[...] = a
        e_low[...] = a[0:nextw]
        e_high[...] = a[AZ - nextw :]


def _phase(index, a, low, high, nu, oc, os, clow, chigh, q, labels):
    first, width = sum(WIDTHS[:index]), WIDTHS[index]
    last = index == len(WIDTHS) - 1
    nextw = None if last else WIDTHS[index + 1]

    def tr(x):
        return pl.BlockSpec((x.shape[0], G, RAD), lambda i: (0, i, 0))

    ins = [a, low, high, nu, oc, os, clow, chigh] + ([] if index == 0 else [q])
    specs = [tr(x) for x in ins]
    nat = pl.BlockSpec((G, AZ, RAD), lambda i: (i, 0, 0))
    scratch = [pltpu.VMEM((2, AZ + 2 * KMAX, G, RAD), F32)]
    if last:
        ins.append(labels)
        specs.append(nat)
        outs = [_sds(AX, AZ, RAD), _sds(AX, AZ, RAD), _sds(SEC, NG, RL, G * AZ)]
        out_specs = [nat, nat, pl.BlockSpec((SEC, 1, RL, G * AZ), lambda i: (0, i, 0, 0))]
        scratch.append(pltpu.VMEM((AZ, G, RAD), F32))
    else:
        outs = [_sds(AZ, AX, RAD), _sds(AZ, AX, RAD), _sds(nextw, AX, RAD), _sds(nextw, AX, RAD)]
        out_specs = [tr(x) for x in outs]
    return pl.pallas_call(
        functools.partial(_phase_kernel, first, width, nextw, last),
        grid=(NG,),
        in_specs=specs,
        out_specs=out_specs,
        out_shape=outs,
        scratch_shapes=scratch,
        compiler_params=_params(),
        name=f"field_{index}",
    )(*ins)


def _gathered(x_ref):
    blk = lax.broadcasted_iota(jnp.int32, (RL, 128), 1) // REGION
    tiles = []
    for s in range(SEC // 8):
        x = [x_ref[s * 8 + j, 0] for j in range(8)]
        for b in (4, 2, 1):
            keep = (blk & b) == 0
            for j in range(8):
                if j & b == 0:
                    p, q = x[j], x[j + b]
                    x[j] = jnp.where(keep, p, pltpu.roll(q, b * REGION, 1))
                    x[j + b] = jnp.where(keep, pltpu.roll(p, 128 - b * REGION, 1), q)
        tiles.append(x)
    return [jnp.concatenate([t[q] for t in tiles], axis=1) for q in range(8)]


def _half_cond(lab, temp):
    k0 = jnp.where(lab == 0.0, 1.0, jnp.where(lab == 1.0, 1.5, jnp.where(lab == 2.0, 0.1, 0.4)))
    return (0.5 * k0) * (1.0 + 0.5 * jnp.tanh(temp))


def _capacity(lab):
    return jnp.where(lab == 1.0, 3.5, jnp.where(lab == 2.0, 0.5, 3.0)).astype(F32)


def _materials_kernel(x_ref, temp_ref, lab_out, h_out, in_out, out_out):
    planes = _gathered(x_ref)
    for q in range(8):
        lab = planes[q]
        t = temp_ref[q]
        h = _half_cond(lab, t)
        lab_out[q] = lab
        h_out[q] = h
        _radial_edges(in_out, out_out, q, t, h)


def _radial_edges(in_out, out_out, q, t, h):
    in_out[0, q : q + 1, :] = t[0:1]
    in_out[1, q : q + 1, :] = h[0:1]
    out_out[0, q : q + 1, :] = t[RL - 1 :]
    out_out[1, q : q + 1, :] = h[RL - 1 :]


_PLANES = pl.BlockSpec((G, RL, ANG), lambda i: (i, 0, 0))
_BLOCKS = pl.BlockSpec((SEC, 1, RL, G * AZ), lambda i: (0, i, 0, 0))
_RADIAL = pl.BlockSpec((2, G, ANG), lambda i: (0, i, 0))


def _materials(x, temp):
    return pl.pallas_call(
        _materials_kernel,
        grid=(NG,),
        in_specs=[_BLOCKS, _PLANES],
        out_specs=[_PLANES, _PLANES, _RADIAL, _RADIAL],
        out_shape=[_sds(AX, RL, ANG)] * 2 + [_sds(2, AX, ANG)] * 2,
        compiler_params=_params(),
        name="materials",
    )(x, temp)


def _first_kernel(x_ref, base_ref, gain_ref, lab_ref, d_out, temp_out, h_out, in_out, out_out):
    planes = _gathered(x_ref)
    for q in range(8):
        d = planes[q]
        t = base_ref[q] + d * gain_ref[q]
        h = _half_cond(lab_ref[q], t)
        d_out[q] = d
        temp_out[q] = t
        h_out[q] = h
        _radial_edges(in_out, out_out, q, t, h)


def _first(x, base, gain, lab):
    return pl.pallas_call(
        _first_kernel,
        grid=(NG,),
        in_specs=[_BLOCKS, _PLANES, _PLANES, _PLANES],
        out_specs=[_PLANES, _PLANES, _PLANES, _RADIAL, _RADIAL],
        out_shape=[_sds(AX, RL, ANG)] * 3 + [_sds(2, AX, ANG)] * 2,
        compiler_params=_params(),
        name="first_sweep",
    )(x, base, gain, lab)


def _faces(i, t_ref, h_ref, inner_ref, outer_ref, below_ref, above_ref):
    t, h = t_ref[i], h_ref[i]
    row = lax.broadcasted_iota(jnp.int32, (RL, ANG), 0)
    prev, following = jnp.maximum(i - 1, 0), jnp.minimum(i + 1, AX - 1)

    def others(ref, k, x):
        lower = jnp.where(i == 0, below_ref[k], ref[prev])
        upper = jnp.where(i == AX - 1, above_ref[k], ref[following])
        inward = jnp.where(row == 0, inner_ref[k, pl.ds(i, 1), :], pltpu.roll(x, 1, 0))
        outward = jnp.where(row == RL - 1, outer_ref[k, pl.ds(i, 1), :], pltpu.roll(x, RL - 1, 0))
        return lower, upper, inward, outward, pltpu.roll(x, 1, 1), pltpu.roll(x, ANG - 1, 1)

    flux, total = None, None
    for tn, hn in zip(others(t_ref, 0, t), others(h_ref, 1, h)):
        kf = h + hn
        term = kf * (tn - t)
        flux = term if flux is None else flux + term
        total = kf if total is None else total + kf
    return t, flux, total


def _ready_kernel(t_ref, h_ref, inner_ref, outer_ref, below_ref, above_ref, lab_ref, base_out, gain_out):
    def plane(i, _):
        t, flux, total = _faces(i, t_ref, h_ref, inner_ref, outer_ref, below_ref, above_ref)
        gain = 1.0 / (_capacity(lab_ref[i]) + total)
        base_out[i] = t + flux * gain
        gain_out[i] = gain
        return 0

    lax.fori_loop(0, AX, plane, 0)


def _second_kernel(t_ref, h_ref, inner_ref, outer_ref, below_ref, above_ref, lab_ref, prior_ref, d_ref, out):
    def plane(i, _):
        t, flux, total = _faces(i, t_ref, h_ref, inner_ref, outer_ref, below_ref, above_ref)
        cap = _capacity(lab_ref[i])
        mismatch = cap * (t - prior_ref[i]) - flux - d_ref[i]
        out[i] = t - mismatch / (cap + total)
        return 0

    lax.fori_loop(0, AX, plane, 0)


def _whole(kernel, n_out, name, *ins):
    return pl.pallas_call(
        kernel,
        out_shape=[_sds(AX, RL, ANG)] * n_out,
        compiler_params=_params(32),
        name=name,
    )(*ins)


def _ring(axis, x, step, closed):
    count = lax.axis_size(axis)
    if step > 0:
        perm = [(i, (i + 1) % count) for i in range(count if closed else count - 1)]
    else:
        perm = [((i + 1) % count, i) for i in range(count if closed else count - 1)]
    return lax.ppermute(x, axis, perm)


def _thermal_halo(t, h, inner_edge, outer_edge):
    inner = _ring("sec", outer_edge, 1, False)
    outer = _ring("sec", inner_edge, -1, False)
    below = _ring("ax", jnp.stack([t[-1], h[-1]]), 1, False)
    above = _ring("ax", jnp.stack([t[0], h[0]]), -1, False)
    return inner, outer, below, above


def shards(labels, exc, a0, prior):
    e_low, e_high = _edges(labels, exc, a0)
    clow = _ring("sec", e_high, 1, True)
    chigh = _ring("sec", e_low, -1, True)
    a, nu, oc, os, lt = _prepare(labels, exc, a0)
    lab_blocks = lax.all_to_all(lt, "sec", 0, 0)
    lab, h0, in0, out0 = _materials(lab_blocks, prior)
    halo0 = _thermal_halo(prior, h0, in0, out0)
    base, gain = _whole(_ready_kernel, 2, "first_ready", prior, h0, *halo0, lab)
    low, high, q = clow, chigh, None
    for index in range(len(WIDTHS)):
        if index:
            low = _ring("sec", e_high, 1, True)
            high = _ring("sec", e_low, -1, True)
        outs = _phase(index, a, low, high, nu, oc, os, clow, chigh, q, labels)
        if index < len(WIDTHS) - 1:
            a, q, e_low, e_high = outs
    closing, dissipation, dt = outs
    blocks = lax.all_to_all(dt, "sec", 0, 0)
    d, t1, h1, in1, out1 = _first(blocks, base, gain, lab)
    halo1 = _thermal_halo(t1, h1, in1, out1)
    (t2,) = _whole(_second_kernel, 1, "second_sweep", t1, h1, *halo1, lab, prior, d)
    return closing, dissipation, t2


def solution(mesh):
    spec = P("ax", "sec", None)
    return jax.shard_map(
        shards,
        mesh=mesh,
        in_specs=(spec, P(None, "ax", "sec", None), spec, spec),
        out_specs=(spec, spec, spec),
        check_vma=False,
    )
```

```python
import functools
import math

import jax
import jax.numpy as jnp
from jax import lax
from jax.experimental import pallas as pl
from jax.experimental.pallas import tpu as pltpu
from jax.sharding import PartitionSpec as P

SAMPLES = 16
PERIOD = 32
WIDTHS = (4, 4, 4, 4)
KMAX = max(WIDTHS)
W0 = WIDTHS[0]
C0 = W0 - 1
CH = KMAX - 1
FIRST = (C0, C0, C0 - 1 if KMAX > W0 else C0)
REST = tuple(CH - n for n in FIRST)

F32 = jnp.float32
AX, AZ, RAD, ANG = 64, 16, 256, 512
SEC = 32
RL = RAD // SEC
G = 8
NG = AX // G


def _params(mib=16):
    return pltpu.CompilerParams(vmem_limit_bytes=mib * 2**20)


def _sds(*shape):
    return jax.ShapeDtypeStruct(shape, F32)


def _cost(flops, nbytes):
    return pl.CostEstimate(flops=flops, bytes_accessed=nbytes, transcendentals=0)


def _loop(body):
    def step(g, _):
        body(g)
        return 0

    lax.fori_loop(0, NG, step, 0)


def _planes(g):
    return pl.ds(pl.multiple_of(g * G, G), G)


def _reluct(lab):
    return jnp.where(lab == 0, 0.05, jnp.where(lab == 3, 0.2, 0.24)).astype(F32)


def _sigma(lab):
    return jnp.where(lab == 0, 0.3, jnp.where(lab == 1, 1.0, jnp.where(lab == 2, 0.0, 0.6))).astype(F32)


def _driven(lab, x):
    return jnp.where((lab == 1) | (lab == 3), x, 0.0)


def _edges_kernel(lab_hbm, exc_hbm, a_hbm, low_ref, high_ref, lab_v, exc_v, a_v, sems):
    copies = []
    for g in range(NG):
        at = pl.ds(g * G, G)
        copies.append(
            [
                pltpu.make_async_copy(lab_hbm.at[at], lab_v.at[at], sems.at[g, 0]),
                pltpu.make_async_copy(exc_hbm.at[0, at], exc_v.at[0, at], sems.at[g, 1]),
                pltpu.make_async_copy(exc_hbm.at[1, at], exc_v.at[1, at], sems.at[g, 2]),
                pltpu.make_async_copy(a_hbm.at[at], a_v.at[at], sems.at[g, 3]),
            ]
        )
        for copy in copies[-1]:
            copy.start()
    for g in range(NG):
        for copy in copies[g]:
            copy.wait()
        at = pl.ds(g * G, G)
        lab = jnp.swapaxes(lab_v[at], 0, 1)
        c = jnp.swapaxes(exc_v[0, at], 0, 1)
        s = jnp.swapaxes(exc_v[1, at], 0, 1)
        a = jnp.swapaxes(a_v[at], 0, 1)
        for out, high in ((low_ref, False), (high_ref, True)):

            def edge(x, n):
                return x[AZ - n :] if high else x[:n]

            out[0:W0, g] = edge(a, W0)
            n1, n2, n3 = FIRST
            at1, at2 = W0 + n1, W0 + n1 + n2
            out[W0:at1, g] = _reluct(edge(lab, n1))
            out[at1:at2, g] = _driven(edge(lab, n2), edge(c, n2))
            out[at2 : at2 + n3, g] = _driven(edge(lab, n3), edge(s, n3))


def _edges(labels, exc, a):
    n = W0 + sum(FIRST)
    return pl.pallas_call(
        _edges_kernel,
        in_specs=[pl.BlockSpec(memory_space=pl.ANY)] * 3,
        out_shape=[_sds(n, NG, G, RAD)] * 2,
        scratch_shapes=[
            pltpu.VMEM((AX, AZ, RAD), jnp.int32),
            pltpu.VMEM((2, AX, AZ, RAD), F32),
            pltpu.VMEM((AX, AZ, RAD), F32),
            pltpu.SemaphoreType.DMA((NG, 4)),
        ],
        compiler_params=_params(56),
        cost_estimate=_cost(2**20, 6 * 2**20),
        name="edge_layers",
    )(labels, exc, a)


def _prepare_kernel(lab_ref, exc_ref, a_ref, a_out, nu_out, oc_out, os_out, *rest):
    def group(g):
        at = _planes(g)
        lab = jnp.swapaxes(lab_ref[at], 0, 1)
        a_out[:, g] = jnp.swapaxes(a_ref[at], 0, 1)
        nu = _reluct(lab)
        oc = _driven(lab, jnp.swapaxes(exc_ref[0, at], 0, 1))
        os = _driven(lab, jnp.swapaxes(exc_ref[1, at], 0, 1))
        nu_out[:, g] = nu
        oc_out[:, g] = oc
        os_out[:, g] = os
        to = 0
        for x, n, m in zip((nu, oc, os), FIRST, REST):
            if m:
                rest[0][to : to + m, g] = x[n : n + m]
                rest[1][to : to + m, g] = x[AZ - n - m : AZ - n]
                to += m

    _loop(group)


def _prepare(labels, exc, a):
    n = sum(REST)
    return pl.pallas_call(
        _prepare_kernel,
        out_shape=[_sds(AZ, NG, G, RAD)] * 4 + ([_sds(n, NG, G, RAD)] * 2 if n else []),
        compiler_params=_params(),
        cost_estimate=_cost(2**22, 8 * 2**20),
        name="prepare",
    )(labels, exc, a)


def _labels_kernel(lab_ref, lt_out):
    def group(g):
        lab = lab_ref[_planes(g)].astype(F32)
        lt_out[:, g] = jnp.transpose(lab.reshape(G * AZ, RAD)).reshape(SEC, RL, G * AZ)

    _loop(group)


def _turned_labels(labels):
    return pl.pallas_call(
        _labels_kernel,
        out_shape=_sds(SEC, NG, RL, G * AZ),
        compiler_params=_params(),
        cost_estimate=_cost(2**22, 2 * 2**20),
        name="turned_labels",
    )(labels)


def _advance(first, width, a_rows, nu_of, oc_of, os_of, add_square, bufs):
    half = RAD // 2
    lane = lax.broadcasted_iota(jnp.int32, (G, half), 1)
    at_low, at_high = lane == 0, lane == half - 1

    def get(t, r):
        return a_rows(r) if t == 0 else bufs[(t - 1) % 2, r + KMAX]

    for t in range(width):
        phase = 2.0 * math.pi / PERIOD * (first + t)
        cc, ss = math.cos(phase), math.sin(phase)
        lo, hi = -width + 1 + t, AZ - 1 + width - 1 - t
        down, mid = get(t, lo - 1), get(t, lo)
        for r in range(lo, hi + 1):
            up = get(t, r + 1)
            m0, m1 = mid[:, :half], mid[:, half:]
            f0, f1 = pltpu.roll(m0, 1, 1), pltpu.roll(m1, 1, 1)
            b0, b1 = pltpu.roll(m0, half - 1, 1), pltpu.roll(m1, half - 1, 1)
            side0 = jnp.where(at_low, 0.0, f0) + jnp.where(at_high, b1, b0)
            side1 = jnp.where(at_low, f0, f1) + jnp.where(at_high, 0.0, b1)
            side = jnp.concatenate([side0, side1], axis=1)
            source = cc * oc_of(r) if first + t == 0 else cc * oc_of(r) + ss * os_of(r)
            change = nu_of(r) * ((down + up) + side - 4.0 * mid) + source
            new = mid + change
            if 0 <= r < AZ:
                add_square(t, r, change * change)
            bufs[t % 2, r + KMAX] = new
            down, mid = mid, up


def _phase_kernel(first, width, nextw, last, *refs):
    refs = list(refs)
    a_ref, low_ref, high_ref, nu_ref, oc_ref, os_ref, clow_ref, chigh_ref = refs[:8]
    refs = refs[8:]
    fresh = first == 0
    if not fresh:
        if any(REST):
            rlow_ref, rhigh_ref = refs[:2]
            refs = refs[2:]
        q_in, refs = refs[0], refs[1:]
    if last:
        lab_ref, a_out, d_out, dt_out, bufs, q_ref = refs
    else:
        a_out, q_ref, e_low, e_high, bufs = refs

    def group(g):
        def rows(r):
            if r < 0:
                return low_ref[width + r, g]
            if r >= AZ:
                return high_ref[r - AZ, g]
            return a_ref[r, g]

        def const(ref, k):
            n, m = FIRST[k], REST[k]
            at, rest_at = W0 + sum(FIRST[:k]), sum(REST[:k])

            def get(r):
                if 0 <= r < AZ:
                    return ref[r, g]
                if r < 0:
                    return clow_ref[at + n + r, g] if r >= -n else rlow_ref[rest_at + n + m + r, g]
                r -= AZ
                return chigh_ref[at + r, g] if r < n else rhigh_ref[rest_at + r - n, g]

            return get

        def slot(r):
            return (r,) if last else (r, g)

        def add_square(t, r, sq):
            if t > 0:
                sq = q_ref[slot(r)] + sq
            elif not fresh:
                sq = q_in[r, g] + sq
            q_ref[slot(r)] = sq

        _advance(first, width, rows, const(nu_ref, 0), const(oc_ref, 1), const(os_ref, 2), add_square, bufs)
        a = bufs[(width - 1) % 2, KMAX : KMAX + AZ]
        if last:
            at = _planes(g)
            a_out[at] = jnp.swapaxes(a, 0, 1)
            d = _sigma(lab_ref[at]) * jnp.swapaxes(q_ref[...], 0, 1)
            d_out[at] = d
            dt_out[:, g] = jnp.transpose(d.reshape(G * AZ, RAD)).reshape(SEC, RL, G * AZ)
        else:
            a_out[:, g] = a
            e_low[:, g] = a[0:nextw]
            e_high[:, g] = a[AZ - nextw :]

    _loop(group)


def _phase(index, a, low, high, consts, first_halo, rest_halo, q, labels):
    first, width = sum(WIDTHS[:index]), WIDTHS[index]
    last = index == len(WIDTHS) - 1
    nextw = None if last else WIDTHS[index + 1]
    ins = [a, low, high, *consts, *first_halo] + ([*rest_halo, q] if index else [])
    scratch = [pltpu.VMEM((2, AZ + 2 * KMAX, G, RAD), F32)]
    if last:
        ins.append(labels)
        outs = [_sds(AX, AZ, RAD), _sds(AX, AZ, RAD), _sds(SEC, NG, RL, G * AZ)]
        scratch.append(pltpu.VMEM((AZ, G, RAD), F32))
    else:
        outs = [_sds(AZ, NG, G, RAD)] * 2 + [_sds(nextw, NG, G, RAD)] * 2
    return pl.pallas_call(
        functools.partial(_phase_kernel, first, width, nextw, last),
        out_shape=outs,
        scratch_shapes=scratch,
        compiler_params=_params(),
        cost_estimate=_cost(2**24, 2**23),
        name=f"field_{index}",
    )(*ins)


def _gathered(x_ref, g):
    blk = lax.broadcasted_iota(jnp.int32, (RL, 128), 1) // AZ
    tiles = []
    for s in range(SEC // 8):
        x = [x_ref[s * 8 + j, g] for j in range(8)]
        for b in (4, 2, 1):
            keep = (blk & b) == 0
            for j in range(8):
                if j & b == 0:
                    p, q = x[j], x[j + b]
                    x[j] = jnp.where(keep, p, pltpu.roll(q, b * AZ, 1))
                    x[j + b] = jnp.where(keep, pltpu.roll(p, 128 - b * AZ, 1), q)
        tiles.append(x)
    return [jnp.concatenate([t[q] for t in tiles], axis=1) for q in range(8)]


def _half_cond(lab, temp):
    k0 = jnp.where(lab == 0.0, 1.0, jnp.where(lab == 1.0, 1.5, jnp.where(lab == 2.0, 0.1, 0.4)))
    return (0.5 * k0) * (1.0 + 0.5 * jnp.tanh(temp))


def _capacity(lab):
    return jnp.where(lab == 1.0, 3.5, jnp.where(lab == 2.0, 0.5, 3.0)).astype(F32)


def _store_edges(g, q, t, h, in_out, out_out, lo_out, hi_out):
    for k, x in enumerate((t, h)):
        in_out[k, g, q : q + 1, :] = x[0:1]
        out_out[k, g, q : q + 1, :] = x[RL - 1 :]
        if q == 0:

            @pl.when(g == 0)
            def _():
                lo_out[k] = x

        if q == G - 1:

            @pl.when(g == NG - 1)
            def _():
                hi_out[k] = x


_EDGES = [_sds(2, NG, G, ANG)] * 2 + [_sds(2, RL, ANG)] * 2


def _materials_kernel(x_ref, temp_ref, lab_out, h_out, *edges):
    def group(g):
        planes = _gathered(x_ref, g)
        for q in range(G):
            lab = planes[q]
            t = temp_ref[g * G + q]
            h = _half_cond(lab, t)
            lab_out[g * G + q] = lab
            h_out[g * G + q] = h
            _store_edges(g, q, t, h, *edges)

    _loop(group)


def _materials(x, temp):
    return pl.pallas_call(
        _materials_kernel,
        out_shape=[_sds(AX, RL, ANG)] * 2 + _EDGES,
        compiler_params=_params(),
        cost_estimate=_cost(2**22, 2**22),
        name="materials",
    )(x, temp)


def _first_kernel(x_ref, base_ref, gain_ref, lab_ref, d_out, temp_out, h_out, *edges):
    def group(g):
        planes = _gathered(x_ref, g)
        for q in range(G):
            at = g * G + q
            d = planes[q]
            t = base_ref[at] + d * gain_ref[at]
            h = _half_cond(lab_ref[at], t)
            d_out[at] = d
            temp_out[at] = t
            h_out[at] = h
            _store_edges(g, q, t, h, *edges)

    _loop(group)


def _first(x, base, gain, lab):
    return pl.pallas_call(
        _first_kernel,
        out_shape=[_sds(AX, RL, ANG)] * 3 + _EDGES,
        compiler_params=_params(),
        cost_estimate=_cost(2**22, 2**22),
        name="first_sweep",
    )(x, base, gain, lab)


def _faces(g, q, t_ref, h_ref, inner_ref, outer_ref, below_ref, above_ref):
    i = g * G + q
    row = lax.broadcasted_iota(jnp.int32, (RL, ANG), 0)

    def others(ref, k, x):
        lower = ref[i - 1] if q else jnp.where(g == 0, below_ref[k], ref[jnp.maximum(i - 1, 0)])
        upper = ref[i + 1] if q < G - 1 else jnp.where(g == NG - 1, above_ref[k], ref[jnp.minimum(i + 1, AX - 1)])
        inward = jnp.where(row == 0, inner_ref[k, g, q : q + 1, :], pltpu.roll(x, 1, 0))
        outward = jnp.where(row == RL - 1, outer_ref[k, g, q : q + 1, :], pltpu.roll(x, RL - 1, 0))
        return lower, upper, inward, outward, pltpu.roll(x, 1, 1), pltpu.roll(x, ANG - 1, 1)

    t, h = t_ref[i], h_ref[i]
    flux, total = None, None
    for tn, hn in zip(others(t_ref, 0, t), others(h_ref, 1, h)):
        kf = h + hn
        term = kf * (tn - t)
        flux = term if flux is None else flux + term
        total = kf if total is None else total + kf
    return t, flux, total


def _ready_kernel(t_ref, h_ref, inner_ref, outer_ref, below_ref, above_ref, lab_ref, base_out, gain_out):
    def group(g):
        for q in range(G):
            i = g * G + q
            t, flux, total = _faces(g, q, t_ref, h_ref, inner_ref, outer_ref, below_ref, above_ref)
            gain = 1.0 / (_capacity(lab_ref[i]) + total)
            base_out[i] = t + flux * gain
            gain_out[i] = gain

    _loop(group)


def _second_kernel(t_ref, h_ref, inner_ref, outer_ref, below_ref, above_ref, lab_ref, prior_ref, d_ref, out):
    def group(g):
        for q in range(G):
            i = g * G + q
            t, flux, total = _faces(g, q, t_ref, h_ref, inner_ref, outer_ref, below_ref, above_ref)
            cap = _capacity(lab_ref[i])
            mismatch = cap * (t - prior_ref[i]) - flux - d_ref[i]
            out[i] = t - mismatch / (cap + total)

    _loop(group)


def _whole(kernel, n_out, name, *ins):
    return pl.pallas_call(
        kernel,
        out_shape=[_sds(AX, RL, ANG)] * n_out,
        compiler_params=_params(),
        cost_estimate=_cost(2**24, 2**23),
        name=name,
    )(*ins)


def _ring(axis, x, step, closed):
    count = lax.axis_size(axis)
    if step > 0:
        perm = [(i, (i + 1) % count) for i in range(count if closed else count - 1)]
    else:
        perm = [((i + 1) % count, i) for i in range(count if closed else count - 1)]
    return lax.ppermute(x, axis, perm)


def _around(low_edge, high_edge):
    return _ring("sec", high_edge, 1, True), _ring("sec", low_edge, -1, True)


def _thermal_halo(inner_edge, outer_edge, lo_plane, hi_plane):
    inner = _ring("sec", outer_edge, 1, False)
    outer = _ring("sec", inner_edge, -1, False)
    below = _ring("ax", hi_plane, 1, False)
    above = _ring("ax", lo_plane, -1, False)
    return inner, outer, below, above


def shards(labels, exc, a0, prior):
    first_halo = _around(*_edges(labels, exc, a0))
    lt = _turned_labels(labels)
    lab_blocks = lax.all_to_all(lt, "sec", 0, 0)
    a, nu, oc, os, *rest = _prepare(labels, exc, a0)
    rest_halo = _around(*rest) if rest else ()
    low, high = first_halo
    q = None
    for index in range(len(WIDTHS)):
        outs = _phase(index, a, low, high, (nu, oc, os), first_halo, rest_halo, q, labels)
        if index < len(WIDTHS) - 1:
            a, q, *edges = outs
            low, high = _around(*edges)
    closing, dissipation, dt = outs
    lab, h0, *edges = _materials(lab_blocks, prior)
    halo0 = _thermal_halo(*edges)
    base, gain = _whole(_ready_kernel, 2, "first_ready", prior, h0, *halo0, lab)
    blocks = lax.all_to_all(dt, "sec", 0, 0)
    d, t1, h1, *edges = _first(blocks, base, gain, lab)
    halo1 = _thermal_halo(*edges)
    (t2,) = _whole(_second_kernel, 1, "second_sweep", t1, h1, *halo1, lab, prior, d)
    return closing, dissipation, t2


def solution(mesh):
    spec = P("ax", "sec", None)
    return jax.shard_map(
        shards,
        mesh=mesh,
        in_specs=(spec, P(None, "ax", "sec", None), spec, spec),
        out_specs=(spec, spec, spec),
        check_vma=False,
    )
```

```python
import functools
import math

import jax
import jax.numpy as jnp
from jax import lax
from jax.experimental import pallas as pl
from jax.experimental.pallas import tpu as pltpu
from jax.sharding import PartitionSpec as P

SAMPLES = 16
PERIOD = 32
WIDTHS = (5, 4, 4, 3)
REACH = (5, 4, 4, 4)
PRIOR_AT = 2
H0 = REACH[0]
HMAX = max(REACH)
C = HMAX - 1
LAYERS = (C, C, C - 1)
AT = (H0, H0 + C, H0 + 2 * C)
NSEND = H0 + sum(LAYERS)

F32 = jnp.float32
AX, AZ, RAD, ANG = 64, 16, 256, 512
SEC = 32
RL = RAD // SEC
G = 8
NG = AX // G
ENDS = (0, NG - 1)
HALF = RAD // 2


def _params(mib=16):
    return pltpu.CompilerParams(vmem_limit_bytes=mib * 2**20)


def _sds(*shape):
    return jax.ShapeDtypeStruct(shape, F32)


def _cost(flops, nbytes):
    return pl.CostEstimate(flops=flops, bytes_accessed=nbytes, transcendentals=0)


def _loop(n, body):
    def step(i, _):
        body(i)
        return 0

    lax.fori_loop(0, n, step, 0)


def _planes(g):
    return pl.ds(pl.multiple_of(g * G, G), G)


def _reluct(lab):
    return jnp.where(lab == 0, 0.05, jnp.where(lab == 3, 0.2, 0.24)).astype(F32)


def _sigma(lab):
    return jnp.where(lab == 0, 0.3, jnp.where(lab == 1, 1.0, jnp.where(lab == 2, 0.0, 0.6))).astype(F32)


def _driven(lab, x):
    return jnp.where((lab == 1) | (lab == 3), x, 0.0)


def _half_cond(lab, temp):
    half_k0 = jnp.where(lab == 0, 0.5, jnp.where(lab == 1, 0.75, jnp.where(lab == 2, 0.05, 0.2)))
    return half_k0 * (1.0 + 0.5 * jnp.tanh(temp))


def _capacity(lab):
    return jnp.where(lab == 1, 3.5, jnp.where(lab == 2, 0.5, 3.0)).astype(F32)


def _send_layers(store, high, a, lab, c, s):
    def edge(x, n):
        return x[AZ - n :] if high else x[:n]

    store(0, edge(a, H0))
    store(AT[0], edge(lab, LAYERS[0]).astype(F32))
    store(AT[1], _driven(edge(lab, LAYERS[1]), edge(c, LAYERS[1])))
    store(AT[2], _driven(edge(lab, LAYERS[2]), edge(s, LAYERS[2])))


def _edges_kernel(lab_hbm, exc_hbm, a_hbm, low_ref, high_ref, lab_v, exc_v, a_v, sems):
    copies = []
    for g in range(NG):
        at = pl.ds(g * G, G)
        copies.append(
            [
                pltpu.make_async_copy(lab_hbm.at[at], lab_v.at[at], sems.at[g, 0]),
                pltpu.make_async_copy(exc_hbm.at[0, at], exc_v.at[0, at], sems.at[g, 1]),
                pltpu.make_async_copy(exc_hbm.at[1, at], exc_v.at[1, at], sems.at[g, 2]),
                pltpu.make_async_copy(a_hbm.at[at], a_v.at[at], sems.at[g, 3]),
            ]
        )
        for copy in copies[-1]:
            copy.start()

    def group(g, a, c, s, lab):
        for out, high in ((low_ref, False), (high_ref, True)):

            def store(k, x, out=out):
                out[k : k + x.shape[0], g] = x

            _send_layers(store, high, a, lab, c, s)

    for g in range(NG):
        for copy in copies[g]:
            copy.wait()
        at = pl.ds(g * G, G)
        group(g, *[jnp.swapaxes(x, 0, 1) for x in (a_v[at], exc_v[0, at], exc_v[1, at], lab_v[at])])


def _edges(labels, exc, a):
    return pl.pallas_call(
        _edges_kernel,
        in_specs=[pl.BlockSpec(memory_space=pl.ANY)] * 3,
        out_shape=[_sds(NSEND, NG, G, RAD)] * 2,
        scratch_shapes=[
            pltpu.VMEM((AX, AZ, RAD), jnp.int32),
            pltpu.VMEM((2, AX, AZ, RAD), F32),
            pltpu.VMEM((AX, AZ, RAD), F32),
            pltpu.SemaphoreType.DMA((NG, 4)),
        ],
        compiler_params=_params(56),
        cost_estimate=_cost(2**20, 6 * 2**20),
        name="edge_layers",
    )(labels, exc, a)


def _prepare_kernel(lab_ref, exc_ref, a_ref, a_out, lab_out, nu_out, oc_out, os_out):
    def group(g, a, c, s, lab):
        a_out[:, g] = a
        lab_out[:, g] = lab.astype(F32)
        nu_out[:, g] = _reluct(lab)
        oc_out[:, g] = _driven(lab, c)
        os_out[:, g] = _driven(lab, s)

    def own(g):
        at = _planes(g)
        group(g, *[jnp.swapaxes(x, 0, 1) for x in (a_ref[at], exc_ref[0, at], exc_ref[1, at], lab_ref[at])])

    _loop(NG, own)


def _prepare(labels, exc, a):
    return pl.pallas_call(
        _prepare_kernel,
        out_shape=[_sds(AZ, NG, G, RAD)] * 5,
        compiler_params=_params(),
        cost_estimate=_cost(2**22, 8 * 2**20),
        name="prepare",
    )(labels, exc, a)


PG = 16
NP = AX // PG


def _prior_send_kernel(prior_ref, out):
    def block(p):
        x = prior_ref[pl.ds(pl.multiple_of(p * PG, PG), PG)]
        out[:, p] = jnp.transpose(x.reshape(PG * RL, ANG)).reshape(SEC, AZ, PG * RL)

    _loop(NP, block)


def _prior_send(prior):
    return pl.pallas_call(
        _prior_send_kernel,
        out_shape=_sds(SEC, NP, AZ, PG * RL),
        compiler_params=_params(),
        cost_estimate=_cost(2**20, 3 * 2**20),
        name="prior_send",
    )(prior)


def _swap_blocks(x, lanes):
    count = 128 // lanes
    blk = lax.broadcasted_iota(jnp.int32, (8, 128), 1) // lanes
    x = list(x)
    b = count // 2
    while b:
        keep = (blk & b) == 0
        for j in range(count):
            if j & b == 0:
                p, q = x[j], x[j + b]
                x[j] = jnp.where(keep, p, pltpu.roll(q, b * lanes, 1))
                x[j + b] = jnp.where(keep, pltpu.roll(p, 128 - b * lanes, 1), q)
        b //= 2
    return x


def _prior_take_kernel(x_ref, out, nat):
    def block(p):
        for tile in range(AZ // 8):
            rows = slice(tile * 8, tile * 8 + 8)
            for half in range(2):
                got = _swap_blocks([x_ref[half * PG + j, p, rows] for j in range(PG)], RL)
                for k in range(PG):
                    nat[k, rows, half * 128 : half * 128 + 128] = got[k]
        for k in range(PG // G):
            out[:, p * (PG // G) + k] = jnp.swapaxes(nat[k * G : k * G + G], 0, 1)

    _loop(NP, block)


def _prior_take(x):
    return pl.pallas_call(
        _prior_take_kernel,
        out_shape=_sds(AZ, NG, G, RAD),
        scratch_shapes=[pltpu.VMEM((PG, AZ, RAD), F32)],
        compiler_params=_params(),
        cost_estimate=_cost(2**22, 3 * 2**20),
        name="prior_take",
    )(x)


def _temperature_take_kernel(x_ref, out):
    def group(g):
        tiles = [_swap_blocks([x_ref[s * 8 + j, g] for j in range(8)], AZ) for s in range(SEC // 8)]
        for q in range(G):
            out[g * G + q] = jnp.concatenate([t[q] for t in tiles], axis=1)

    _loop(NG, group)


def _temperature_take(x):
    return pl.pallas_call(
        _temperature_take_kernel,
        out_shape=_sds(AX, RL, ANG),
        compiler_params=_params(),
        cost_estimate=_cost(2**22, 2**21),
        name="temperature_take",
    )(x)


def _sides(x, lane):
    x0, x1 = x[:, :HALF], x[:, HALF:]
    f0, f1 = pltpu.roll(x0, 1, 1), pltpu.roll(x1, 1, 1)
    b0, b1 = pltpu.roll(x0, HALF - 1, 1), pltpu.roll(x1, HALF - 1, 1)
    at_low, at_high = lane == 0, lane == HALF - 1
    inward = jnp.concatenate([jnp.where(at_low, 0.0, f0), jnp.where(at_low, f0, f1)], axis=1)
    outward = jnp.concatenate([jnp.where(at_high, b1, b0), jnp.where(at_high, 0.0, b1)], axis=1)
    return inward, outward


def _axial(row, first, last, i, g, x, sub):
    before = pltpu.roll(row(i, g - 1), 1, 0) if g else first
    after = pltpu.roll(row(i, g + 1), G - 1, 0) if g < NG - 1 else last
    lower = jnp.where(sub == 0, before, pltpu.roll(x, 1, 0))
    return lower, jnp.where(sub == G - 1, after, pltpu.roll(x, G - 1, 0))


def _faces(t_row, h_row, i, g, beside, lane, sub):
    t, h = t_row(i, g), h_row(i, g)
    pairs = [(t_row(i - 1, g), h_row(i - 1, g)), (t_row(i + 1, g), h_row(i + 1, g))]
    pairs += list(zip(_sides(t, lane), _sides(h, lane)))
    if beside is None:
        (t_lo, h_lo), (t_hi, h_hi) = (t, -h), (t, -h)
    else:
        (t_lo, h_lo), (t_hi, h_hi) = beside
    pairs += list(zip(_axial(t_row, t_lo, t_hi, i, g, t, sub), _axial(h_row, h_lo, h_hi, i, g, h, sub)))
    flux, total = None, None
    for tn, hn in pairs:
        kf = h + hn
        term = kf * (tn - t)
        flux = term if flux is None else flux + term
        total = kf if total is None else total + kf
    return t, flux, total


def _iotas():
    lane = lax.broadcasted_iota(jnp.int32, (G, HALF), 1)
    sub = lax.broadcasted_iota(jnp.int32, (G, RAD), 0)
    return lane, sub


def _advance(first, width, reach, state, nu_of, oc_of, os_of, add_square, bufs, lane):
    def get(t, r):
        return state(r) if t == 0 else bufs[(t - 1) % 2, r + HMAX]

    for t in range(width):
        phase = 2.0 * math.pi / PERIOD * (first + t)
        cc, ss = math.cos(phase), math.sin(phase)
        lo, hi = -reach + 1 + t, AZ - 1 + reach - 1 - t
        down, mid = get(t, lo - 1), get(t, lo)
        for r in range(lo, hi + 1):
            up = get(t, r + 1)
            inward, outward = _sides(mid, lane)
            source = cc * oc_of(r) if first + t == 0 else cc * oc_of(r) + ss * os_of(r)
            change = nu_of(r) * ((down + up) + (inward + outward) - 4.0 * mid) + source
            if -1 <= r <= AZ:
                add_square(t, r, change * change)
            bufs[t % 2, r + HMAX] = mid + change
            down, mid = mid, up
    return lambda r: get(width - 1, r)


_CONSTS = ["lab", "nu", "oc", "os", "f_low", "f_high"]


def _getters(R, g):
    low, high = R["f_low"], R["f_high"]

    def const(name, k):
        def get(r):
            if r < 0:
                return low[AT[k] + LAYERS[k] + r, g]
            if r >= AZ:
                return high[AT[k] + r - AZ, g]
            return R[name][r, g]

        return get

    label, oc, os = const("lab", 0), const("oc", 1), const("os", 2)
    kept = {}

    def nu(r):
        if 0 <= r < AZ:
            return R["nu"][r, g]
        if r not in kept:
            kept[r] = _reluct(label(r))
        return kept[r]

    def start(r):
        if r < 0:
            return low[H0 + r, g]
        if r >= AZ:
            return high[r - AZ, g]
        return R["a"][r, g]

    return label, nu, oc, os, start


def _run(index, R, g, bufs, lane):
    first, width, reach = sum(WIDTHS[:index]), WIDTHS[index], REACH[index]
    last = index == len(WIDTHS) - 1
    label, nu, oc, os, start = _getters(R, g)

    def state(r):
        if index == 0:
            return start(r)
        if r < 0:
            return R["low"][reach + r, g]
        if r >= AZ:
            return R["high"][r - AZ, g]
        return R["a"][r, g]

    def slot(r):
        return (r + 1,) if last else (r + 1, g)

    def add_square(t, r, sq):
        if t > 0:
            sq = R["q_out"][slot(r)] + sq
        elif index:
            sq = R["q"][r + 1, g] + sq
            if not 0 <= r < AZ:
                missed = state(r) - R["before"][0 if r < 0 else 1, g]
                sq = sq + missed * missed
        R["q_out"][slot(r)] = sq

    return label, _advance(first, width, reach, state, nu, oc, os, add_square, bufs, lane)


def _phase_kernel(index, names, *refs):
    R = dict(zip(names, refs))
    bufs = R["bufs"]
    lane, _ = _iotas()
    n = REACH[index + 1]

    def group(g):
        _, previous = _run(index, R, g, bufs, lane)
        a = bufs[(WIDTHS[index] - 1) % 2, HMAX : HMAX + AZ]
        R["a_out"][:, g] = a
        R["before_out"][0, g] = previous(-1)
        R["before_out"][1, g] = previous(AZ)
        R["e_low"][0:n, g] = a[0:n]
        R["e_high"][0:n, g] = a[AZ - n :]
        if index + 1 == PRIOR_AT:
            R["e_low"][n : n + 2, g] = R["prior"][0:2, g]
            R["e_high"][n : n + 2, g] = R["prior"][AZ - 2 :, g]

    _loop(NG, group)


def _losses(R, g, bufs, lane, store):
    label, _ = _run(len(WIDTHS) - 1, R, g, bufs, lane)
    for r in range(-1, AZ + 1):
        lab = label(r)
        store(r, _sigma(lab) * R["q_out"][r + 1], lab)


_T, _H, _J, _N, _L = range(5)
_END = (5, AZ + 2, RAD)


def _ends_kernel(names, *refs):
    R = dict(zip(names, refs))
    lane, _ = _iotas()
    for out, part, g, q in ((R["down"], R["part_lo"], ENDS[0], 0), (R["up"], R["part_hi"], ENDS[1], G - 1)):
        out[...] = part[...]

        def store(r, d, lab, out=out, part=part, q=q):
            out[_N, r + 1 : r + 2, :] = part[_N, r + 1 : r + 2, :] + d[q : q + 1]

        _losses(R, g, R["bufs"], lane, store)


def _last_kernel(names, *refs):
    R = dict(zip(names, refs))
    bufs = R["bufs"]
    lane, _ = _iotas()

    def group(g):
        def store(r, d, lab):
            t = R["base"][r + 1, g] + d * R["gain"][r + 1, g]
            R["t1"][r + 1, g] = t
            R["h1"][r + 1, g] = _half_cond(lab, t)
            if 0 <= r < AZ:
                R["loss"][r, g] = d

        _losses(R, g, bufs, lane, store)
        a = bufs[(WIDTHS[-1] - 1) % 2, HMAX : HMAX + AZ]
        R["closing"][_planes(g)] = jnp.swapaxes(a, 0, 1)
        R["dissipation"][_planes(g)] = jnp.swapaxes(R["loss"][:, g], 0, 1)

    _loop(NG, group)


def _second_kernel(names, *refs):
    R = dict(zip(names, refs))
    lane, sub = _iotas()
    ax = lax.axis_index("ax")
    exists = (ax > 0, ax < lax.axis_size("ax") - 1)
    for side, (own, other) in enumerate(((R["down"], R["t_lo"]), (R["up"], R["t_hi"]))):
        kf = own[_H] + other[_H]
        jump = kf * (other[_T] - own[_T])
        t = own[_T] + (own[_N] + jump) / (own[_J] + kf)
        R["own1"][side, 0] = t
        R["own1"][side, 1] = _half_cond(own[_L], t)
        t = other[_T] + (other[_N] - jump) / (other[_J] + kf)
        R["beside1"][side, 0] = jnp.where(exists[side], t, 0.0)
        R["beside1"][side, 1] = jnp.where(exists[side], _half_cond(other[_L], t), 0.0)

    def patched(name, k):
        def row(i, g):
            x = R[name][i, g]
            if g == ENDS[0]:
                x = jnp.where(sub == 0, R["own1"][0, k, pl.ds(i, 1), :], x)
            if g == ENDS[1]:
                x = jnp.where(sub == G - 1, R["own1"][1, k, pl.ds(i, 1), :], x)
            return x

        return row

    t_row, h_row = patched("t1", 0), patched("h1", 1)

    def row(r):
        at = pl.ds(r + 1, 1)
        beside = [[R["beside1"][side, k, at, :] for k in range(2)] for side in range(2)]
        for g in range(NG):
            t, flux, total = _faces(t_row, h_row, r + 1, g, beside, lane, sub)
            cap = _capacity(R["lab"][r, g])
            mismatch = cap * (t - R["prior"][r, g]) - flux - R["loss"][r, g]
            R["t2"][r, g] = t - mismatch / (cap + total)

    _loop(AZ, row)

    def turn(g):
        nat = jnp.swapaxes(R["t2"][:, g], 0, 1).reshape(G * AZ, RAD)
        R["blocks"][:, g] = jnp.transpose(nat).reshape(SEC, RL, G * AZ)

    _loop(NG, turn)


def _prior_rows(R, g):
    n = REACH[PRIOR_AT]
    label = _getters(R, g)[0]

    def row(r):
        if r < 0:
            return R["low1"][n + 2 + r, g]
        if r >= AZ:
            return R["high1"][n + r - AZ, g]
        return R["prior"][r, g]

    return row, label


def _ready_kernel(names, *refs):
    R = dict(zip(names, refs))
    lane, sub = _iotas()

    def fill(g):
        prior, label = _prior_rows(R, g)
        for r in range(-2, AZ + 2):
            t, lab = prior(r), label(r)
            R["t0"][r + 2, g] = t
            R["h0"][r + 2, g] = _half_cond(lab, t)
            R["cap"][r + 2, g] = _capacity(lab)

    _loop(NG, fill)

    def row(k):
        for g in range(NG):
            t, flux, total = _faces(
                lambda i, g: R["t0"][i, g], lambda i, g: R["h0"][i, g], k + 1, g, None, lane, sub
            )
            jac = R["cap"][k + 1, g] + total
            gain = 1.0 / jac
            R["base"][k, g] = t + flux * gain
            R["gain"][k, g] = gain
            if g in ENDS:
                end = 0 if g == ENDS[0] else 1
                R["jac"][end, k] = jac
                R["flux"][end, k] = flux

    _loop(AZ + 2, row)
    for end, (out, g, q) in enumerate(((R["part_lo"], ENDS[0], 0), (R["part_hi"], ENDS[1], G - 1))):
        label = _prior_rows(R, g)[1]
        plane = slice(q, q + 1)
        for k in range(AZ + 2):
            at = slice(k, k + 1)
            out[_T, at, :] = R["t0"][k + 1, g, plane, :]
            out[_H, at, :] = R["h0"][k + 1, g, plane, :]
            out[_J, at, :] = R["jac"][end, k, plane, :]
            out[_N, at, :] = R["flux"][end, k, plane, :]
            out[_L, at, :] = label(k - 1)[plane]


def _call(kernel, name, given, names, outs, scratch, *bound):
    results = pl.pallas_call(
        functools.partial(kernel, *bound, names + list(outs) + list(scratch)),
        out_shape=[_sds(*shape) for shape in outs.values()],
        scratch_shapes=[pltpu.VMEM(shape, F32) for shape in scratch.values()],
        compiler_params=_params(),
        cost_estimate=_cost(2**24, 2**23),
        name=name,
    )(*[given[key] for key in names])
    return dict(zip(outs, results))


_OWN = (AZ, NG, G, RAD)
_MORE = (AZ + 2, NG, G, RAD)
_BUFS = (2, AZ + 2 * HMAX, G, RAD)
_STATE = ["a", "q", "before", "low", "high"]
_LAST = _CONSTS + _STATE
_PRIOR = ["lab", "f_low", "f_high", "nu", "oc", "os", "prior", "low1", "high1"]


def _phase(index, V):
    n = REACH[index + 1] + (2 if index + 1 == PRIOR_AT else 0)
    names = _CONSTS + (_STATE if index else ["a"]) + (["prior"] if index + 1 == PRIOR_AT else [])
    outs = {"a_out": _OWN, "q_out": _MORE, "before_out": (2, NG, G, RAD)}
    outs.update(e_low=(n, NG, G, RAD), e_high=(n, NG, G, RAD))
    return _call(_phase_kernel, f"field_{index}", V, names, outs, {"bufs": _BUFS}, index)


def _ring(axis, x, step, closed):
    count = lax.axis_size(axis)
    pairs = [(i, (i + 1) % count) for i in range(count if closed else count - 1)]
    return lax.ppermute(x, axis, pairs if step > 0 else [(b, a) for a, b in pairs])


def _around(low_edge, high_edge):
    return _ring("sec", high_edge, 1, True), _ring("sec", low_edge, -1, True)


def shards(labels, exc, a0, prior):
    V = {}
    V["f_low"], V["f_high"] = _around(*_edges(labels, exc, a0))
    got = lax.all_to_all(_prior_send(prior), "sec", 0, 0)
    V["prior"] = _prior_take(got)
    V.update(zip(("a", "lab", "nu", "oc", "os"), _prepare(labels, exc, a0)))
    last = len(WIDTHS) - 1
    for index in range(last):
        out = _phase(index, V)
        V["a"], V["q"], V["before"] = out["a_out"], out["q_out"], out["before_out"]
        V["low"], V["high"] = _around(out["e_low"], out["e_high"])
        if index + 1 == PRIOR_AT:
            V["low1"], V["high1"] = V["low"], V["high"]
        if index + 1 == last:
            scratch = {name: (AZ + 4, NG, G, RAD) for name in ("t0", "h0", "cap")}
            scratch.update(jac=(2, AZ + 2, G, RAD), flux=(2, AZ + 2, G, RAD))
            outs = {"base": _MORE, "gain": _MORE, "part_lo": _END, "part_hi": _END}
            V.update(_call(_ready_kernel, "first_ready", V, _PRIOR, outs, scratch))
    scratch = {"bufs": _BUFS, "q_out": (AZ + 2, G, RAD)}
    outs = {"down": _END, "up": _END}
    V.update(_call(_ends_kernel, "last_ends", V, _LAST + ["part_lo", "part_hi"], outs, scratch))
    V["t_lo"], V["t_hi"] = _ring("ax", V["up"], 1, False), _ring("ax", V["down"], -1, False)
    outs = {"closing": (AX, AZ, RAD), "dissipation": (AX, AZ, RAD), "t1": _MORE, "h1": _MORE, "loss": _OWN}
    V.update(_call(_last_kernel, "field_last", V, _LAST + ["base", "gain"], outs, scratch))
    names = ["t1", "h1", "down", "up", "t_lo", "t_hi", "lab", "prior", "loss"]
    shape = (2, 2, AZ + 2, RAD)
    scratch = {"t2": _OWN, "own1": shape, "beside1": shape}
    out = _call(_second_kernel, "second_sweep", V, names, {"blocks": (SEC, NG, RL, G * AZ)}, scratch)
    temperature = _temperature_take(lax.all_to_all(out["blocks"], "sec", 0, 0))
    return V["closing"], V["dissipation"], temperature


def solution(mesh):
    spec = P("ax", "sec", None)
    return jax.shard_map(
        shards,
        mesh=mesh,
        in_specs=(spec, P(None, "ax", "sec", None), spec, spec),
        out_specs=(spec, spec, spec),
        check_vma=False,
    )
```

```python
import functools
import math

import jax
import jax.numpy as jnp
from jax import lax
from jax.experimental import pallas as pl
from jax.experimental.pallas import tpu as pltpu
from jax.sharding import PartitionSpec as P

SAMPLES = 16
PERIOD = 32
SPAN = 8
DEPTH = SPAN // 2
FIRST_AT = (0, DEPTH, 2 * DEPTH, 3 * DEPTH, 4 * DEPTH)
NSEND = 5 * DEPTH
NLATEST = DEPTH + 1

F32 = jnp.float32
AX, AZ, RAD, ANG = 64, 16, 256, 512
SEC = 32
RL = RAD // SEC
G = 8
NG = AX // G
ENDS = (0, NG - 1)
HALF = RAD // 2


def _params(mib=16):
    return pltpu.CompilerParams(vmem_limit_bytes=mib * 2**20)


def _sds(*shape):
    return jax.ShapeDtypeStruct(shape, F32)


def _cost(flops, nbytes):
    return pl.CostEstimate(flops=flops, bytes_accessed=nbytes, transcendentals=0)


def _loop(n, body):
    def step(i, _):
        body(i)
        return 0

    lax.fori_loop(0, n, step, 0)


def _lockstep(chains):
    results = [None] * len(chains)
    going = dict(enumerate(chains))
    while going:
        for k in list(going):
            try:
                next(going[k])
            except StopIteration as end:
                results[k] = end.value
                del going[k]
    return results


def _pairs(body):
    _loop(NG // 2, lambda i: body([2 * i, 2 * i + 1]))


def _planes(g):
    return pl.ds(pl.multiple_of(g * G, G), G)


def _reluct(lab):
    return jnp.where(lab == 0, 0.05, jnp.where(lab == 3, 0.2, 0.24)).astype(F32)


def _sigma(lab):
    return jnp.where(lab == 0, 0.3, jnp.where(lab == 1, 1.0, jnp.where(lab == 2, 0.0, 0.6))).astype(F32)


def _driven(lab, x):
    return jnp.where((lab == 1) | (lab == 3), x, 0.0)


def _half_cond(lab, temp):
    half_k0 = jnp.where(lab == 0, 0.5, jnp.where(lab == 1, 0.75, jnp.where(lab == 2, 0.05, 0.2)))
    return half_k0 * (1.0 + 0.5 * jnp.tanh(temp))


def _capacity(lab):
    return jnp.where(lab == 1, 3.5, jnp.where(lab == 2, 0.5, 3.0)).astype(F32)


def _edges_kernel(lab_hbm, exc_hbm, a_hbm, low_ref, high_ref, lab_v, exc_v, a_v, sems):
    copies = []
    for g in range(NG):
        at = pl.ds(g * G, G)
        copies.append(
            [
                pltpu.make_async_copy(lab_hbm.at[at], lab_v.at[at], sems.at[g, 0]),
                pltpu.make_async_copy(exc_hbm.at[0, at], exc_v.at[0, at], sems.at[g, 1]),
                pltpu.make_async_copy(exc_hbm.at[1, at], exc_v.at[1, at], sems.at[g, 2]),
                pltpu.make_async_copy(a_hbm.at[at], a_v.at[at], sems.at[g, 3]),
            ]
        )
        for copy in copies[-1]:
            copy.start()

    lane, _ = _iotas()

    def corner(g, out, row, a, c, s, lab):
        nu, oc, os = {}, {}, {}
        for j in range(2 * DEPTH - 1):
            r = row(j)
            nu[j], oc[j], os[j] = _reluct(lab[r]), _driven(lab[r], c[r]), _driven(lab[r], s[r])
            if j < DEPTH:
                out[FIRST_AT[2] + j, g] = lab[r].astype(F32)
                out[FIRST_AT[3] + j, g] = oc[j]
                out[FIRST_AT[4] + j, g] = os[j]
        level = {j: a[row(j)] for j in range(2 * DEPTH)}
        for t in range(DEPTH):
            yield
            out[FIRST_AT[0] + t, g] = level[t]
            out[FIRST_AT[1] + t, g] = level[t + 1]
            level = {
                j: _step(t, level[j - 1], level[j], level[j + 1], nu[j], oc[j], os[j], lane)[0]
                for j in range(t + 1, 2 * DEPTH - 1 - t)
            }

    for pair in range(NG // 2):
        chains = []
        for g in (2 * pair, 2 * pair + 1):
            for copy in copies[g]:
                copy.wait()
            at = pl.ds(g * G, G)
            given = [jnp.swapaxes(x, 0, 1) for x in (a_v[at], exc_v[0, at], exc_v[1, at], lab_v[at])]
            chains.append(corner(g, low_ref, lambda j: j, *given))
            chains.append(corner(g, high_ref, lambda j: AZ - 1 - j, *given))
        _lockstep(chains)


def _edges(labels, exc, a):
    return pl.pallas_call(
        _edges_kernel,
        in_specs=[pl.BlockSpec(memory_space=pl.ANY)] * 3,
        out_shape=[_sds(NSEND, NG, G, RAD)] * 2,
        scratch_shapes=[
            pltpu.VMEM((AX, AZ, RAD), jnp.int32),
            pltpu.VMEM((2, AX, AZ, RAD), F32),
            pltpu.VMEM((AX, AZ, RAD), F32),
            pltpu.SemaphoreType.DMA((NG, 4)),
        ],
        compiler_params=_params(56),
        cost_estimate=_cost(2**20, 6 * 2**20),
        name="edge_layers",
    )(labels, exc, a)


def _prepare_kernel(lab_ref, exc_ref, a_ref, latest, earlier, q, lab_out, nu_out, oc_out, os_out, bufs, a_v):
    lane, _ = _iotas()

    def group(g, k):
        at = _planes(g)
        lab = jnp.swapaxes(lab_ref[at], 0, 1)
        lab_out[:, g] = lab.astype(F32)
        nu_out[:, g] = _reluct(lab)
        oc_out[:, g] = _driven(lab, jnp.swapaxes(exc_ref[0, at], 0, 1))
        os_out[:, g] = _driven(lab, jnp.swapaxes(exc_ref[1, at], 0, 1))
        a_v[k] = jnp.swapaxes(a_ref[at], 0, 1)
        zero = jnp.zeros((G, RAD), F32)
        for r in (-1, 0, AZ - 1, AZ):
            q[r + 1, g] = zero

        def add_square(t, r, sq):
            q[r + 1, g] = sq if t == 0 else q[r + 1, g] + sq

        consts = [lambda r, ref=ref: ref[r, g] for ref in (nu_out, oc_out, os_out)]
        return _triangle(0, lambda r: a_v[k, r], consts, add_square, latest, earlier, g, bufs.at[k], lane)

    _pairs(lambda gs: _lockstep([group(g, k) for k, g in enumerate(gs)]))


def _prepare(labels, exc, a):
    return pl.pallas_call(
        _prepare_kernel,
        out_shape=[_sds(AZ, NG, G, RAD)] * 2 + [_sds(AZ + 2, NG, G, RAD)] + [_sds(AZ, NG, G, RAD)] * 4,
        scratch_shapes=[pltpu.VMEM((2, 2, AZ, G, RAD), F32), pltpu.VMEM((2, AZ, G, RAD), F32)],
        compiler_params=_params(),
        cost_estimate=_cost(2**22, 8 * 2**20),
        name="prepare",
    )(labels, exc, a)


PG = 16
NP = AX // PG


def _prior_send_kernel(prior_ref, out):
    for p in range(NP):
        x = prior_ref[p * PG : p * PG + PG]
        x = jnp.transpose(x.reshape(PG * RL, ANG)).reshape(SEC, AZ, PG * RL)
        out[:, p] = x
        for e, r in enumerate((AZ - 2, AZ - 1, 0, 1)):
            line = x[:, r : r + 1, :]
            at = slice(p * 4 + e, p * 4 + e + 1)
            if e < 2:
                out[1:, NP, at, :] = line[:-1]
                out[0:1, NP, at, :] = line[-1:]
            else:
                out[:-1, NP, at, :] = line[1:]
                out[SEC - 1 :, NP, at, :] = line[:1]


def _prior_send(prior):
    return pl.pallas_call(
        _prior_send_kernel,
        out_shape=_sds(SEC, NP + 1, AZ, PG * RL),
        compiler_params=_params(),
        cost_estimate=_cost(2**20, 3 * 2**20),
        name="prior_send",
    )(prior)


def _swap_blocks(x, lanes):
    count = 128 // lanes
    blk = lax.broadcasted_iota(jnp.int32, (8, 128), 1) // lanes
    x = list(x)
    b = count // 2
    while b:
        keep = (blk & b) == 0
        for j in range(count):
            if j & b == 0:
                p, q = x[j], x[j + b]
                x[j] = jnp.where(keep, p, pltpu.roll(q, b * lanes, 1))
                x[j + b] = jnp.where(keep, pltpu.roll(p, 128 - b * lanes, 1), q)
        b //= 2
    return x


def _prior_take_kernel(x_ref, out, more, nat):
    def fill(p):
        for tile in range(AZ // 8):
            rows = slice(tile * 8, tile * 8 + 8)
            for half in range(2):
                got = _swap_blocks([x_ref[half * PG + j, p, rows] for j in range(PG)], RL)
                for k in range(PG):
                    nat[k, rows, half * 128 : half * 128 + 128] = got[k]

    def block(p):
        fill(p)
        for k in range(PG // G):
            out[:, p * (PG // G) + k] = jnp.swapaxes(nat[k * G : k * G + G], 0, 1)

    _loop(NP, block)
    fill(NP)
    for k in range(PG // G):
        x = jnp.swapaxes(nat[k * G : k * G + G], 0, 1)
        for p in range(NP):
            more[:, p * (PG // G) + k] = x[p * 4 : p * 4 + 4]


def _prior_take(x):
    return pl.pallas_call(
        _prior_take_kernel,
        out_shape=[_sds(AZ, NG, G, RAD), _sds(4, NG, G, RAD)],
        scratch_shapes=[pltpu.VMEM((PG, AZ, RAD), F32)],
        compiler_params=_params(),
        cost_estimate=_cost(2**22, 3 * 2**20),
        name="prior_take",
    )(x)


def _temperature_take_kernel(x_ref, out):
    def group(g):
        tiles = [_swap_blocks([x_ref[s * 8 + j, g] for j in range(8)], AZ) for s in range(SEC // 8)]
        for q in range(G):
            out[g * G + q] = jnp.concatenate([t[q] for t in tiles], axis=1)

    _loop(NG, group)


def _temperature_take(x):
    return pl.pallas_call(
        _temperature_take_kernel,
        out_shape=_sds(AX, RL, ANG),
        compiler_params=_params(),
        cost_estimate=_cost(2**22, 2**21),
        name="temperature_take",
    )(x)


def _sides(x, lane):
    x0, x1 = x[:, :HALF], x[:, HALF:]
    f0, f1 = pltpu.roll(x0, 1, 1), pltpu.roll(x1, 1, 1)
    b0, b1 = pltpu.roll(x0, HALF - 1, 1), pltpu.roll(x1, HALF - 1, 1)
    at_low, at_high = lane == 0, lane == HALF - 1
    inward = jnp.concatenate([jnp.where(at_low, 0.0, f0), jnp.where(at_low, f0, f1)], axis=1)
    outward = jnp.concatenate([jnp.where(at_high, b1, b0), jnp.where(at_high, 0.0, b1)], axis=1)
    return inward, outward


def _axial(row, first, last, i, g, x, sub):
    before = pltpu.roll(row(i, g - 1), 1, 0) if g else first
    after = pltpu.roll(row(i, g + 1), G - 1, 0) if g < NG - 1 else last
    lower = jnp.where(sub == 0, before, pltpu.roll(x, 1, 0))
    return lower, jnp.where(sub == G - 1, after, pltpu.roll(x, G - 1, 0))


def _faces(t_row, h_row, i, g, beside, lane, sub):
    t, h = t_row(i, g), h_row(i, g)
    pairs = [(t_row(i - 1, g), h_row(i - 1, g)), (t_row(i + 1, g), h_row(i + 1, g))]
    pairs += list(zip(_sides(t, lane), _sides(h, lane)))
    if beside is None:
        (t_lo, h_lo), (t_hi, h_hi) = (t, -h), (t, -h)
    else:
        (t_lo, h_lo), (t_hi, h_hi) = beside
    pairs += list(zip(_axial(t_row, t_lo, t_hi, i, g, t, sub), _axial(h_row, h_lo, h_hi, i, g, h, sub)))
    flux, total = None, None
    for tn, hn in pairs:
        kf = h + hn
        term = kf * (tn - t)
        flux = term if flux is None else flux + term
        total = kf if total is None else total + kf
    return t, flux, total


def _iotas():
    lane = lax.broadcasted_iota(jnp.int32, (G, HALF), 1)
    sub = lax.broadcasted_iota(jnp.int32, (G, RAD), 0)
    return lane, sub


def _step(sample, down, mid, up, nu, oc, os, lane):
    phase = 2.0 * math.pi / PERIOD * sample
    cc, ss = math.cos(phase), math.sin(phase)
    inward, outward = _sides(mid, lane)
    source = cc * oc if sample == 0 else cc * oc + ss * os
    change = nu * ((down + up) + (inward + outward) - 4.0 * mid) + source
    return mid + change, change


def _triangle(first, rows, consts, add_square, latest, earlier, g, bufs, lane):
    nu, oc, os = consts

    def get(t, r):
        return rows(r) if t == 0 else bufs[(t - 1) % 2, r]

    latest[0, g] = rows(0)
    latest[AZ - 1, g] = rows(AZ - 1)
    earlier[1, g] = rows(1)
    earlier[AZ - 2, g] = rows(AZ - 2)
    for t in range(SPAN - 1):
        yield
        down, mid = get(t, t), get(t, t + 1)
        for r in range(t + 1, AZ - 1 - t):
            up = get(t, r + 1)
            new, change = _step(first + t, down, mid, up, nu(r), oc(r), os(r), lane)
            add_square(t, r, change * change)
            bufs[t % 2, r] = new
            if r in (t + 1, AZ - 2 - t):
                latest[r, g] = new
            elif r in (t + 2, AZ - 3 - t):
                earlier[r, g] = new
            down, mid = mid, up


def _valley(first, limit, own, halo, consts, add_square, bufs, final, lane):
    nu, oc, os = consts

    def get(t, x):
        j = x if x >= 0 else -1 - x
        if j < t:
            return bufs[(t - 1) % 2, x + DEPTH]
        latest, earlier = own if x >= 0 else halo
        if j == t or j == SPAN:
            return latest(j)
        return earlier(j)

    for t in range(SPAN):
        yield
        lo = -1 - min(t, limit - 1 - t)
        down, mid = get(t, lo - 1), get(t, lo)
        for x in range(lo, t + 1):
            up = get(t, x + 1)
            new, change = _step(first + t, down, mid, up, nu(x), oc(x), os(x), lane)
            if x >= -1:
                add_square(x, change * change)
            if t == SPAN - 1 and x >= 0:
                final(x, new)
            else:
                bufs[t % 2, x + DEPTH] = new
            down, mid = mid, up
    return bufs[SPAN % 2, DEPTH - 1]


_CONSTS = ["lab", "nu", "oc", "os", "f_low", "f_high"]
_STATE = ["latest", "earlier", "q"]


def _label(R, g):
    def get(r):
        if r < 0:
            return R["f_low"][FIRST_AT[2] - 1 - r, g]
        if r >= AZ:
            return R["f_high"][FIRST_AT[2] + r - AZ, g]
        return R["lab"][r, g]

    return get


def _fill(second, R, g, q_slot, final, bufs, lane):
    chains = []
    for high in (False, True):
        name = "high" if high else "low"
        consts_from = R["f_" + name]
        halo_from = R[name] if second else consts_from
        n = NLATEST if second else DEPTH

        def row(x, high=high):
            return AZ - 1 - x if high else x

        def const(name, k, row=row, consts_from=consts_from):
            return lambda x: R[name][row(x), g] if x >= 0 else consts_from[FIRST_AT[k] - 1 - x, g]

        kept = {}

        def nu(x, row=row, consts_from=consts_from, kept=kept):
            if x >= 0:
                return R["nu"][row(x), g]
            if x not in kept:
                kept[x] = _reluct(consts_from[FIRST_AT[2] - 1 - x, g])
            return kept[x]

        own = (lambda j, row=row: R["latest"][row(j), g], lambda j, row=row: R["earlier"][row(j), g])
        halo = (
            lambda j, halo_from=halo_from: halo_from[j, g],
            lambda j, halo_from=halo_from, n=n: halo_from[n + j - 1, g],
        )
        seen = set()

        def add_square(x, sq, row=row, seen=seen, high=high, halo=halo):
            r = row(x)
            if r in seen:
                before = R["q_out"][q_slot(r)]
            else:
                seen.add(r)
                before = R["q"][r + 1, g]
                if second and x < 0:
                    missed = halo[0](0) - R["gone"][int(high), g]
                    before = before + missed * missed
            R["q_out"][q_slot(r)] = before + sq

        chains.append(
            _valley(
                SPAN if second else 0,
                SPAN if second else SPAN - 1,
                own,
                halo,
                (nu, const("oc", 3), const("os", 4)),
                add_square,
                bufs.at[int(high)],
                lambda x, v, row=row: final(row(x), v),
                lane,
            )
        )
    return chains


def _middle_kernel(names, *refs):
    R = dict(zip(names, refs))
    lane, _ = _iotas()

    def groups(gs):
        chains = []
        for k, g in enumerate(gs):

            def final(r, v, k=k):
                R["rows"][k, r] = v

            chains += _fill(False, R, g, lambda r, g=g: (r + 1, g), final, R["ends"].at[k], lane)
        gone = _lockstep(chains)
        chains = []
        for k, g in enumerate(gs):
            for end in range(2):
                R["gone"][end, g] = gone[2 * k + end]
            consts = [lambda r, name=name, g=g: R[name][r, g] for name in ("nu", "oc", "os")]

            def add_square(t, r, sq, g=g):
                R["q_out"][r + 1, g] = R["q_out"][r + 1, g] + sq

            latest, earlier = R["latest_out"], R["earlier_out"]
            start = lambda r, k=k: R["rows"][k, r]
            chains.append(_triangle(SPAN, start, consts, add_square, latest, earlier, g, R["bufs"].at[k], lane))
        _lockstep(chains)
        for g in gs:
            for name, row in (("e_low", lambda j: j), ("e_high", lambda j: AZ - 1 - j)):
                for j in range(NLATEST):
                    R[name][j, g] = latest[row(j), g]
                for j in range(1, DEPTH + 1):
                    R[name][NLATEST + j - 1, g] = earlier[row(j), g]

    _pairs(groups)


def _losses(R, gs, lane, store, final):
    chains = []
    for k, g in enumerate(gs):
        chains += _fill(
            True, R, g, lambda r, k=k: (k, r + 1), lambda r, v, k=k: final(k, r, v), R["ends"].at[k], lane
        )
    _lockstep(chains)
    for k, g in enumerate(gs):
        label = _label(R, g)
        for r in range(-1, AZ + 1):
            lab = label(r)
            store(k, r, _sigma(lab) * R["q_out"][k, r + 1], lab)


_T, _H, _J, _N, _L = range(5)
_END = (5, AZ + 2, RAD)


def _ends_kernel(names, *refs):
    R = dict(zip(names, refs))
    lane, _ = _iotas()
    outs, parts = (R["down"], R["up"]), (R["part_lo"], R["part_hi"])
    for out, part in zip(outs, parts):
        out[...] = part[...]

    def store(k, r, d, lab):
        at, q = slice(r + 1, r + 2), (0, G - 1)[k]
        outs[k][_N, at, :] = parts[k][_N, at, :] + d[q : q + 1]

    _losses(R, ENDS, lane, store, lambda k, r, v: None)


def _last_kernel(names, *refs):
    R = dict(zip(names, refs))
    lane, _ = _iotas()

    def groups(gs):
        def final(k, r, v):
            R["rows"][k, r] = v

        def store(k, r, d, lab):
            g = gs[k]
            t = R["base"][r + 1, g] + d * R["gain"][r + 1, g]
            R["t1"][r + 1, g] = t
            R["h1"][r + 1, g] = _half_cond(lab, t)
            if 0 <= r < AZ:
                R["loss"][r, g] = d

        _losses(R, gs, lane, store, final)
        for k, g in enumerate(gs):
            R["closing"][_planes(g)] = jnp.swapaxes(R["rows"][k], 0, 1)
            R["dissipation"][_planes(g)] = jnp.swapaxes(R["loss"][:, g], 0, 1)

    _pairs(groups)


def _second_kernel(names, *refs):
    R = dict(zip(names, refs))
    lane, sub = _iotas()
    ax = lax.axis_index("ax")
    exists = (ax > 0, ax < lax.axis_size("ax") - 1)
    for side, (own, other) in enumerate(((R["down"], R["t_lo"]), (R["up"], R["t_hi"]))):
        kf = own[_H] + other[_H]
        jump = kf * (other[_T] - own[_T])
        t = own[_T] + (own[_N] + jump) / (own[_J] + kf)
        R["own1"][side, 0] = t
        R["own1"][side, 1] = _half_cond(own[_L], t)
        t = other[_T] + (other[_N] - jump) / (other[_J] + kf)
        R["beside1"][side, 0] = jnp.where(exists[side], t, 0.0)
        R["beside1"][side, 1] = jnp.where(exists[side], _half_cond(other[_L], t), 0.0)

    def patched(name, k):
        def row(i, g):
            x = R[name][i, g]
            if g == ENDS[0]:
                x = jnp.where(sub == 0, R["own1"][0, k, pl.ds(i, 1), :], x)
            if g == ENDS[1]:
                x = jnp.where(sub == G - 1, R["own1"][1, k, pl.ds(i, 1), :], x)
            return x

        return row

    t_row, h_row = patched("t1", 0), patched("h1", 1)

    def row(r):
        at = pl.ds(r + 1, 1)
        beside = [[R["beside1"][side, k, at, :] for k in range(2)] for side in range(2)]
        for g in range(NG):
            t, flux, total = _faces(t_row, h_row, r + 1, g, beside, lane, sub)
            cap = _capacity(R["lab"][r, g])
            mismatch = cap * (t - R["prior"][r, g]) - flux - R["loss"][r, g]
            R["t2"][r, g] = t - mismatch / (cap + total)

    _loop(AZ, row)

    def turn(g):
        nat = jnp.swapaxes(R["t2"][:, g], 0, 1).reshape(G * AZ, RAD)
        R["blocks"][:, g] = jnp.transpose(nat).reshape(SEC, RL, G * AZ)

    _loop(NG, turn)


def _prior_row(R, g, r):
    if 0 <= r < AZ:
        return R["prior"][r, g]
    return R["prior_more"][r + 2 if r < 0 else r - AZ + 2, g]


def _ready_kernel(names, *refs):
    R = dict(zip(names, refs))
    lane, sub = _iotas()

    def fill(g):
        label = _label(R, g)
        for r in range(-2, AZ + 2):
            t, lab = _prior_row(R, g, r), label(r)
            R["t0"][r + 2, g] = t
            R["h0"][r + 2, g] = _half_cond(lab, t)
            R["cap"][r + 2, g] = _capacity(lab)

    _loop(NG, fill)

    def row(k):
        for g in range(NG):
            t, flux, total = _faces(
                lambda i, g: R["t0"][i, g], lambda i, g: R["h0"][i, g], k + 1, g, None, lane, sub
            )
            jac = R["cap"][k + 1, g] + total
            gain = 1.0 / jac
            R["base"][k, g] = t + flux * gain
            R["gain"][k, g] = gain
            if g in ENDS:
                end = 0 if g == ENDS[0] else 1
                R["jac"][end, k] = jac
                R["flux"][end, k] = flux

    _loop(AZ + 2, row)
    for end, (out, g, q) in enumerate(((R["part_lo"], ENDS[0], 0), (R["part_hi"], ENDS[1], G - 1))):
        label = _label(R, g)
        plane = slice(q, q + 1)
        for k in range(AZ + 2):
            at = slice(k, k + 1)
            out[_T, at, :] = R["t0"][k + 1, g, plane, :]
            out[_H, at, :] = R["h0"][k + 1, g, plane, :]
            out[_J, at, :] = R["jac"][end, k, plane, :]
            out[_N, at, :] = R["flux"][end, k, plane, :]
            out[_L, at, :] = label(k - 1)[plane]


def _call(kernel, name, given, names, outs, scratch, *bound):
    results = pl.pallas_call(
        functools.partial(kernel, *bound, names + list(outs) + list(scratch)),
        out_shape=[_sds(*shape) for shape in outs.values()],
        scratch_shapes=[pltpu.VMEM(shape, F32) for shape in scratch.values()],
        compiler_params=_params(),
        cost_estimate=_cost(2**24, 2**23),
        name=name,
    )(*[given[key] for key in names])
    return dict(zip(outs, results))


_OWN = (AZ, NG, G, RAD)
_MORE = (AZ + 2, NG, G, RAD)
_FILL = {"ends": (2, 2, 2, SPAN + DEPTH, G, RAD), "rows": (2, AZ, G, RAD)}
_LAST = _CONSTS + _STATE + ["gone", "low", "high"]
_PRIOR = ["lab", "f_low", "f_high", "prior", "prior_more"]


def _ring(axis, x, step, closed):
    count = lax.axis_size(axis)
    pairs = [(i, (i + 1) % count) for i in range(count if closed else count - 1)]
    return lax.ppermute(x, axis, pairs if step > 0 else [(b, a) for a, b in pairs])


def _around(low_edge, high_edge):
    return _ring("sec", high_edge, 1, True), _ring("sec", low_edge, -1, True)


def shards(labels, exc, a0, prior):
    V = {}
    V["f_low"], V["f_high"] = _around(*_edges(labels, exc, a0))
    got = lax.all_to_all(_prior_send(prior), "sec", 0, 0)
    V.update(zip(_STATE + _CONSTS[:4], _prepare(labels, exc, a0)))
    edge = (NLATEST + DEPTH, NG, G, RAD)
    outs = {"latest_out": _OWN, "earlier_out": _OWN, "q_out": _MORE, "gone": (2, NG, G, RAD), "e_low": edge, "e_high": edge}
    out = _call(_middle_kernel, "field_middle", V, _CONSTS + _STATE, outs, {"bufs": (2, 2, AZ, G, RAD), **_FILL})
    V["low"], V["high"] = _around(out["e_low"], out["e_high"])
    for name in _STATE:
        V[name] = out[name + "_out"]
    V["gone"] = out["gone"]
    V["prior"], V["prior_more"] = _prior_take(got)
    scratch = {name: (AZ + 4, NG, G, RAD) for name in ("t0", "h0", "cap")}
    scratch.update(jac=(2, AZ + 2, G, RAD), flux=(2, AZ + 2, G, RAD))
    outs = {"base": _MORE, "gain": _MORE, "part_lo": _END, "part_hi": _END}
    V.update(_call(_ready_kernel, "first_ready", V, _PRIOR, outs, scratch))
    scratch = {"q_out": (2, AZ + 2, G, RAD), **_FILL}
    outs = {"down": _END, "up": _END}
    V.update(_call(_ends_kernel, "last_ends", V, _LAST + ["part_lo", "part_hi"], outs, scratch))
    V["t_lo"], V["t_hi"] = _ring("ax", V["up"], 1, False), _ring("ax", V["down"], -1, False)
    outs = {"closing": (AX, AZ, RAD), "dissipation": (AX, AZ, RAD), "t1": _MORE, "h1": _MORE, "loss": _OWN}
    V.update(_call(_last_kernel, "field_last", V, _LAST + ["base", "gain"], outs, scratch))
    names = ["t1", "h1", "down", "up", "t_lo", "t_hi", "lab", "prior", "loss"]
    shape = (2, 2, AZ + 2, RAD)
    scratch = {"t2": _OWN, "own1": shape, "beside1": shape}
    out = _call(_second_kernel, "second_sweep", V, names, {"blocks": (SEC, NG, RL, G * AZ)}, scratch)
    temperature = _temperature_take(lax.all_to_all(out["blocks"], "sec", 0, 0))
    return V["closing"], V["dissipation"], temperature


def solution(mesh):
    spec = P("ax", "sec", None)
    return jax.shard_map(
        shards,
        mesh=mesh,
        in_specs=(spec, P(None, "ax", "sec", None), spec, spec),
        out_specs=(spec, spec, spec),
        check_vma=False,
    )
```

```python
import functools
import math

import jax
import jax.numpy as jnp
from jax import lax
from jax.experimental import pallas as pl
from jax.experimental.pallas import tpu as pltpu
from jax.sharding import PartitionSpec as P

SAMPLES = 16
PERIOD = 32
SPAN = 8
DEPTH = SPAN // 2
FIRST_AT = (0, DEPTH, 2 * DEPTH, 3 * DEPTH, 4 * DEPTH)
NSEND = 5 * DEPTH
NLATEST = DEPTH + 1

F32 = jnp.float32
AX, AZ, RAD, ANG = 64, 16, 256, 512
SEC = 32
RL = RAD // SEC
G = 8
NG = AX // G
ENDS = (0, NG - 1)
HALF = RAD // 2


def _params(mib=16):
    return pltpu.CompilerParams(vmem_limit_bytes=mib * 2**20)


def _sds(*shape):
    return jax.ShapeDtypeStruct(shape, F32)


def _cost(flops, nbytes):
    return pl.CostEstimate(flops=flops, bytes_accessed=nbytes, transcendentals=0)


def _loop(n, body):
    def step(i, _):
        body(i)
        return 0

    lax.fori_loop(0, n, step, 0)


def _lockstep(chains):
    results = [None] * len(chains)
    going = dict(enumerate(chains))
    while going:
        for k in list(going):
            try:
                next(going[k])
            except StopIteration as end:
                results[k] = end.value
                del going[k]
    return results


def _pairs(body):
    _loop(NG // 2, lambda i: body([2 * i, 2 * i + 1]))


def _planes(g):
    return pl.ds(pl.multiple_of(g * G, G), G)


def _reluct(lab):
    return jnp.where(lab == 0, 0.05, jnp.where(lab == 3, 0.2, 0.24)).astype(F32)


def _sigma(lab):
    return jnp.where(lab == 0, 0.3, jnp.where(lab == 1, 1.0, jnp.where(lab == 2, 0.0, 0.6))).astype(F32)


def _driven(lab, x):
    return jnp.where((lab == 1) | (lab == 3), x, 0.0)


def _half_cond(lab, temp):
    half_k0 = jnp.where(lab == 0, 0.5, jnp.where(lab == 1, 0.75, jnp.where(lab == 2, 0.05, 0.2)))
    return half_k0 * (1.0 + 0.5 * jnp.tanh(temp))


def _capacity(lab):
    return jnp.where(lab == 1, 3.5, jnp.where(lab == 2, 0.5, 3.0)).astype(F32)


def _corner(first, latest_count, rows, consts, store, lane):
    top = 2 * DEPTH - 1 + latest_count - DEPTH
    level = {j: rows(j) for j in range(top + 1)}
    for t in range(latest_count):
        yield
        store(t, level[t])
        if t < DEPTH:
            store(latest_count + t, level[t + 1])
        level = {
            j: _step(first + t, level[j - 1], level[j], level[j + 1], *consts(j), lane)[0]
            for j in range(t + 1, top - t)
        }


def _edges_kernel(lab_hbm, exc_hbm, a_hbm, low_ref, high_ref, lab_v, exc_v, a_v, sems):
    copies = []
    for g in range(NG):
        at = pl.ds(g * G, G)
        copies.append(
            [
                pltpu.make_async_copy(lab_hbm.at[at], lab_v.at[at], sems.at[g, 0]),
                pltpu.make_async_copy(exc_hbm.at[0, at], exc_v.at[0, at], sems.at[g, 1]),
                pltpu.make_async_copy(exc_hbm.at[1, at], exc_v.at[1, at], sems.at[g, 2]),
                pltpu.make_async_copy(a_hbm.at[at], a_v.at[at], sems.at[g, 3]),
            ]
        )
        for copy in copies[-1]:
            copy.start()

    lane, _ = _iotas()

    def corner(g, out, row, a, c, s, lab):
        kept = {}
        for j in range(2 * DEPTH - 1):
            r = row(j)
            kept[j] = _reluct(lab[r]), _driven(lab[r], c[r]), _driven(lab[r], s[r])
            if j < DEPTH:
                out[FIRST_AT[2] + j, g] = lab[r].astype(F32)
                out[FIRST_AT[3] + j, g] = kept[j][1]
                out[FIRST_AT[4] + j, g] = kept[j][2]

        def store(k, x):
            out[k, g] = x

        return _corner(0, DEPTH, lambda j: a[row(j)], lambda j: kept[j], store, lane)

    for pair in range(NG // 2):
        chains = []
        for g in (2 * pair, 2 * pair + 1):
            for copy in copies[g]:
                copy.wait()
            at = pl.ds(g * G, G)
            given = [jnp.swapaxes(x, 0, 1) for x in (a_v[at], exc_v[0, at], exc_v[1, at], lab_v[at])]
            chains.append(corner(g, low_ref, lambda j: j, *given))
            chains.append(corner(g, high_ref, lambda j: AZ - 1 - j, *given))
        _lockstep(chains)


def _edges(labels, exc, a):
    return pl.pallas_call(
        _edges_kernel,
        in_specs=[pl.BlockSpec(memory_space=pl.ANY)] * 3,
        out_shape=[_sds(NSEND, NG, G, RAD)] * 2,
        scratch_shapes=[
            pltpu.VMEM((AX, AZ, RAD), jnp.int32),
            pltpu.VMEM((2, AX, AZ, RAD), F32),
            pltpu.VMEM((AX, AZ, RAD), F32),
            pltpu.SemaphoreType.DMA((NG, 4)),
        ],
        compiler_params=_params(56),
        cost_estimate=_cost(2**20, 6 * 2**20),
        name="edge_layers",
    )(labels, exc, a)


def _prepare_kernel(lab_ref, exc_ref, a_ref, latest, earlier, q, lab_out, nu_out, oc_out, os_out, bufs, a_v):
    lane, _ = _iotas()

    def group(g, k):
        at = _planes(g)
        lab = jnp.swapaxes(lab_ref[at], 0, 1)
        lab_out[:, g] = lab.astype(F32)
        nu_out[:, g] = _reluct(lab)
        oc_out[:, g] = _driven(lab, jnp.swapaxes(exc_ref[0, at], 0, 1))
        os_out[:, g] = _driven(lab, jnp.swapaxes(exc_ref[1, at], 0, 1))
        a_v[k] = jnp.swapaxes(a_ref[at], 0, 1)
        zero = jnp.zeros((G, RAD), F32)
        for r in (-1, 0, AZ - 1, AZ):
            q[r + 1, g] = zero

        def add_square(t, r, sq):
            q[r + 1, g] = sq if t == 0 else q[r + 1, g] + sq

        consts = [lambda r, ref=ref: ref[r, g] for ref in (nu_out, oc_out, os_out)]
        return _triangle(0, lambda r: a_v[k, r], consts, add_square, latest, earlier, g, bufs.at[k], lane)

    _pairs(lambda gs: _lockstep([group(g, k) for k, g in enumerate(gs)]))


def _prepare(labels, exc, a):
    return pl.pallas_call(
        _prepare_kernel,
        out_shape=[_sds(AZ, NG, G, RAD)] * 2 + [_sds(AZ + 2, NG, G, RAD)] + [_sds(AZ, NG, G, RAD)] * 4,
        scratch_shapes=[pltpu.VMEM((2, 2, AZ, G, RAD), F32), pltpu.VMEM((2, AZ, G, RAD), F32)],
        compiler_params=_params(),
        cost_estimate=_cost(2**22, 8 * 2**20),
        name="prepare",
    )(labels, exc, a)


PG = 16
NP = AX // PG


def _prior_send_kernel(prior_ref, out):
    for p in range(NP):
        x = prior_ref[p * PG : p * PG + PG]
        x = jnp.transpose(x.reshape(PG * RL, ANG)).reshape(SEC, AZ, PG * RL)
        out[:, p] = x
        for e, r in enumerate((AZ - 2, AZ - 1, 0, 1)):
            line = x[:, r : r + 1, :]
            at = slice(p * 4 + e, p * 4 + e + 1)
            if e < 2:
                out[1:, NP, at, :] = line[:-1]
                out[0:1, NP, at, :] = line[-1:]
            else:
                out[:-1, NP, at, :] = line[1:]
                out[SEC - 1 :, NP, at, :] = line[:1]


def _prior_send(prior):
    return pl.pallas_call(
        _prior_send_kernel,
        out_shape=_sds(SEC, NP + 1, AZ, PG * RL),
        compiler_params=_params(),
        cost_estimate=_cost(2**20, 3 * 2**20),
        name="prior_send",
    )(prior)


def _swap_blocks(x, lanes):
    count = 128 // lanes
    blk = lax.broadcasted_iota(jnp.int32, (8, 128), 1) // lanes
    x = list(x)
    b = count // 2
    while b:
        keep = (blk & b) == 0
        for j in range(count):
            if j & b == 0:
                p, q = x[j], x[j + b]
                x[j] = jnp.where(keep, p, pltpu.roll(q, b * lanes, 1))
                x[j + b] = jnp.where(keep, pltpu.roll(p, 128 - b * lanes, 1), q)
        b //= 2
    return x


def _prior_take_kernel(x_ref, out, more, nat):
    def fill(p):
        for tile in range(AZ // 8):
            rows = slice(tile * 8, tile * 8 + 8)
            for half in range(2):
                got = _swap_blocks([x_ref[half * PG + j, p, rows] for j in range(PG)], RL)
                for k in range(PG):
                    nat[k, rows, half * 128 : half * 128 + 128] = got[k]

    def block(p):
        fill(p)
        for k in range(PG // G):
            out[:, p * (PG // G) + k] = jnp.swapaxes(nat[k * G : k * G + G], 0, 1)

    _loop(NP, block)
    fill(NP)
    for k in range(PG // G):
        x = jnp.swapaxes(nat[k * G : k * G + G], 0, 1)
        for p in range(NP):
            more[:, p * (PG // G) + k] = x[p * 4 : p * 4 + 4]


def _prior_take(x):
    return pl.pallas_call(
        _prior_take_kernel,
        out_shape=[_sds(AZ, NG, G, RAD), _sds(4, NG, G, RAD)],
        scratch_shapes=[pltpu.VMEM((PG, AZ, RAD), F32)],
        compiler_params=_params(),
        cost_estimate=_cost(2**22, 3 * 2**20),
        name="prior_take",
    )(x)


def _temperature_take_kernel(x_ref, out, planes, sems):
    def copy(g):
        at = _planes(g)
        return pltpu.make_async_copy(planes.at[at], out.at[at], sems.at[g])

    def group(g):
        tiles = [_swap_blocks([x_ref[s * 8 + j, g] for j in range(8)], AZ) for s in range(SEC // 8)]
        for q in range(G):
            planes[g * G + q] = jnp.concatenate([t[q] for t in tiles], axis=1)
        copy(g).start()

    _loop(NG, group)
    for g in range(NG):
        copy(g).wait()


def _temperature_take(x):
    return pl.pallas_call(
        _temperature_take_kernel,
        out_shape=_sds(AX, RL, ANG),
        out_specs=pl.BlockSpec(memory_space=pl.ANY),
        scratch_shapes=[pltpu.VMEM((AX, RL, ANG), F32), pltpu.SemaphoreType.DMA((NG,))],
        compiler_params=_params(),
        cost_estimate=_cost(2**22, 2**21),
        name="temperature_take",
    )(x)


def _sides(x, lane):
    x0, x1 = x[:, :HALF], x[:, HALF:]
    f0, f1 = pltpu.roll(x0, 1, 1), pltpu.roll(x1, 1, 1)
    b0, b1 = pltpu.roll(x0, HALF - 1, 1), pltpu.roll(x1, HALF - 1, 1)
    at_low, at_high = lane == 0, lane == HALF - 1
    inward = jnp.concatenate([jnp.where(at_low, 0.0, f0), jnp.where(at_low, f0, f1)], axis=1)
    outward = jnp.concatenate([jnp.where(at_high, b1, b0), jnp.where(at_high, 0.0, b1)], axis=1)
    return inward, outward


def _axial(row, first, last, i, g, x, sub):
    before = pltpu.roll(row(i, g - 1), 1, 0) if g else first
    after = pltpu.roll(row(i, g + 1), G - 1, 0) if g < NG - 1 else last
    lower = jnp.where(sub == 0, before, pltpu.roll(x, 1, 0))
    return lower, jnp.where(sub == G - 1, after, pltpu.roll(x, G - 1, 0))


def _faces(t_row, h_row, i, g, beside, lane, sub):
    t, h = t_row(i, g), h_row(i, g)
    pairs = [(t_row(i - 1, g), h_row(i - 1, g)), (t_row(i + 1, g), h_row(i + 1, g))]
    pairs += list(zip(_sides(t, lane), _sides(h, lane)))
    if beside is None:
        (t_lo, h_lo), (t_hi, h_hi) = (t, -h), (t, -h)
    else:
        (t_lo, h_lo), (t_hi, h_hi) = beside
    pairs += list(zip(_axial(t_row, t_lo, t_hi, i, g, t, sub), _axial(h_row, h_lo, h_hi, i, g, h, sub)))
    flux, total = None, None
    for tn, hn in pairs:
        kf = h + hn
        term = kf * (tn - t)
        flux = term if flux is None else flux + term
        total = kf if total is None else total + kf
    return t, flux, total


def _iotas():
    lane = lax.broadcasted_iota(jnp.int32, (G, HALF), 1)
    sub = lax.broadcasted_iota(jnp.int32, (G, RAD), 0)
    return lane, sub


def _step(sample, down, mid, up, nu, oc, os, lane):
    phase = 2.0 * math.pi / PERIOD * sample
    cc, ss = math.cos(phase), math.sin(phase)
    inward, outward = _sides(mid, lane)
    source = cc * oc if sample == 0 else cc * oc + ss * os
    change = nu * ((down + up) + (inward + outward) - 4.0 * mid) + source
    return mid + change, change


def _triangle(first, rows, consts, add_square, latest, earlier, g, bufs, lane):
    nu, oc, os = consts

    def get(t, r):
        return rows(r) if t == 0 else bufs[(t - 1) % 2, r]

    latest[0, g] = rows(0)
    latest[AZ - 1, g] = rows(AZ - 1)
    earlier[1, g] = rows(1)
    earlier[AZ - 2, g] = rows(AZ - 2)
    for t in range(SPAN - 1):
        yield
        down, mid = get(t, t), get(t, t + 1)
        for r in range(t + 1, AZ - 1 - t):
            up = get(t, r + 1)
            new, change = _step(first + t, down, mid, up, nu(r), oc(r), os(r), lane)
            add_square(t, r, change * change)
            bufs[t % 2, r] = new
            if r in (t + 1, AZ - 2 - t):
                latest[r, g] = new
            elif r in (t + 2, AZ - 3 - t):
                earlier[r, g] = new
            down, mid = mid, up


def _valley(first, limit, own, halo, consts, add_square, bufs, final, lane):
    nu, oc, os = consts

    def get(t, x):
        j = x if x >= 0 else -1 - x
        if j < t:
            return bufs[(t - 1) % 2, x + DEPTH]
        latest, earlier = own if x >= 0 else halo
        if j == t or j == SPAN:
            return latest(j)
        return earlier(j)

    for t in range(SPAN):
        yield
        lo = -1 - min(t, limit - 1 - t)
        down, mid = get(t, lo - 1), get(t, lo)
        for x in range(lo, t + 1):
            up = get(t, x + 1)
            new, change = _step(first + t, down, mid, up, nu(x), oc(x), os(x), lane)
            if x >= -1:
                add_square(x, change * change)
            if t == SPAN - 1 and x >= 0:
                final(x, new)
            else:
                bufs[t % 2, x + DEPTH] = new
            down, mid = mid, up
    return bufs[SPAN % 2, DEPTH - 1]


_CONSTS = ["lab", "nu", "oc", "os", "f_low", "f_high"]
_STATE = ["latest", "earlier", "q"]


def _label(R, g):
    def get(r):
        if r < 0:
            return R["f_low"][FIRST_AT[2] - 1 - r, g]
        if r >= AZ:
            return R["f_high"][FIRST_AT[2] + r - AZ, g]
        return R["lab"][r, g]

    return get


def _fill(second, R, g, q_slot, final, bufs, lane):
    chains = []
    for high in (False, True):
        name = "high" if high else "low"
        consts_from = R["f_" + name]
        halo_from = R[name] if second else consts_from
        n = NLATEST if second else DEPTH

        def row(x, high=high):
            return AZ - 1 - x if high else x

        def const(name, k, row=row, consts_from=consts_from):
            return lambda x: R[name][row(x), g] if x >= 0 else consts_from[FIRST_AT[k] - 1 - x, g]

        kept = {}

        def nu(x, row=row, consts_from=consts_from, kept=kept):
            if x >= 0:
                return R["nu"][row(x), g]
            if x not in kept:
                kept[x] = _reluct(consts_from[FIRST_AT[2] - 1 - x, g])
            return kept[x]

        own = (lambda j, row=row: R["latest"][row(j), g], lambda j, row=row: R["earlier"][row(j), g])
        halo = (
            lambda j, halo_from=halo_from: halo_from[j, g],
            lambda j, halo_from=halo_from, n=n: halo_from[n + j - 1, g],
        )
        seen = set()

        def add_square(x, sq, row=row, seen=seen, high=high, halo=halo):
            r = row(x)
            if r in seen:
                before = R["q_out"][q_slot(r)]
            else:
                seen.add(r)
                before = R["q"][r + 1, g]
                if second and x < 0:
                    missed = halo[0](0) - R["gone"][int(high), g]
                    before = before + missed * missed
            R["q_out"][q_slot(r)] = before + sq

        chains.append(
            _valley(
                SPAN if second else 0,
                SPAN if second else SPAN - 1,
                own,
                halo,
                (nu, const("oc", 3), const("os", 4)),
                add_square,
                bufs.at[int(high)],
                lambda x, v, row=row: final(row(x), v),
                lane,
            )
        )
    return chains


def _middle_kernel(names, *refs):
    R = dict(zip(names, refs))
    lane, _ = _iotas()

    def groups(gs):
        chains = []
        for k, g in enumerate(gs):

            def final(r, v, g=g):
                R["rows8"][r, g] = v

            chains += _fill(False, R, g, lambda r, g=g: (r + 1, g), final, R["ends"].at[k], lane)
        gone = _lockstep(chains)
        chains = []
        for k, g in enumerate(gs):
            for end, (name, row) in enumerate((("e_low", lambda j: j), ("e_high", lambda j: AZ - 1 - j))):
                R["gone"][end, g] = gone[2 * k + end]

                def rows(j, g=g, row=row):
                    return R["rows8"][row(j), g]

                def consts(j, g=g, row=row):
                    return [R[c][row(j), g] for c in ("nu", "oc", "os")]

                def store(at, x, g=g, name=name):
                    R[name][at, g] = x

                chains.append(_corner(SPAN, NLATEST, rows, consts, store, lane))
        _lockstep(chains)

    _pairs(groups)


def _triangle_kernel(names, *refs):
    R = dict(zip(names, refs))
    lane, _ = _iotas()

    def group(g, k):
        q, q_out = R["q"], R["q_out"]
        for r in (-1, 0, AZ - 1, AZ):
            q_out[r + 1, g] = q[r + 1, g]

        def add_square(t, r, sq):
            q_out[r + 1, g] = (q if t == 0 else q_out)[r + 1, g] + sq

        consts = [lambda r, name=name: R[name][r, g] for name in ("nu", "oc", "os")]
        latest, earlier = R["latest_out"], R["earlier_out"]
        start = lambda r: R["rows8"][r, g]
        return _triangle(SPAN, start, consts, add_square, latest, earlier, g, R["bufs"].at[k], lane)

    _pairs(lambda gs: _lockstep([group(g, k) for k, g in enumerate(gs)]))


def _losses(R, gs, lane, store, final):
    chains = []
    for k, g in enumerate(gs):
        chains += _fill(
            True, R, g, lambda r, k=k: (k, r + 1), lambda r, v, k=k: final(k, r, v), R["ends"].at[k], lane
        )
    _lockstep(chains)
    for k, g in enumerate(gs):
        label = _label(R, g)
        for r in range(-1, AZ + 1):
            lab = label(r)
            store(k, r, _sigma(lab) * R["q_out"][k, r + 1], lab)


_T, _H, _J, _N, _L = range(5)
_END = (5, AZ + 2, RAD)


def _last(R, gs, lane, rows, send=None):
    def final(k, r, v):
        rows[k, r] = v

    def store(k, r, d, lab):
        g = gs[k]
        t = R["base"][r + 1, g] + d * R["gain"][r + 1, g]
        R["t1_out"][r + 1, g] = t
        R["h1_out"][r + 1, g] = _half_cond(lab, t)
        if 0 <= r < AZ:
            R["loss_out"][r, g] = d
        if send is not None:
            send(k, r, d)

    _losses(R, gs, lane, store, final)


def _last_ends_kernel(names, *refs):
    R = dict(zip(names, refs))
    lane, _ = _iotas()
    outs, parts = (R["down"], R["up"]), (R["part_lo"], R["part_hi"])
    for out, part in zip(outs, parts):
        out[...] = part[...]

    def send(k, r, d):
        at, q = slice(r + 1, r + 2), (0, G - 1)[k]
        outs[k][_N, at, :] = parts[k][_N, at, :] + d[q : q + 1]

    _last(R, ENDS, lane, R["end_rows"], send)


def _last_kernel(names, *refs):
    R = dict(zip(names, refs))
    lane, _ = _iotas()
    closing, dissipation = R["closing_v"], R["dissipation_v"]

    def copies(g):
        at = _planes(g)
        return [
            pltpu.make_async_copy(closing.at[at], R["closing"].at[at], R["sems"].at[0, g]),
            pltpu.make_async_copy(dissipation.at[at], R["dissipation"].at[at], R["sems"].at[1, g]),
        ]

    def natural(g, rows):
        closing[_planes(g)] = jnp.swapaxes(rows, 0, 1)
        dissipation[_planes(g)] = jnp.swapaxes(R["loss_out"][:, g], 0, 1)
        for copy in copies(g):
            copy.start()

    for k, g in enumerate(ENDS):
        natural(g, R["end_rows"][k])

    def groups(i):
        gs = [2 * i + 1, 2 * i + 2]
        _last(R, gs, lane, R["rows"])
        for k, g in enumerate(gs):
            natural(g, R["rows"][k])

    _loop(NG // 2 - 1, groups)
    for g in range(NG):
        for copy in copies(g):
            copy.wait()


def _second_kernel(names, *refs):
    R = dict(zip(names, refs))
    lane, sub = _iotas()
    ax = lax.axis_index("ax")
    exists = (ax > 0, ax < lax.axis_size("ax") - 1)
    for side, (own, other) in enumerate(((R["down"], R["t_lo"]), (R["up"], R["t_hi"]))):
        kf = own[_H] + other[_H]
        jump = kf * (other[_T] - own[_T])
        t = own[_T] + (own[_N] + jump) / (own[_J] + kf)
        R["own1"][side, 0] = t
        R["own1"][side, 1] = _half_cond(own[_L], t)
        t = other[_T] + (other[_N] - jump) / (other[_J] + kf)
        R["beside1"][side, 0] = jnp.where(exists[side], t, 0.0)
        R["beside1"][side, 1] = jnp.where(exists[side], _half_cond(other[_L], t), 0.0)

    def patched(name, k):
        def row(i, g):
            x = R[name][i, g]
            if g == ENDS[0]:
                x = jnp.where(sub == 0, R["own1"][0, k, pl.ds(i, 1), :], x)
            if g == ENDS[1]:
                x = jnp.where(sub == G - 1, R["own1"][1, k, pl.ds(i, 1), :], x)
            return x

        return row

    t_row, h_row = patched("t1", 0), patched("h1", 1)

    def row(r):
        at = pl.ds(r + 1, 1)
        beside = [[R["beside1"][side, k, at, :] for k in range(2)] for side in range(2)]
        for g in range(NG):
            t, flux, total = _faces(t_row, h_row, r + 1, g, beside, lane, sub)
            cap = _capacity(R["lab"][r, g])
            mismatch = cap * (t - R["prior"][r, g]) - flux - R["loss"][r, g]
            R["t2"][r, g] = t - mismatch / (cap + total)

    _loop(AZ, row)

    def turn(g):
        nat = jnp.swapaxes(R["t2"][:, g], 0, 1).reshape(G * AZ, RAD)
        R["blocks"][:, g] = jnp.transpose(nat).reshape(SEC, RL, G * AZ)

    _loop(NG, turn)


def _prior_row(R, g, r):
    if 0 <= r < AZ:
        return R["prior"][r, g]
    return R["prior_more"][r + 2 if r < 0 else r - AZ + 2, g]


def _ready_kernel(names, *refs):
    R = dict(zip(names, refs))
    lane, sub = _iotas()

    def fill(g):
        label = _label(R, g)
        for r in range(-2, AZ + 2):
            t, lab = _prior_row(R, g, r), label(r)
            R["t0"][r + 2, g] = t
            R["h0"][r + 2, g] = _half_cond(lab, t)
            R["cap"][r + 2, g] = _capacity(lab)

    _loop(NG, fill)

    def row(k):
        for g in range(NG):
            t, flux, total = _faces(
                lambda i, g: R["t0"][i, g], lambda i, g: R["h0"][i, g], k + 1, g, None, lane, sub
            )
            jac = R["cap"][k + 1, g] + total
            gain = 1.0 / jac
            R["base"][k, g] = t + flux * gain
            R["gain"][k, g] = gain
            if g in ENDS:
                end = 0 if g == ENDS[0] else 1
                R["jac"][end, k] = jac
                R["flux"][end, k] = flux

    _loop(AZ + 2, row)
    for end, (out, g, q) in enumerate(((R["part_lo"], ENDS[0], 0), (R["part_hi"], ENDS[1], G - 1))):
        label = _label(R, g)
        plane = slice(q, q + 1)
        for k in range(AZ + 2):
            at = slice(k, k + 1)
            out[_T, at, :] = R["t0"][k + 1, g, plane, :]
            out[_H, at, :] = R["h0"][k + 1, g, plane, :]
            out[_J, at, :] = R["jac"][end, k, plane, :]
            out[_N, at, :] = R["flux"][end, k, plane, :]
            out[_L, at, :] = label(k - 1)[plane]


def _call(kernel, name, given, names, outs, scratch, alias=(), apart=()):
    shapes = {key: pltpu.VMEM(shape, F32) for key, shape in scratch.items()}
    if apart:
        shapes["sems"] = pltpu.SemaphoreType.DMA((len(apart), NG))
    space = {True: pl.ANY, False: pltpu.VMEM}
    results = pl.pallas_call(
        functools.partial(kernel, names + list(outs) + list(shapes)),
        out_shape=[_sds(*shape) for shape in outs.values()],
        out_specs=[pl.BlockSpec(memory_space=space[key in apart]) for key in outs],
        scratch_shapes=list(shapes.values()),
        input_output_aliases={names.index(key): list(outs).index(key + "_out") for key in alias},
        compiler_params=_params(),
        cost_estimate=_cost(2**24, 2**23),
        name=name,
    )(*[given[key] for key in names])
    return dict(zip(outs, results))


_OWN = (AZ, NG, G, RAD)
_MORE = (AZ + 2, NG, G, RAD)
_ENDS = (2, 2, 2, SPAN + DEPTH, G, RAD)
_LAST = _CONSTS + _STATE + ["gone", "low", "high", "base", "gain"]
_PRIOR = ["lab", "f_low", "f_high", "prior", "prior_more"]


def _ring(axis, x, step, closed):
    count = lax.axis_size(axis)
    pairs = [(i, (i + 1) % count) for i in range(count if closed else count - 1)]
    return lax.ppermute(x, axis, pairs if step > 0 else [(b, a) for a, b in pairs])


def _around(low_edge, high_edge):
    return _ring("sec", high_edge, 1, True), _ring("sec", low_edge, -1, True)


def shards(labels, exc, a0, prior):
    V = {}
    V["f_low"], V["f_high"] = _around(*_edges(labels, exc, a0))
    got = lax.all_to_all(_prior_send(prior), "sec", 0, 0)
    V.update(zip(_STATE + _CONSTS[:4], _prepare(labels, exc, a0)))
    edge = (NLATEST + DEPTH, NG, G, RAD)
    outs = {"rows8": _OWN, "q_out": _MORE, "gone": (2, NG, G, RAD), "e_low": edge, "e_high": edge}
    out = _call(_middle_kernel, "field_middle", V, _CONSTS + _STATE, outs, {"ends": _ENDS})
    V["low"], V["high"] = _around(out["e_low"], out["e_high"])
    V.update(rows8=out["rows8"], q=out["q_out"], gone=out["gone"])
    outs = {"latest_out": _OWN, "earlier_out": _OWN, "q_out": _MORE}
    names = ["rows8", "q", "nu", "oc", "os"]
    out = _call(_triangle_kernel, "field_triangle", V, names, outs, {"bufs": (2, 2, AZ, G, RAD)})
    for name in _STATE:
        V[name] = out[name + "_out"]
    got, V["latest"] = lax.optimization_barrier((got, V["latest"]))
    V["prior"], V["prior_more"] = _prior_take(got)
    scratch = {name: (AZ + 4, NG, G, RAD) for name in ("t0", "h0", "cap")}
    scratch.update(jac=(2, AZ + 2, G, RAD), flux=(2, AZ + 2, G, RAD))
    outs = {"base": _MORE, "gain": _MORE, "part_lo": _END, "part_hi": _END}
    V.update(_call(_ready_kernel, "first_ready", V, _PRIOR, outs, scratch))
    scratch = {"q_out": (2, AZ + 2, G, RAD), "ends": _ENDS}
    state = {"t1_out": _MORE, "h1_out": _MORE, "loss_out": _OWN}
    outs = {**state, "down": _END, "up": _END, "end_rows": (2, AZ, G, RAD)}
    V.update(_call(_last_ends_kernel, "last_ends", V, _LAST + ["part_lo", "part_hi"], outs, scratch))
    V["t_lo"], V["t_hi"] = _ring("ax", V["up"], 1, False), _ring("ax", V["down"], -1, False)
    V.update(t1=V["t1_out"], h1=V["h1_out"], loss=V["loss_out"])
    results = {"closing": (AX, AZ, RAD), "dissipation": (AX, AZ, RAD)}
    scratch.update(rows=(2, AZ, G, RAD), closing_v=(AX, AZ, RAD), dissipation_v=(AX, AZ, RAD))
    names = _LAST + ["end_rows", "t1", "h1", "loss"]
    V.update(
        _call(_last_kernel, "field_last", V, names, {**results, **state}, scratch, ["t1", "h1", "loss"], list(results))
    )
    V.update(t1=V["t1_out"], h1=V["h1_out"], loss=V["loss_out"])
    names = ["t1", "h1", "down", "up", "t_lo", "t_hi", "lab", "prior", "loss"]
    shape = (2, 2, AZ + 2, RAD)
    scratch = {"t2": _OWN, "own1": shape, "beside1": shape}
    out = _call(_second_kernel, "second_sweep", V, names, {"blocks": (SEC, NG, RL, G * AZ)}, scratch)
    temperature = _temperature_take(lax.all_to_all(out["blocks"], "sec", 0, 0))
    return V["closing"], V["dissipation"], temperature


def solution(mesh):
    spec = P("ax", "sec", None)
    return jax.shard_map(
        shards,
        mesh=mesh,
        in_specs=(spec, P(None, "ax", "sec", None), spec, spec),
        out_specs=(spec, spec, spec),
        check_vma=False,
    )
```

```python
import functools
import math

import jax
import jax.numpy as jnp
from jax import lax
from jax.experimental import pallas as pl
from jax.experimental.pallas import tpu as pltpu
from jax.sharding import PartitionSpec as P

SAMPLES = 16
PERIOD = 32
SPAN = 8
DEPTH = SPAN // 2
FIRST_AT = (0, DEPTH, 2 * DEPTH, 3 * DEPTH, 4 * DEPTH)
NSEND = 5 * DEPTH
NLATEST = DEPTH + 1

F32 = jnp.float32
AX, AZ, RAD, ANG = 64, 16, 256, 512
SEC = 32
RL = RAD // SEC
G = 8
NG = AX // G
ENDS = (0, NG - 1)
HALF = RAD // 2


def _params(mib=16):
    return pltpu.CompilerParams(vmem_limit_bytes=mib * 2**20)


def _sds(*shape):
    return jax.ShapeDtypeStruct(shape, F32)


def _cost(flops, nbytes):
    return pl.CostEstimate(flops=flops, bytes_accessed=nbytes, transcendentals=0)


def _loop(n, body):
    def step(i, _):
        body(i)
        return 0

    lax.fori_loop(0, n, step, 0)


def _lockstep(chains):
    results = [None] * len(chains)
    going = dict(enumerate(chains))
    while going:
        for k in list(going):
            try:
                next(going[k])
            except StopIteration as end:
                results[k] = end.value
                del going[k]
    return results


def _pairs(body):
    _loop(NG // 2, lambda i: body([2 * i, 2 * i + 1]))


def _planes(g):
    return pl.ds(pl.multiple_of(g * G, G), G)


def _reluct(lab):
    return jnp.where(lab == 0, 0.05, jnp.where(lab == 3, 0.2, 0.24)).astype(F32)


def _sigma(lab):
    return jnp.where(lab == 0, 0.3, jnp.where(lab == 1, 1.0, jnp.where(lab == 2, 0.0, 0.6))).astype(F32)


def _driven(lab, x):
    return jnp.where((lab == 1) | (lab == 3), x, 0.0)


def _half_cond(lab, temp):
    half_k0 = jnp.where(lab == 0, 0.5, jnp.where(lab == 1, 0.75, jnp.where(lab == 2, 0.05, 0.2)))
    return half_k0 * (1.0 + 0.5 * jnp.tanh(temp))


def _capacity(lab):
    return jnp.where(lab == 1, 3.5, jnp.where(lab == 2, 0.5, 3.0)).astype(F32)


def _corner(first, latest_count, rows, consts, store, lane):
    top = 2 * DEPTH - 1 + latest_count - DEPTH
    level = {j: rows(j) for j in range(top + 1)}
    for t in range(latest_count):
        yield
        store(t, level[t])
        if t < DEPTH:
            store(latest_count + t, level[t + 1])
        level = {
            j: _step(first + t, level[j - 1], level[j], level[j + 1], *consts(j), lane)[0]
            for j in range(t + 1, top - t)
        }


def _edges_kernel(lab_hbm, exc_hbm, a_hbm, low_out, high_out, lab_v, exc_v, a_v, low_ref, high_ref, sems, out_sems):
    copies = []
    for g in range(NG):
        at = pl.ds(g * G, G)
        copies.append(
            [
                pltpu.make_async_copy(lab_hbm.at[at], lab_v.at[at], sems.at[g, 0]),
                pltpu.make_async_copy(exc_hbm.at[0, at], exc_v.at[0, at], sems.at[g, 1]),
                pltpu.make_async_copy(exc_hbm.at[1, at], exc_v.at[1, at], sems.at[g, 2]),
                pltpu.make_async_copy(a_hbm.at[at], a_v.at[at], sems.at[g, 3]),
            ]
        )
        for copy in copies[-1]:
            copy.start()

    lane, _ = _iotas()

    def sent(g):
        return [
            pltpu.make_async_copy(low_ref.at[:, g], low_out.at[:, g], out_sems.at[0, g]),
            pltpu.make_async_copy(high_ref.at[:, g], high_out.at[:, g], out_sems.at[1, g]),
        ]

    def corner(g, out, row, a, c, s, lab):
        kept = {}
        for j in range(2 * DEPTH - 1):
            r = row(j)
            kept[j] = _reluct(lab[r]), _driven(lab[r], c[r]), _driven(lab[r], s[r])
            if j < DEPTH:
                out[FIRST_AT[2] + j, g] = lab[r].astype(F32)
                out[FIRST_AT[3] + j, g] = kept[j][1]
                out[FIRST_AT[4] + j, g] = kept[j][2]

        def store(k, x):
            out[k, g] = x

        return _corner(0, DEPTH, lambda j: a[row(j)], lambda j: kept[j], store, lane)

    for pair in range(NG // 2):
        chains = []
        for g in (2 * pair, 2 * pair + 1):
            for copy in copies[g]:
                copy.wait()
            at = pl.ds(g * G, G)
            given = [jnp.swapaxes(x, 0, 1) for x in (a_v[at], exc_v[0, at], exc_v[1, at], lab_v[at])]
            chains.append(corner(g, low_ref, lambda j: j, *given))
            chains.append(corner(g, high_ref, lambda j: AZ - 1 - j, *given))
        _lockstep(chains)
        for g in (2 * pair, 2 * pair + 1):
            for copy in sent(g):
                copy.start()
    for g in range(NG):
        for copy in sent(g):
            copy.wait()


def _edges(labels, exc, a):
    return pl.pallas_call(
        _edges_kernel,
        in_specs=[pl.BlockSpec(memory_space=pl.ANY)] * 3,
        out_specs=[pl.BlockSpec(memory_space=pl.ANY)] * 2,
        out_shape=[_sds(NSEND, NG, G, RAD)] * 2,
        scratch_shapes=[
            pltpu.VMEM((AX, AZ, RAD), jnp.int32),
            pltpu.VMEM((2, AX, AZ, RAD), F32),
            pltpu.VMEM((AX, AZ, RAD), F32),
            pltpu.VMEM((NSEND, NG, G, RAD), F32),
            pltpu.VMEM((NSEND, NG, G, RAD), F32),
            pltpu.SemaphoreType.DMA((NG, 4)),
            pltpu.SemaphoreType.DMA((2, NG)),
        ],
        compiler_params=_params(56),
        cost_estimate=_cost(2**20, 6 * 2**20),
        name="edge_layers",
    )(labels, exc, a)


def _prepare_kernel(lab_ref, exc_ref, a_ref, latest, earlier, q, lab_out, nu_out, oc_out, os_out, bufs, a_v):
    lane, _ = _iotas()

    def group(g, k):
        at = _planes(g)
        lab = jnp.swapaxes(lab_ref[at], 0, 1)
        lab_out[:, g] = lab.astype(F32)
        nu_out[:, g] = _reluct(lab)
        oc_out[:, g] = _driven(lab, jnp.swapaxes(exc_ref[0, at], 0, 1))
        os_out[:, g] = _driven(lab, jnp.swapaxes(exc_ref[1, at], 0, 1))
        a_v[k] = jnp.swapaxes(a_ref[at], 0, 1)
        zero = jnp.zeros((G, RAD), F32)
        for r in (-1, 0, AZ - 1, AZ):
            q[r + 1, g] = zero

        def add_square(t, r, sq):
            q[r + 1, g] = sq if t == 0 else q[r + 1, g] + sq

        consts = [lambda r, ref=ref: ref[r, g] for ref in (nu_out, oc_out, os_out)]
        return _triangle(0, lambda r: a_v[k, r], consts, add_square, latest, earlier, g, bufs.at[k], lane)

    _pairs(lambda gs: _lockstep([group(g, k) for k, g in enumerate(gs)]))


def _prepare(labels, exc, a):
    return pl.pallas_call(
        _prepare_kernel,
        out_shape=[_sds(AZ, NG, G, RAD)] * 2 + [_sds(AZ + 2, NG, G, RAD)] + [_sds(AZ, NG, G, RAD)] * 4,
        scratch_shapes=[pltpu.VMEM((2, 2, AZ, G, RAD), F32), pltpu.VMEM((2, AZ, G, RAD), F32)],
        compiler_params=_params(),
        cost_estimate=_cost(2**22, 8 * 2**20),
        name="prepare",
    )(labels, exc, a)


PG = 16
NP = AX // PG


def _prior_send_kernel(prior_ref, out):
    for p in range(NP):
        x = prior_ref[p * PG : p * PG + PG]
        x = jnp.transpose(x.reshape(PG * RL, ANG)).reshape(SEC, AZ, PG * RL)
        out[:, p] = x
        for e, r in enumerate((AZ - 2, AZ - 1, 0, 1)):
            line = x[:, r : r + 1, :]
            at = slice(p * 4 + e, p * 4 + e + 1)
            if e < 2:
                out[1:, NP, at, :] = line[:-1]
                out[0:1, NP, at, :] = line[-1:]
            else:
                out[:-1, NP, at, :] = line[1:]
                out[SEC - 1 :, NP, at, :] = line[:1]


def _prior_send(prior):
    return pl.pallas_call(
        _prior_send_kernel,
        out_shape=_sds(SEC, NP + 1, AZ, PG * RL),
        compiler_params=_params(),
        cost_estimate=_cost(2**20, 3 * 2**20),
        name="prior_send",
    )(prior)


def _swap_blocks(x, lanes):
    count = 128 // lanes
    blk = lax.broadcasted_iota(jnp.int32, (8, 128), 1) // lanes
    x = list(x)
    b = count // 2
    while b:
        keep = (blk & b) == 0
        for j in range(count):
            if j & b == 0:
                p, q = x[j], x[j + b]
                x[j] = jnp.where(keep, p, pltpu.roll(q, b * lanes, 1))
                x[j + b] = jnp.where(keep, pltpu.roll(p, 128 - b * lanes, 1), q)
        b //= 2
    return x


def _prior_take_kernel(x_hbm, out, more, x_ref, nat, sems):
    copies = [pltpu.make_async_copy(x_hbm.at[:, p], x_ref.at[:, p], sems.at[p]) for p in range(NP + 1)]
    for copy in copies:
        copy.start()

    def fill(p):
        for tile in range(AZ // 8):
            rows = slice(tile * 8, tile * 8 + 8)
            for half in range(2):
                got = _swap_blocks([x_ref[half * PG + j, p, rows] for j in range(PG)], RL)
                for k in range(PG):
                    nat[k, rows, half * 128 : half * 128 + 128] = got[k]

    def block(p):
        pltpu.make_async_copy(x_hbm.at[:, p], x_ref.at[:, p], sems.at[p]).wait()
        fill(p)
        for k in range(PG // G):
            out[:, p * (PG // G) + k] = jnp.swapaxes(nat[k * G : k * G + G], 0, 1)

    _loop(NP, block)
    copies[NP].wait()
    fill(NP)
    for k in range(PG // G):
        x = jnp.swapaxes(nat[k * G : k * G + G], 0, 1)
        for p in range(NP):
            more[:, p * (PG // G) + k] = x[p * 4 : p * 4 + 4]


def _prior_take(x):
    return pl.pallas_call(
        _prior_take_kernel,
        in_specs=[pl.BlockSpec(memory_space=pl.ANY)],
        out_shape=[_sds(AZ, NG, G, RAD), _sds(4, NG, G, RAD)],
        scratch_shapes=[
            pltpu.VMEM((SEC, NP + 1, AZ, PG * RL), F32),
            pltpu.VMEM((PG, AZ, RAD), F32),
            pltpu.SemaphoreType.DMA((NP + 1,)),
        ],
        compiler_params=_params(),
        cost_estimate=_cost(2**24, 2**25),
        name="prior_take",
    )(x)


def _temperature_take_kernel(x_ref, out, planes, sems):
    def copy(g):
        at = _planes(g)
        return pltpu.make_async_copy(planes.at[at], out.at[at], sems.at[g])

    def group(g):
        for s in range(SEC // 8):
            got = _swap_blocks([x_ref[s * 8 + j, g] for j in range(8)], AZ)
            for q in range(G):
                planes[g * G + q, :, s * 128 : s * 128 + 128] = got[q]
        copy(g).start()

    _loop(NG, group)
    for g in range(NG):
        copy(g).wait()


def _temperature_take(x):
    return pl.pallas_call(
        _temperature_take_kernel,
        out_shape=_sds(AX, RL, ANG),
        out_specs=pl.BlockSpec(memory_space=pl.ANY),
        scratch_shapes=[pltpu.VMEM((AX, RL, ANG), F32), pltpu.SemaphoreType.DMA((NG,))],
        compiler_params=_params(),
        cost_estimate=_cost(2**22, 2**21),
        name="temperature_take",
    )(x)


def _sides(x, lane):
    x0, x1 = x[:, :HALF], x[:, HALF:]
    f0, f1 = pltpu.roll(x0, 1, 1), pltpu.roll(x1, 1, 1)
    b0, b1 = pltpu.roll(x0, HALF - 1, 1), pltpu.roll(x1, HALF - 1, 1)
    at_low, at_high = lane == 0, lane == HALF - 1
    inward = jnp.concatenate([jnp.where(at_low, 0.0, f0), jnp.where(at_low, f0, f1)], axis=1)
    outward = jnp.concatenate([jnp.where(at_high, b1, b0), jnp.where(at_high, 0.0, b1)], axis=1)
    return inward, outward


def _axial(row, first, last, i, g, x, sub):
    before = pltpu.roll(row(i, g - 1), 1, 0) if g else first
    after = pltpu.roll(row(i, g + 1), G - 1, 0) if g < NG - 1 else last
    lower = jnp.where(sub == 0, before, pltpu.roll(x, 1, 0))
    return lower, jnp.where(sub == G - 1, after, pltpu.roll(x, G - 1, 0))


def _faces(t_row, h_row, i, g, beside, lane, sub):
    t, h = t_row(i, g), h_row(i, g)
    pairs = [(t_row(i - 1, g), h_row(i - 1, g)), (t_row(i + 1, g), h_row(i + 1, g))]
    pairs += list(zip(_sides(t, lane), _sides(h, lane)))
    if beside is None:
        (t_lo, h_lo), (t_hi, h_hi) = (t, -h), (t, -h)
    else:
        (t_lo, h_lo), (t_hi, h_hi) = beside
    pairs += list(zip(_axial(t_row, t_lo, t_hi, i, g, t, sub), _axial(h_row, h_lo, h_hi, i, g, h, sub)))
    flux, total = None, None
    for tn, hn in pairs:
        kf = h + hn
        term = kf * (tn - t)
        flux = term if flux is None else flux + term
        total = kf if total is None else total + kf
    return t, flux, total


def _iotas():
    lane = lax.broadcasted_iota(jnp.int32, (G, HALF), 1)
    sub = lax.broadcasted_iota(jnp.int32, (G, RAD), 0)
    return lane, sub


def _step(sample, down, mid, up, nu, oc, os, lane):
    phase = 2.0 * math.pi / PERIOD * sample
    cc, ss = math.cos(phase), math.sin(phase)
    inward, outward = _sides(mid, lane)
    source = cc * oc if sample == 0 else cc * oc + ss * os
    change = nu * ((down + up) + (inward + outward) - 4.0 * mid) + source
    return mid + change, change


def _triangle(first, rows, consts, add_square, latest, earlier, g, bufs, lane):
    nu, oc, os = consts

    def get(t, r):
        return rows(r) if t == 0 else bufs[(t - 1) % 2, r]

    latest[0, g] = rows(0)
    latest[AZ - 1, g] = rows(AZ - 1)
    earlier[1, g] = rows(1)
    earlier[AZ - 2, g] = rows(AZ - 2)
    for t in range(SPAN - 1):
        yield
        down, mid = get(t, t), get(t, t + 1)
        for r in range(t + 1, AZ - 1 - t):
            up = get(t, r + 1)
            new, change = _step(first + t, down, mid, up, nu(r), oc(r), os(r), lane)
            add_square(t, r, change * change)
            bufs[t % 2, r] = new
            if r in (t + 1, AZ - 2 - t):
                latest[r, g] = new
            elif r in (t + 2, AZ - 3 - t):
                earlier[r, g] = new
            down, mid = mid, up


def _valley(first, limit, own, halo, consts, add_square, bufs, final, lane):
    nu, oc, os = consts

    def get(t, x):
        j = x if x >= 0 else -1 - x
        if j < t:
            return bufs[(t - 1) % 2, x + DEPTH]
        latest, earlier = own if x >= 0 else halo
        if j == t or j == SPAN:
            return latest(j)
        return earlier(j)

    for t in range(SPAN):
        yield
        lo = -1 - min(t, limit - 1 - t)
        down, mid = get(t, lo - 1), get(t, lo)
        for x in range(lo, t + 1):
            up = get(t, x + 1)
            new, change = _step(first + t, down, mid, up, nu(x), oc(x), os(x), lane)
            if x >= -1:
                add_square(x, change * change)
            if t == SPAN - 1 and x >= 0:
                final(x, new)
            else:
                bufs[t % 2, x + DEPTH] = new
            down, mid = mid, up
    return bufs[SPAN % 2, DEPTH - 1]


_CONSTS = ["nu", "oc", "os"]
_STATE = ["latest", "earlier", "q"]


def _label(R, g):
    def get(r):
        if 0 <= r < AZ:
            return R["lab"][r, g]
        return R["lab_more"][r + 2 if r < 0 else r - AZ + 2, g]

    return get


def _fill(second, R, g, q_slot, final, bufs, lane):
    chains = []
    for high in (False, True):
        name = "high" if high else "low"
        consts_from = R["f_" + name]
        halo_from = R[name] if second else consts_from
        n = NLATEST if second else DEPTH

        def row(x, high=high):
            return AZ - 1 - x if high else x

        def const(name, k, row=row, consts_from=consts_from):
            return lambda x: R[name][row(x), g] if x >= 0 else consts_from[FIRST_AT[k] - 1 - x, g]

        kept = {}

        def nu(x, row=row, consts_from=consts_from, kept=kept):
            if x >= 0:
                return R["nu"][row(x), g]
            if x not in kept:
                kept[x] = _reluct(consts_from[FIRST_AT[2] - 1 - x, g])
            return kept[x]

        own = (lambda j, row=row: R["latest"][row(j), g], lambda j, row=row: R["earlier"][row(j), g])
        halo = (
            lambda j, halo_from=halo_from: halo_from[j, g],
            lambda j, halo_from=halo_from, n=n: halo_from[n + j - 1, g],
        )
        seen = set()

        def add_square(x, sq, row=row, seen=seen, high=high, halo=halo):
            r = row(x)
            if r in seen:
                before = R["q_out"][q_slot(r)]
            else:
                seen.add(r)
                before = R["q"][r + 1, g]
                if second and x < 0:
                    missed = halo[0](0) - R["gone"][int(high), g]
                    before = before + missed * missed
            R["q_out"][q_slot(r)] = before + sq

        chains.append(
            _valley(
                SPAN if second else 0,
                SPAN if second else SPAN - 1,
                own,
                halo,
                (nu, const("oc", 3), const("os", 4)),
                add_square,
                bufs.at[int(high)],
                lambda x, v, row=row: final(row(x), v),
                lane,
            )
        )
    return chains


def _middle_kernel(names, *refs):
    R = dict(zip(names, refs))
    lane, _ = _iotas()
    for g in range(NG):
        for copy in _fetch(R, g):
            copy.start()

    def sent(g):
        return [
            pltpu.make_async_copy(R[name + "_v"].at[:, g], R[name].at[:, g], R["sems"].at[k, g])
            for k, name in enumerate(("e_low", "e_high"))
        ]

    def groups(gs):
        for g in gs:
            for copy in _fetch(R, g):
                copy.wait()
        chains = []
        for k, g in enumerate(gs):

            def final(r, v, g=g):
                R["rows8"][r, g] = v

            chains += _fill(False, R, g, lambda r, g=g: (r + 1, g), final, R["ends"].at[k], lane)
        gone = _lockstep(chains)
        chains = []
        for k, g in enumerate(gs):
            at = FIRST_AT[2]
            R["lab_more"][0, g], R["lab_more"][1, g] = R["f_low"][at + 1, g], R["f_low"][at, g]
            R["lab_more"][2, g], R["lab_more"][3, g] = R["f_high"][at, g], R["f_high"][at + 1, g]
            for end, (name, row) in enumerate((("e_low", lambda j: j), ("e_high", lambda j: AZ - 1 - j))):
                R["gone"][end, g] = gone[2 * k + end]

                def rows(j, g=g, row=row):
                    return R["rows8"][row(j), g]

                def consts(j, g=g, row=row):
                    return [R[c][row(j), g] for c in ("nu", "oc", "os")]

                def store(at, x, g=g, name=name):
                    R[name + "_v"][at, g] = x

                chains.append(_corner(SPAN, NLATEST, rows, consts, store, lane))
        _lockstep(chains)
        for g in gs:
            for copy in sent(g):
                copy.start()

    _pairs(groups)
    for g in range(NG):
        for copy in sent(g):
            copy.wait()


def _triangle_kernel(names, *refs):
    R = dict(zip(names, refs))
    lane, _ = _iotas()

    def group(g, k):
        q, q_out = R["q"], R["q_out"]
        for r in (-1, 0, AZ - 1, AZ):
            q_out[r + 1, g] = q[r + 1, g]

        def add_square(t, r, sq):
            q_out[r + 1, g] = (q if t == 0 else q_out)[r + 1, g] + sq

        consts = [lambda r, name=name: R[name][r, g] for name in ("nu", "oc", "os")]
        latest, earlier = R["latest_out"], R["earlier_out"]
        start = lambda r: R["rows8"][r, g]
        return _triangle(SPAN, start, consts, add_square, latest, earlier, g, R["bufs"].at[k], lane)

    _pairs(lambda gs: _lockstep([group(g, k) for k, g in enumerate(gs)]))


def _losses(R, gs, lane, store, final):
    chains = []
    for k, g in enumerate(gs):
        chains += _fill(
            True, R, g, lambda r, k=k: (k, r + 1), lambda r, v, k=k: final(k, r, v), R["ends"].at[k], lane
        )
    _lockstep(chains)
    for k, g in enumerate(gs):
        label = _label(R, g)
        for r in range(-1, AZ + 1):
            lab = label(r)
            store(k, r, _sigma(lab) * R["q_out"][k, r + 1], lab)


_T, _H, _J, _N, _L = range(5)
_END = (5, AZ + 2, RAD)


def _last(R, gs, lane, rows, send=None):
    def final(k, r, v):
        rows[k, r] = v

    def store(k, r, d, lab):
        g = gs[k]
        t = R["base"][r + 1, g] + d * R["gain"][r + 1, g]
        R["t1_out"][r + 1, g] = t
        R["h1_out"][r + 1, g] = _half_cond(lab, t)
        if 0 <= r < AZ:
            R["loss_out"][r, g] = d
        if send is not None:
            send(k, r, d)

    _losses(R, gs, lane, store, final)


def _last_ends_kernel(names, *refs):
    R = dict(zip(names, refs))
    lane, _ = _iotas()
    outs, parts = (R["down"], R["up"]), (R["part_lo"], R["part_hi"])
    copies = [copy for g in ENDS for copy in _fetch(R, g, FIRST_AT[2])]
    for copy in copies:
        copy.start()
    for out, part in zip(outs, parts):
        out[...] = part[...]
    for copy in copies:
        copy.wait()

    def send(k, r, d):
        at, q = slice(r + 1, r + 2), (0, G - 1)[k]
        outs[k][_N, at, :] = parts[k][_N, at, :] + d[q : q + 1]

    _last(R, ENDS, lane, R["end_rows"], send)


def _last_kernel(names, *refs):
    R = dict(zip(names, refs))
    lane, _ = _iotas()
    closing, dissipation = R["closing_v"], R["dissipation_v"]

    def copies(g):
        at = _planes(g)
        return [
            pltpu.make_async_copy(closing.at[at], R["closing"].at[at], R["sems"].at[0, g]),
            pltpu.make_async_copy(dissipation.at[at], R["dissipation"].at[at], R["sems"].at[1, g]),
        ]

    def natural(g, rows):
        closing[_planes(g)] = jnp.swapaxes(rows, 0, 1)
        dissipation[_planes(g)] = jnp.swapaxes(R["loss_out"][:, g], 0, 1)
        for copy in copies(g):
            copy.start()

    for g in range(1, NG - 1):
        for copy in _fetch(R, g, FIRST_AT[2]):
            copy.start()
    for k, g in enumerate(ENDS):
        natural(g, R["end_rows"][k])

    def groups(i):
        gs = [2 * i + 1, 2 * i + 2]
        for g in gs:
            for copy in _fetch(R, g, FIRST_AT[2]):
                copy.wait()
        _last(R, gs, lane, R["rows"])
        for k, g in enumerate(gs):
            natural(g, R["rows"][k])

    _loop(NG // 2 - 1, groups)
    for g in range(NG):
        for copy in copies(g):
            copy.wait()


def _second_kernel(names, *refs):
    R = dict(zip(names, refs))
    lane, sub = _iotas()
    ax = lax.axis_index("ax")
    exists = (ax > 0, ax < lax.axis_size("ax") - 1)
    for side, (own, other) in enumerate(((R["down"], R["t_lo"]), (R["up"], R["t_hi"]))):
        kf = own[_H] + other[_H]
        jump = kf * (other[_T] - own[_T])
        t = own[_T] + (own[_N] + jump) / (own[_J] + kf)
        R["own1"][side, 0] = t
        R["own1"][side, 1] = _half_cond(own[_L], t)
        t = other[_T] + (other[_N] - jump) / (other[_J] + kf)
        R["beside1"][side, 0] = jnp.where(exists[side], t, 0.0)
        R["beside1"][side, 1] = jnp.where(exists[side], _half_cond(other[_L], t), 0.0)

    def patched(name, k):
        def row(i, g):
            x = R[name][i, g]
            if g == ENDS[0]:
                x = jnp.where(sub == 0, R["own1"][0, k, pl.ds(i, 1), :], x)
            if g == ENDS[1]:
                x = jnp.where(sub == G - 1, R["own1"][1, k, pl.ds(i, 1), :], x)
            return x

        return row

    t_row, h_row = patched("t1", 0), patched("h1", 1)

    def row(r):
        at = pl.ds(r + 1, 1)
        beside = [[R["beside1"][side, k, at, :] for k in range(2)] for side in range(2)]
        for g in range(NG):
            t, flux, total = _faces(t_row, h_row, r + 1, g, beside, lane, sub)
            cap = _capacity(R["lab"][r, g])
            mismatch = cap * (t - R["prior"][r, g]) - flux - R["loss"][r, g]
            R["t2"][r, g] = t - mismatch / (cap + total)

    _loop(AZ, row)

    def turn(i):
        for g in [4 * i + k for k in range(4)]:
            nat = jnp.swapaxes(R["t2"][:, g], 0, 1).reshape(G * AZ, RAD)
            R["blocks"][:, g] = jnp.transpose(nat).reshape(SEC, RL, G * AZ)

    _loop(NG // 4, turn)


def _prior_row(R, g, r):
    if 0 <= r < AZ:
        return R["prior"][r, g]
    return R["prior_more"][r + 2 if r < 0 else r - AZ + 2, g]


def _warmth_kernel(names, *refs):
    R = dict(zip(names, refs))

    def fill(g):
        label = _label(R, g)
        for r in range(-2, AZ + 2):
            t, lab = _prior_row(R, g, r), label(r)
            R["t0"][r + 2, g] = t
            R["h0"][r + 2, g] = _half_cond(lab, t)
            R["cap"][r + 2, g] = _capacity(lab)

    _loop(NG, fill)


def _ready_kernel(names, *refs):
    R = dict(zip(names, refs))
    lane, sub = _iotas()

    def row(k):
        for g in range(NG):
            t, flux, total = _faces(
                lambda i, g: R["t0"][i, g], lambda i, g: R["h0"][i, g], k + 1, g, None, lane, sub
            )
            jac = R["cap"][k + 1, g] + total
            gain = 1.0 / jac
            R["base"][k, g] = t + flux * gain
            R["gain"][k, g] = gain
            if g in ENDS:
                end = 0 if g == ENDS[0] else 1
                R["jac"][end, k] = jac
                R["flux"][end, k] = flux

    _loop(AZ + 2, row)
    for end, (out, g, q) in enumerate(((R["part_lo"], ENDS[0], 0), (R["part_hi"], ENDS[1], G - 1))):
        label = _label(R, g)
        plane = slice(q, q + 1)
        for k in range(AZ + 2):
            at = slice(k, k + 1)
            out[_T, at, :] = R["t0"][k + 1, g, plane, :]
            out[_H, at, :] = R["h0"][k + 1, g, plane, :]
            out[_J, at, :] = R["jac"][end, k, plane, :]
            out[_N, at, :] = R["flux"][end, k, plane, :]
            out[_L, at, :] = label(k - 1)[plane]


def _fetch(R, g, skip=0):
    copies = []
    for k, name in enumerate(sorted(key for key in R if "apart " + key in R)):
        lo = skip if name.startswith("f_") else 0
        at = pl.ds(lo, R[name].shape[0] - lo)
        copies.append(pltpu.make_async_copy(R["apart " + name].at[at, g], R[name].at[at, g], R["in_sems"].at[k, g]))
    return copies


def _call(kernel, name, given, names, outs, scratch, alias=(), apart=(), fetch=()):
    given = {**given, **{"apart " + key: given[key] for key in fetch}}
    names = names + ["apart " + key for key in fetch]
    shapes = {key: pltpu.VMEM(shape, F32) for key, shape in scratch.items()}
    shapes.update({key: pltpu.VMEM(given[key].shape, F32) for key in fetch})
    if fetch:
        shapes["in_sems"] = pltpu.SemaphoreType.DMA((len(fetch), NG))
    if apart:
        shapes["sems"] = pltpu.SemaphoreType.DMA((len(apart), NG))
    space = {True: pl.ANY, False: pltpu.VMEM}
    results = pl.pallas_call(
        functools.partial(kernel, names + list(outs) + list(shapes)),
        out_shape=[_sds(*shape) for shape in outs.values()],
        in_specs=[pl.BlockSpec(memory_space=space[key.startswith("apart ")]) for key in names],
        out_specs=[pl.BlockSpec(memory_space=space[key in apart]) for key in outs],
        scratch_shapes=list(shapes.values()),
        input_output_aliases={names.index(key): list(outs).index(key + "_out") for key in alias},
        compiler_params=_params(),
        cost_estimate=_cost(2**24, 2**25),
        name=name,
    )(*[given[key] for key in names])
    return dict(zip(outs, results))


_OWN = (AZ, NG, G, RAD)
_MORE = (AZ + 2, NG, G, RAD)
_ENDS = (2, 2, 2, SPAN + DEPTH, G, RAD)
_LAST = _CONSTS + _STATE + ["lab", "lab_more", "gone", "base", "gain"]
_FETCH = ["f_low", "f_high", "low", "high"]
_PRIOR = ["lab", "lab_more", "prior", "prior_more"]


def _ring(axis, x, step, closed):
    count = lax.axis_size(axis)
    pairs = [(i, (i + 1) % count) for i in range(count if closed else count - 1)]
    return lax.ppermute(x, axis, pairs if step > 0 else [(b, a) for a, b in pairs])


def _around(low_edge, high_edge):
    return _ring("sec", high_edge, 1, True), _ring("sec", low_edge, -1, True)


def shards(labels, exc, a0, prior):
    V = {}
    V["f_low"], V["f_high"] = _around(*_edges(labels, exc, a0))
    got = lax.all_to_all(_prior_send(prior), "sec", 0, 0)
    V.update(zip(_STATE + ["lab"] + _CONSTS, _prepare(labels, exc, a0)))
    edge = (NLATEST + DEPTH, NG, G, RAD)
    outs = {"rows8": _OWN, "q_out": _MORE, "gone": (2, NG, G, RAD), "lab_more": (4, NG, G, RAD)}
    outs.update(e_low=edge, e_high=edge)
    scratch = {"ends": _ENDS, "e_low_v": edge, "e_high_v": edge}
    out = _call(_middle_kernel, "field_middle", V, _CONSTS + _STATE, outs, scratch, (), ["e_low", "e_high"], ["f_low", "f_high"])
    V["low"], V["high"] = _around(out["e_low"], out["e_high"])
    V.update(rows8=out["rows8"], q=out["q_out"], gone=out["gone"], lab_more=out["lab_more"])
    outs = {"latest_out": _OWN, "earlier_out": _OWN, "q_out": _MORE}
    names = ["rows8", "q", "nu", "oc", "os"]
    out = _call(_triangle_kernel, "field_triangle", V, names, outs, {"bufs": (2, 2, AZ, G, RAD)})
    for name in _STATE:
        V[name] = out[name + "_out"]
    got, V["latest"] = lax.optimization_barrier((got, V["latest"]))
    V["prior"], V["prior_more"] = _prior_take(got)
    warmth = {name: (AZ + 4, NG, G, RAD) for name in ("t0", "h0", "cap")}
    V.update(_call(_warmth_kernel, "prior_warmth", V, _PRIOR, warmth, {}))
    scratch = {"jac": (2, AZ + 2, G, RAD), "flux": (2, AZ + 2, G, RAD)}
    outs = {"base": _MORE, "gain": _MORE, "part_lo": _END, "part_hi": _END}
    V.update(_call(_ready_kernel, "first_ready", V, ["lab", "lab_more", *warmth], outs, scratch))
    scratch = {"q_out": (2, AZ + 2, G, RAD), "ends": _ENDS}
    state = {"t1_out": _MORE, "h1_out": _MORE, "loss_out": _OWN}
    names = _LAST + ["part_lo", "part_hi"]
    outs = {**state, "down": _END, "up": _END, "end_rows": (2, AZ, G, RAD)}
    V.update(_call(_last_ends_kernel, "last_ends", V, names, outs, scratch, fetch=_FETCH))
    V["t_lo"], V["t_hi"] = _ring("ax", V["up"], 1, False), _ring("ax", V["down"], -1, False)
    V.update(t1=V["t1_out"], h1=V["h1_out"], loss=V["loss_out"])
    results = {"closing": (AX, AZ, RAD), "dissipation": (AX, AZ, RAD)}
    scratch.update(rows=(2, AZ, G, RAD), closing_v=(AX, AZ, RAD), dissipation_v=(AX, AZ, RAD))
    names = _LAST + ["end_rows", "t1", "h1", "loss"]
    outs = {**results, **state}
    V.update(
        _call(_last_kernel, "field_last", V, names, outs, scratch, ["t1", "h1", "loss"], list(results), _FETCH)
    )
    V.update(t1=V["t1_out"], h1=V["h1_out"], loss=V["loss_out"])
    names = ["t1", "h1", "down", "up", "t_lo", "t_hi", "lab", "prior", "loss"]
    shape = (2, 2, AZ + 2, RAD)
    scratch = {"t2": _OWN, "own1": shape, "beside1": shape}
    out = _call(_second_kernel, "second_sweep", V, names, {"blocks": (SEC, NG, RL, G * AZ)}, scratch)
    temperature = _temperature_take(lax.all_to_all(out["blocks"], "sec", 0, 0))
    return V["closing"], V["dissipation"], temperature


def solution(mesh):
    spec = P("ax", "sec", None)
    return jax.shard_map(
        shards,
        mesh=mesh,
        in_specs=(spec, P(None, "ax", "sec", None), spec, spec),
        out_specs=(spec, spec, spec),
        check_vma=False,
    )
```

```python
import functools
import math

import jax
import jax.numpy as jnp
from jax import lax
from jax.experimental import pallas as pl
from jax.experimental.pallas import tpu as pltpu
from jax.sharding import PartitionSpec as P

SAMPLES = 16
PERIOD = 32
SPAN = 8
DEPTH = SPAN // 2
FIRST_AT = (0, DEPTH, 2 * DEPTH, 3 * DEPTH, 4 * DEPTH)
NSEND = 5 * DEPTH
NLATEST = DEPTH + 1

F32 = jnp.float32
AX, AZ, RAD, ANG = 64, 16, 256, 512
SEC = 32
RL = RAD // SEC
G = 8
NG = AX // G
ENDS = (0, NG - 1)
HALF = RAD // 2


def _params(mib=16):
    return pltpu.CompilerParams(vmem_limit_bytes=mib * 2**20)


def _sds(*shape):
    return jax.ShapeDtypeStruct(shape, F32)


def _cost(flops, nbytes):
    return pl.CostEstimate(flops=flops, bytes_accessed=nbytes, transcendentals=0)


def _loop(n, body):
    def step(i, _):
        body(i)
        return 0

    lax.fori_loop(0, n, step, 0)


def _lockstep(chains):
    results = [None] * len(chains)
    going = dict(enumerate(chains))
    while going:
        for k in list(going):
            try:
                next(going[k])
            except StopIteration as end:
                results[k] = end.value
                del going[k]
    return results


def _pairs(body):
    _loop(NG // 2, lambda i: body([2 * i, 2 * i + 1]))


def _planes(g):
    return pl.ds(pl.multiple_of(g * G, G), G)


def _reluct(lab):
    return jnp.where(lab == 0, 0.05, jnp.where(lab == 3, 0.2, 0.24)).astype(F32)


def _sigma(lab):
    return jnp.where(lab == 0, 0.3, jnp.where(lab == 1, 1.0, jnp.where(lab == 2, 0.0, 0.6))).astype(F32)


def _driven(lab, x):
    return jnp.where((lab == 1) | (lab == 3), x, 0.0)


def _half_cond(lab, temp):
    half_k0 = jnp.where(lab == 0, 0.5, jnp.where(lab == 1, 0.75, jnp.where(lab == 2, 0.05, 0.2)))
    return half_k0 * (1.0 + 0.5 * jnp.tanh(temp))


def _capacity(lab):
    return jnp.where(lab == 1, 3.5, jnp.where(lab == 2, 0.5, 3.0)).astype(F32)


def _corner(first, latest_count, rows, consts, store, lane):
    top = 2 * DEPTH - 1 + latest_count - DEPTH
    level = {j: rows(j) for j in range(top + 1)}
    for t in range(latest_count):
        yield
        store(t, level[t])
        if t < DEPTH:
            store(latest_count + t, level[t + 1])
        level = {
            j: _step(first + t, level[j - 1], level[j], level[j + 1], *consts(j), lane)[0]
            for j in range(t + 1, top - t)
        }


def _edges_kernel(lab_hbm, exc_hbm, a_hbm, low_out, high_out, lab_v, exc_v, a_v, low_ref, high_ref, sems, out_sems):
    copies = []
    for g in range(NG):
        at = pl.ds(g * G, G)
        copies.append(
            [
                pltpu.make_async_copy(lab_hbm.at[at], lab_v.at[at], sems.at[g, 0]),
                pltpu.make_async_copy(exc_hbm.at[0, at], exc_v.at[0, at], sems.at[g, 1]),
                pltpu.make_async_copy(exc_hbm.at[1, at], exc_v.at[1, at], sems.at[g, 2]),
                pltpu.make_async_copy(a_hbm.at[at], a_v.at[at], sems.at[g, 3]),
            ]
        )
        for copy in copies[-1]:
            copy.start()

    lane, _ = _iotas()

    def sent(g):
        return [
            pltpu.make_async_copy(low_ref.at[:, g], low_out.at[:, g], out_sems.at[0, g]),
            pltpu.make_async_copy(high_ref.at[:, g], high_out.at[:, g], out_sems.at[1, g]),
        ]

    def corner(g, out, row, a, c, s, lab):
        kept = {}
        for j in range(2 * DEPTH - 1):
            r = row(j)
            kept[j] = _reluct(lab[r]), _driven(lab[r], c[r]), _driven(lab[r], s[r])
            if j < DEPTH:
                out[FIRST_AT[2] + j, g] = lab[r].astype(F32)
                out[FIRST_AT[3] + j, g] = kept[j][1]
                out[FIRST_AT[4] + j, g] = kept[j][2]

        def store(k, x):
            out[k, g] = x

        return _corner(0, DEPTH, lambda j: a[row(j)], lambda j: kept[j], store, lane)

    for pair in range(NG // 2):
        chains = []
        for g in (2 * pair, 2 * pair + 1):
            for copy in copies[g]:
                copy.wait()
            at = pl.ds(g * G, G)
            given = [jnp.swapaxes(x, 0, 1) for x in (a_v[at], exc_v[0, at], exc_v[1, at], lab_v[at])]
            chains.append(corner(g, low_ref, lambda j: j, *given))
            chains.append(corner(g, high_ref, lambda j: AZ - 1 - j, *given))
        _lockstep(chains)
        for g in (2 * pair, 2 * pair + 1):
            for copy in sent(g):
                copy.start()
    for g in range(NG):
        for copy in sent(g):
            copy.wait()


def _edges(labels, exc, a):
    return pl.pallas_call(
        _edges_kernel,
        in_specs=[pl.BlockSpec(memory_space=pl.ANY)] * 3,
        out_specs=[pl.BlockSpec(memory_space=pl.ANY)] * 2,
        out_shape=[_sds(NSEND, NG, G, RAD)] * 2,
        scratch_shapes=[
            pltpu.VMEM((AX, AZ, RAD), jnp.int32),
            pltpu.VMEM((2, AX, AZ, RAD), F32),
            pltpu.VMEM((AX, AZ, RAD), F32),
            pltpu.VMEM((NSEND, NG, G, RAD), F32),
            pltpu.VMEM((NSEND, NG, G, RAD), F32),
            pltpu.SemaphoreType.DMA((NG, 4)),
            pltpu.SemaphoreType.DMA((2, NG)),
        ],
        compiler_params=_params(56),
        cost_estimate=_cost(2**20, 6 * 2**20),
        name="edge_layers",
    )(labels, exc, a)


def _prepare_kernel(lab_ref, exc_ref, a_ref, latest, earlier, q, lab_out, nu_out, oc_out, os_out, bufs, a_v):
    lane, _ = _iotas()

    def group(g, k):
        at = _planes(g)
        lab = jnp.swapaxes(lab_ref[at], 0, 1)
        lab_out[:, g] = lab.astype(F32)
        nu_out[:, g] = _reluct(lab)
        oc_out[:, g] = _driven(lab, jnp.swapaxes(exc_ref[0, at], 0, 1))
        os_out[:, g] = _driven(lab, jnp.swapaxes(exc_ref[1, at], 0, 1))
        a_v[k] = jnp.swapaxes(a_ref[at], 0, 1)
        zero = jnp.zeros((G, RAD), F32)
        for r in (-1, 0, AZ - 1, AZ):
            q[r + 1, g] = zero

        def add_square(t, r, sq):
            q[r + 1, g] = sq if t == 0 else q[r + 1, g] + sq

        consts = [lambda r, ref=ref: ref[r, g] for ref in (nu_out, oc_out, os_out)]
        return _triangle(0, lambda r: a_v[k, r], consts, add_square, latest, earlier, g, bufs.at[k], lane)

    _pairs(lambda gs: _lockstep([group(g, k) for k, g in enumerate(gs)]))


def _prepare(labels, exc, a):
    return pl.pallas_call(
        _prepare_kernel,
        out_shape=[_sds(AZ, NG, G, RAD)] * 2 + [_sds(AZ + 2, NG, G, RAD)] + [_sds(AZ, NG, G, RAD)] * 4,
        scratch_shapes=[pltpu.VMEM((2, 2, AZ, G, RAD), F32), pltpu.VMEM((2, AZ, G, RAD), F32)],
        compiler_params=_params(),
        cost_estimate=_cost(2**22, 8 * 2**20),
        name="prepare",
    )(labels, exc, a)


PG = 16
NP = AX // PG


def _prior_send_kernel(prior_ref, out):
    for p in range(NP):
        x = prior_ref[p * PG : p * PG + PG]
        x = jnp.transpose(x.reshape(PG * RL, ANG)).reshape(SEC, AZ, PG * RL)
        out[:, p] = x
        for e, r in enumerate((AZ - 2, AZ - 1, 0, 1)):
            line = x[:, r : r + 1, :]
            at = slice(p * 4 + e, p * 4 + e + 1)
            if e < 2:
                out[1:, NP, at, :] = line[:-1]
                out[0:1, NP, at, :] = line[-1:]
            else:
                out[:-1, NP, at, :] = line[1:]
                out[SEC - 1 :, NP, at, :] = line[:1]


def _prior_send(prior):
    return pl.pallas_call(
        _prior_send_kernel,
        out_shape=_sds(SEC, NP + 1, AZ, PG * RL),
        compiler_params=_params(),
        cost_estimate=_cost(2**20, 3 * 2**20),
        name="prior_send",
    )(prior)


def _swap_blocks(x, lanes):
    count = 128 // lanes
    blk = lax.broadcasted_iota(jnp.int32, (8, 128), 1) // lanes
    x = list(x)
    b = count // 2
    while b:
        keep = (blk & b) == 0
        for j in range(count):
            if j & b == 0:
                p, q = x[j], x[j + b]
                x[j] = jnp.where(keep, p, pltpu.roll(q, b * lanes, 1))
                x[j + b] = jnp.where(keep, pltpu.roll(p, 128 - b * lanes, 1), q)
        b //= 2
    return x


def _prior_take_kernel(x_hbm, out, more, x_ref, nat, sems):
    copies = [pltpu.make_async_copy(x_hbm.at[:, p], x_ref.at[:, p], sems.at[p]) for p in range(NP + 1)]
    for copy in copies:
        copy.start()

    def fill(p):
        for tile in range(AZ // 8):
            rows = slice(tile * 8, tile * 8 + 8)
            for half in range(2):
                got = _swap_blocks([x_ref[half * PG + j, p, rows] for j in range(PG)], RL)
                for k in range(PG):
                    nat[k, rows, half * 128 : half * 128 + 128] = got[k]

    def block(p):
        pltpu.make_async_copy(x_hbm.at[:, p], x_ref.at[:, p], sems.at[p]).wait()
        fill(p)
        for k in range(PG // G):
            out[:, p * (PG // G) + k] = jnp.swapaxes(nat[k * G : k * G + G], 0, 1)

    _loop(NP, block)
    copies[NP].wait()
    fill(NP)
    for k in range(PG // G):
        x = jnp.swapaxes(nat[k * G : k * G + G], 0, 1)
        for p in range(NP):
            more[:, p * (PG // G) + k] = x[p * 4 : p * 4 + 4]


def _prior_take(x):
    return pl.pallas_call(
        _prior_take_kernel,
        in_specs=[pl.BlockSpec(memory_space=pl.ANY)],
        out_shape=[_sds(AZ, NG, G, RAD), _sds(4, NG, G, RAD)],
        scratch_shapes=[
            pltpu.VMEM((SEC, NP + 1, AZ, PG * RL), F32),
            pltpu.VMEM((PG, AZ, RAD), F32),
            pltpu.SemaphoreType.DMA((NP + 1,)),
        ],
        compiler_params=_params(),
        cost_estimate=_cost(2**24, 2**25),
        name="prior_take",
    )(x)


def _temperature_take_kernel(x_ref, out, planes, sems):
    def copy(g):
        at = _planes(g)
        return pltpu.make_async_copy(planes.at[at], out.at[at], sems.at[g])

    def groups(gs):
        for g in gs:
            for s in range(SEC // 8):
                got = _swap_blocks([x_ref[s * 8 + j, g] for j in range(8)], AZ)
                for q in range(G):
                    planes[g * G + q, :, s * 128 : s * 128 + 128] = got[q]
        for g in gs:
            copy(g).start()

    _pairs(groups)
    for g in range(NG):
        copy(g).wait()


def _temperature_take(x):
    return pl.pallas_call(
        _temperature_take_kernel,
        out_shape=_sds(AX, RL, ANG),
        out_specs=pl.BlockSpec(memory_space=pl.ANY),
        scratch_shapes=[pltpu.VMEM((AX, RL, ANG), F32), pltpu.SemaphoreType.DMA((NG,))],
        compiler_params=_params(),
        cost_estimate=_cost(2**22, 2**21),
        name="temperature_take",
    )(x)


def _sides(x, lane):
    x0, x1 = x[:, :HALF], x[:, HALF:]
    f0, f1 = pltpu.roll(x0, 1, 1), pltpu.roll(x1, 1, 1)
    b0, b1 = pltpu.roll(x0, HALF - 1, 1), pltpu.roll(x1, HALF - 1, 1)
    at_low, at_high = lane == 0, lane == HALF - 1
    inward = jnp.concatenate([jnp.where(at_low, 0.0, f0), jnp.where(at_low, f0, f1)], axis=1)
    outward = jnp.concatenate([jnp.where(at_high, b1, b0), jnp.where(at_high, 0.0, b1)], axis=1)
    return inward, outward


def _axial(row, first, last, i, g, x, sub):
    before = pltpu.roll(row(i, g - 1), 1, 0) if g else first
    after = pltpu.roll(row(i, g + 1), G - 1, 0) if g < NG - 1 else last
    lower = jnp.where(sub == 0, before, pltpu.roll(x, 1, 0))
    return lower, jnp.where(sub == G - 1, after, pltpu.roll(x, G - 1, 0))


def _faces(t_row, h_row, i, g, beside, lane, sub):
    t, h = t_row(i, g), h_row(i, g)
    pairs = [(t_row(i - 1, g), h_row(i - 1, g)), (t_row(i + 1, g), h_row(i + 1, g))]
    pairs += list(zip(_sides(t, lane), _sides(h, lane)))
    if beside is None:
        (t_lo, h_lo), (t_hi, h_hi) = (t, -h), (t, -h)
    else:
        (t_lo, h_lo), (t_hi, h_hi) = beside
    pairs += list(zip(_axial(t_row, t_lo, t_hi, i, g, t, sub), _axial(h_row, h_lo, h_hi, i, g, h, sub)))
    flux, total = None, None
    for tn, hn in pairs:
        kf = h + hn
        term = kf * (tn - t)
        flux = term if flux is None else flux + term
        total = kf if total is None else total + kf
    return t, flux, total


def _iotas():
    lane = lax.broadcasted_iota(jnp.int32, (G, HALF), 1)
    sub = lax.broadcasted_iota(jnp.int32, (G, RAD), 0)
    return lane, sub


def _step(sample, down, mid, up, nu, oc, os, lane):
    phase = 2.0 * math.pi / PERIOD * sample
    cc, ss = math.cos(phase), math.sin(phase)
    inward, outward = _sides(mid, lane)
    source = cc * oc if sample == 0 else cc * oc + ss * os
    change = nu * ((down + up) + (inward + outward) - 4.0 * mid) + source
    return mid + change, change


def _triangle(first, rows, consts, add_square, latest, earlier, g, bufs, lane):
    nu, oc, os = consts

    def get(t, r):
        return rows(r) if t == 0 else bufs[(t - 1) % 2, r]

    latest[0, g] = rows(0)
    latest[AZ - 1, g] = rows(AZ - 1)
    earlier[1, g] = rows(1)
    earlier[AZ - 2, g] = rows(AZ - 2)
    for t in range(SPAN - 1):
        yield
        down, mid = get(t, t), get(t, t + 1)
        for r in range(t + 1, AZ - 1 - t):
            up = get(t, r + 1)
            new, change = _step(first + t, down, mid, up, nu(r), oc(r), os(r), lane)
            add_square(t, r, change * change)
            bufs[t % 2, r] = new
            if r in (t + 1, AZ - 2 - t):
                latest[r, g] = new
            elif r in (t + 2, AZ - 3 - t):
                earlier[r, g] = new
            down, mid = mid, up


def _valley(first, limit, own, halo, consts, add_square, bufs, final, lane):
    nu, oc, os = consts

    def get(t, x):
        j = x if x >= 0 else -1 - x
        if j < t:
            return bufs[(t - 1) % 2, x + DEPTH]
        latest, earlier = own if x >= 0 else halo
        if j == t or j == SPAN:
            return latest(j)
        return earlier(j)

    for t in range(SPAN):
        yield
        lo = -1 - min(t, limit - 1 - t)
        down, mid = get(t, lo - 1), get(t, lo)
        for x in range(lo, t + 1):
            up = get(t, x + 1)
            new, change = _step(first + t, down, mid, up, nu(x), oc(x), os(x), lane)
            if x >= -1:
                add_square(x, change * change)
            if t == SPAN - 1 and x >= 0:
                final(x, new)
            else:
                bufs[t % 2, x + DEPTH] = new
            down, mid = mid, up
    return bufs[SPAN % 2, DEPTH - 1]


_CONSTS = ["nu", "oc", "os"]
_STATE = ["latest", "earlier", "q"]


def _label(R, g):
    def get(r):
        if 0 <= r < AZ:
            return R["lab"][r, g]
        return R["lab_more"][r + 2 if r < 0 else r - AZ + 2, g]

    return get


def _fill(second, R, g, q_slot, final, bufs, lane):
    chains = []
    for high in (False, True):
        name = "high" if high else "low"
        consts_from = R["f_" + name]
        halo_from = R[name] if second else consts_from
        n = NLATEST if second else DEPTH

        def row(x, high=high):
            return AZ - 1 - x if high else x

        def const(name, k, row=row, consts_from=consts_from):
            return lambda x: R[name][row(x), g] if x >= 0 else consts_from[FIRST_AT[k] - 1 - x, g]

        kept = {}

        def nu(x, row=row, consts_from=consts_from, kept=kept):
            if x >= 0:
                return R["nu"][row(x), g]
            if x not in kept:
                kept[x] = _reluct(consts_from[FIRST_AT[2] - 1 - x, g])
            return kept[x]

        own = (lambda j, row=row: R["latest"][row(j), g], lambda j, row=row: R["earlier"][row(j), g])
        halo = (
            lambda j, halo_from=halo_from: halo_from[j, g],
            lambda j, halo_from=halo_from, n=n: halo_from[n + j - 1, g],
        )
        seen = set()

        def add_square(x, sq, row=row, seen=seen, high=high, halo=halo):
            r = row(x)
            if r in seen:
                before = R["q_out"][q_slot(r)]
            else:
                seen.add(r)
                before = R["q"][r + 1, g]
                if second and x < 0:
                    missed = halo[0](0) - R["gone"][int(high), g]
                    before = before + missed * missed
            R["q_out"][q_slot(r)] = before + sq

        chains.append(
            _valley(
                SPAN if second else 0,
                SPAN if second else SPAN - 1,
                own,
                halo,
                (nu, const("oc", 3), const("os", 4)),
                add_square,
                bufs.at[int(high)],
                lambda x, v, row=row: final(row(x), v),
                lane,
            )
        )
    return chains


def _middle_kernel(names, *refs):
    R = dict(zip(names, refs))
    lane, _ = _iotas()
    for g in range(NG):
        for copy in _fetch(R, g):
            copy.start()

    def sent(g):
        return [
            pltpu.make_async_copy(R[name + "_v"].at[:, g], R[name].at[:, g], R["sems"].at[k, g])
            for k, name in enumerate(("e_low", "e_high"))
        ]

    def groups(gs):
        for g in gs:
            for copy in _fetch(R, g):
                copy.wait()
        chains = []
        for k, g in enumerate(gs):

            def final(r, v, g=g):
                R["rows8"][r, g] = v

            chains += _fill(False, R, g, lambda r, g=g: (r + 1, g), final, R["ends"].at[k], lane)
        gone = _lockstep(chains)
        chains = []
        for k, g in enumerate(gs):
            at = FIRST_AT[2]
            R["lab_more"][0, g], R["lab_more"][1, g] = R["f_low"][at + 1, g], R["f_low"][at, g]
            R["lab_more"][2, g], R["lab_more"][3, g] = R["f_high"][at, g], R["f_high"][at + 1, g]
            for end, (name, row) in enumerate((("e_low", lambda j: j), ("e_high", lambda j: AZ - 1 - j))):
                R["gone"][end, g] = gone[2 * k + end]

                def rows(j, g=g, row=row):
                    return R["rows8"][row(j), g]

                def consts(j, g=g, row=row):
                    return [R[c][row(j), g] for c in ("nu", "oc", "os")]

                def store(at, x, g=g, name=name):
                    R[name + "_v"][at, g] = x

                chains.append(_corner(SPAN, NLATEST, rows, consts, store, lane))
        _lockstep(chains)
        for g in gs:
            for copy in sent(g):
                copy.start()

    _pairs(groups)
    for g in range(NG):
        for copy in sent(g):
            copy.wait()


def _triangle_kernel(names, *refs):
    R = dict(zip(names, refs))
    lane, _ = _iotas()

    def group(g, k):
        q, q_out = R["q"], R["q_out"]
        for r in (-1, 0, AZ - 1, AZ):
            q_out[r + 1, g] = q[r + 1, g]

        def add_square(t, r, sq):
            q_out[r + 1, g] = (q if t == 0 else q_out)[r + 1, g] + sq

        consts = [lambda r, name=name: R[name][r, g] for name in ("nu", "oc", "os")]
        latest, earlier = R["latest_out"], R["earlier_out"]
        start = lambda r: R["rows8"][r, g]
        return _triangle(SPAN, start, consts, add_square, latest, earlier, g, R["bufs"].at[k], lane)

    _pairs(lambda gs: _lockstep([group(g, k) for k, g in enumerate(gs)]))


def _losses(R, gs, lane, store, final):
    chains = []
    for k, g in enumerate(gs):
        chains += _fill(
            True, R, g, lambda r, k=k: (k, r + 1), lambda r, v, k=k: final(k, r, v), R["ends"].at[k], lane
        )
    _lockstep(chains)
    for k, g in enumerate(gs):
        label = _label(R, g)
        for r in range(-1, AZ + 1):
            lab = label(r)
            store(k, r, _sigma(lab) * R["q_out"][k, r + 1], lab)


_T, _H, _J, _N, _L = range(5)
_END = (5, AZ + 2, RAD)


def _last(R, gs, lane, rows, send=None):
    def final(k, r, v):
        rows[k, r] = v

    def store(k, r, d, lab):
        g = gs[k]
        t = R["base"][r + 1, g] + d * R["gain"][r + 1, g]
        R["t1_out"][r + 1, g] = t
        R["h1_out"][r + 1, g] = _half_cond(lab, t)
        if 0 <= r < AZ:
            R["loss_out"][r, g] = d
        if send is not None:
            send(k, r, d)

    _losses(R, gs, lane, store, final)


def _even():
    return lax.rem(lax.axis_index("ax"), 2) == 0


def _last_ends_kernel(names, *refs):
    R = dict(zip(names, refs))
    lane, _ = _iotas()
    outs, parts = (R["down"], R["up"]), (R["part_lo"], R["part_hi"])
    copies = [copy for g in ENDS for copy in _fetch(R, g, FIRST_AT[2])]
    for copy in copies:
        copy.start()
    for out, part in zip(outs, parts):
        out[...] = part[...]
    for copy in copies:
        copy.wait()

    def send(k, r, d):
        at, q = slice(r + 1, r + 2), (0, G - 1)[k]
        outs[k][_N, at, :] = parts[k][_N, at, :] + d[q : q + 1]

    _last(R, ENDS, lane, R["end_rows"], send)
    even = _even()
    R["swap_a"][...] = jnp.where(even, R["up"][...], R["down"][...])
    R["swap_b"][...] = jnp.where(even, R["down"][...], R["up"][...])


def _last_kernel(names, *refs):
    R = dict(zip(names, refs))
    lane, _ = _iotas()
    closing, dissipation = R["closing_v"], R["dissipation_v"]

    def copies(g):
        at = _planes(g)
        return [
            pltpu.make_async_copy(closing.at[at], R["closing"].at[at], R["sems"].at[0, g]),
            pltpu.make_async_copy(dissipation.at[at], R["dissipation"].at[at], R["sems"].at[1, g]),
        ]

    def natural(g, rows):
        closing[_planes(g)] = jnp.swapaxes(rows, 0, 1)
        dissipation[_planes(g)] = jnp.swapaxes(R["loss_out"][:, g], 0, 1)
        for copy in copies(g):
            copy.start()

    for g in range(1, NG - 1):
        for copy in _fetch(R, g, FIRST_AT[2]):
            copy.start()
    for k, g in enumerate(ENDS):
        natural(g, R["end_rows"][k])

    def groups(i):
        gs = [2 * i + 1, 2 * i + 2]
        for g in gs:
            for copy in _fetch(R, g, FIRST_AT[2]):
                copy.wait()
        _last(R, gs, lane, R["rows"])
        for k, g in enumerate(gs):
            natural(g, R["rows"][k])

    _loop(NG // 2 - 1, groups)
    for g in range(NG):
        for copy in copies(g):
            copy.wait()


def _second_kernel(names, *refs):
    R = dict(zip(names, refs))
    lane, sub = _iotas()
    ax = lax.axis_index("ax")
    exists = (ax > 0, ax < lax.axis_size("ax") - 1)
    even = _even()
    for k in range(5):
        a, b = R["got_a"][k], R["got_b"][k]
        R["t_lo"][k] = jnp.where(even, b, a)
        R["t_hi"][k] = jnp.where(even, a, b)
    for side, (own, other) in enumerate(((R["down"], R["t_lo"]), (R["up"], R["t_hi"]))):
        kf = own[_H] + other[_H]
        jump = kf * (other[_T] - own[_T])
        t = own[_T] + (own[_N] + jump) / (own[_J] + kf)
        R["own1"][side, 0] = t
        R["own1"][side, 1] = _half_cond(own[_L], t)
        t = other[_T] + (other[_N] - jump) / (other[_J] + kf)
        R["beside1"][side, 0] = jnp.where(exists[side], t, 0.0)
        R["beside1"][side, 1] = jnp.where(exists[side], _half_cond(other[_L], t), 0.0)

    def patched(name, k):
        def row(i, g):
            x = R[name][i, g]
            if g == ENDS[0]:
                x = jnp.where(sub == 0, R["own1"][0, k, pl.ds(i, 1), :], x)
            if g == ENDS[1]:
                x = jnp.where(sub == G - 1, R["own1"][1, k, pl.ds(i, 1), :], x)
            return x

        return row

    t_row, h_row = patched("t1", 0), patched("h1", 1)

    def row(r):
        at = pl.ds(r + 1, 1)
        beside = [[R["beside1"][side, k, at, :] for k in range(2)] for side in range(2)]
        for g in range(NG):
            t, flux, total = _faces(t_row, h_row, r + 1, g, beside, lane, sub)
            cap = _capacity(R["lab"][r, g])
            mismatch = cap * (t - R["prior"][r, g]) - flux - R["loss"][r, g]
            R["t2"][r, g] = t - mismatch / (cap + total)

    _loop(AZ, row)

    def turn(i):
        for g in [4 * i + k for k in range(4)]:
            nat = jnp.swapaxes(R["t2"][:, g], 0, 1).reshape(G * AZ, RAD)
            R["blocks"][:, g] = jnp.transpose(nat).reshape(SEC, RL, G * AZ)

    _loop(NG // 4, turn)


def _prior_row(R, g, r):
    if 0 <= r < AZ:
        return R["prior"][r, g]
    return R["prior_more"][r + 2 if r < 0 else r - AZ + 2, g]


def _warmth_kernel(names, *refs):
    R = dict(zip(names, refs))

    def fill(g):
        label = _label(R, g)
        for r in range(-2, AZ + 2):
            t, lab = _prior_row(R, g, r), label(r)
            R["t0"][r + 2, g] = t
            R["h0"][r + 2, g] = _half_cond(lab, t)
            R["cap"][r + 2, g] = _capacity(lab)

    _loop(NG, fill)


def _ready_kernel(names, *refs):
    R = dict(zip(names, refs))
    lane, sub = _iotas()

    def row(k):
        for g in range(NG):
            t, flux, total = _faces(
                lambda i, g: R["t0"][i, g], lambda i, g: R["h0"][i, g], k + 1, g, None, lane, sub
            )
            jac = R["cap"][k + 1, g] + total
            gain = 1.0 / jac
            R["base"][k, g] = t + flux * gain
            R["gain"][k, g] = gain
            if g in ENDS:
                end = 0 if g == ENDS[0] else 1
                R["jac"][end, k] = jac
                R["flux"][end, k] = flux

    _loop(AZ + 2, row)
    for end, (out, g, q) in enumerate(((R["part_lo"], ENDS[0], 0), (R["part_hi"], ENDS[1], G - 1))):
        label = _label(R, g)
        plane = slice(q, q + 1)
        for k in range(AZ + 2):
            at = slice(k, k + 1)
            out[_T, at, :] = R["t0"][k + 1, g, plane, :]
            out[_H, at, :] = R["h0"][k + 1, g, plane, :]
            out[_J, at, :] = R["jac"][end, k, plane, :]
            out[_N, at, :] = R["flux"][end, k, plane, :]
            out[_L, at, :] = label(k - 1)[plane]


def _fetch(R, g, skip=0):
    copies = []
    for k, name in enumerate(sorted(key for key in R if "apart " + key in R)):
        lo = skip if name.startswith("f_") else 0
        at = pl.ds(lo, R[name].shape[0] - lo)
        copies.append(pltpu.make_async_copy(R["apart " + name].at[at, g], R[name].at[at, g], R["in_sems"].at[k, g]))
    return copies


def _call(kernel, name, given, names, outs, scratch, alias=(), apart=(), fetch=()):
    given = {**given, **{"apart " + key: given[key] for key in fetch}}
    names = names + ["apart " + key for key in fetch]
    shapes = {key: pltpu.VMEM(shape, F32) for key, shape in scratch.items()}
    shapes.update({key: pltpu.VMEM(given[key].shape, F32) for key in fetch})
    if fetch:
        shapes["in_sems"] = pltpu.SemaphoreType.DMA((len(fetch), NG))
    if apart:
        shapes["sems"] = pltpu.SemaphoreType.DMA((len(apart), NG))
    space = {True: pl.ANY, False: pltpu.VMEM}
    results = pl.pallas_call(
        functools.partial(kernel, names + list(outs) + list(shapes)),
        out_shape=[_sds(*shape) for shape in outs.values()],
        in_specs=[pl.BlockSpec(memory_space=space[key.startswith("apart ")]) for key in names],
        out_specs=[pl.BlockSpec(memory_space=space[key in apart]) for key in outs],
        scratch_shapes=list(shapes.values()),
        input_output_aliases={names.index(key): list(outs).index(key + "_out") for key in alias},
        compiler_params=_params(),
        cost_estimate=_cost(2**24, 2**25),
        name=name,
    )(*[given[key] for key in names])
    return dict(zip(outs, results))


_OWN = (AZ, NG, G, RAD)
_MORE = (AZ + 2, NG, G, RAD)
_ENDS = (2, 2, 2, SPAN + DEPTH, G, RAD)
_LAST = _CONSTS + _STATE + ["lab", "lab_more", "gone", "base", "gain"]
_FETCH = ["f_low", "f_high", "low", "high"]
_PRIOR = ["lab", "lab_more", "prior", "prior_more"]


def _ring(axis, x, step, closed):
    count = lax.axis_size(axis)
    pairs = [(i, (i + 1) % count) for i in range(count if closed else count - 1)]
    return lax.ppermute(x, axis, pairs if step > 0 else [(b, a) for a, b in pairs])


def _swap(axis, x, start):
    pairs = [(i, i + 1) for i in range(start, lax.axis_size(axis) - 1, 2)]
    return lax.ppermute(x, axis, pairs + [(b, a) for a, b in pairs])


def _around(low_edge, high_edge):
    return _ring("sec", high_edge, 1, True), _ring("sec", low_edge, -1, True)


def shards(labels, exc, a0, prior):
    V = {}
    V["f_low"], V["f_high"] = _around(*_edges(labels, exc, a0))
    got = lax.all_to_all(_prior_send(prior), "sec", 0, 0)
    V.update(zip(_STATE + ["lab"] + _CONSTS, _prepare(labels, exc, a0)))
    edge = (NLATEST + DEPTH, NG, G, RAD)
    outs = {"rows8": _OWN, "q_out": _MORE, "gone": (2, NG, G, RAD), "lab_more": (4, NG, G, RAD)}
    outs.update(e_low=edge, e_high=edge)
    scratch = {"ends": _ENDS, "e_low_v": edge, "e_high_v": edge}
    out = _call(_middle_kernel, "field_middle", V, _CONSTS + _STATE, outs, scratch, (), ["e_low", "e_high"], ["f_low", "f_high"])
    V["low"], V["high"] = _around(out["e_low"], out["e_high"])
    V.update(rows8=out["rows8"], q=out["q_out"], gone=out["gone"], lab_more=out["lab_more"])
    outs = {"latest_out": _OWN, "earlier_out": _OWN, "q_out": _MORE}
    names = ["rows8", "q", "nu", "oc", "os"]
    out = _call(_triangle_kernel, "field_triangle", V, names, outs, {"bufs": (2, 2, AZ, G, RAD)})
    for name in _STATE:
        V[name] = out[name + "_out"]
    got, V["latest"] = lax.optimization_barrier((got, V["latest"]))
    V["prior"], V["prior_more"] = _prior_take(got)
    warmth = {name: (AZ + 4, NG, G, RAD) for name in ("t0", "h0", "cap")}
    V.update(_call(_warmth_kernel, "prior_warmth", V, _PRIOR, warmth, {}))
    scratch = {"jac": (2, AZ + 2, G, RAD), "flux": (2, AZ + 2, G, RAD)}
    outs = {"base": _MORE, "gain": _MORE, "part_lo": _END, "part_hi": _END}
    V.update(_call(_ready_kernel, "first_ready", V, ["lab", "lab_more", *warmth], outs, scratch))
    scratch = {"q_out": (2, AZ + 2, G, RAD), "ends": _ENDS}
    state = {"t1_out": _MORE, "h1_out": _MORE, "loss_out": _OWN}
    names = _LAST + ["part_lo", "part_hi"]
    outs = {**state, "down": _END, "up": _END, "swap_a": _END, "swap_b": _END, "end_rows": (2, AZ, G, RAD)}
    V.update(_call(_last_ends_kernel, "last_ends", V, names, outs, scratch, fetch=_FETCH))
    V["got_a"], V["got_b"] = _swap("ax", V["swap_a"], 0), _swap("ax", V["swap_b"], 1)
    V.update(t1=V["t1_out"], h1=V["h1_out"], loss=V["loss_out"])
    results = {"closing": (AX, AZ, RAD), "dissipation": (AX, AZ, RAD)}
    scratch.update(rows=(2, AZ, G, RAD), closing_v=(AX, AZ, RAD), dissipation_v=(AX, AZ, RAD))
    names = _LAST + ["end_rows", "t1", "h1", "loss"]
    outs = {**results, **state}
    V.update(
        _call(_last_kernel, "field_last", V, names, outs, scratch, ["t1", "h1", "loss"], list(results), _FETCH)
    )
    V.update(t1=V["t1_out"], h1=V["h1_out"], loss=V["loss_out"])
    names = ["t1", "h1", "down", "up", "got_a", "got_b", "lab", "prior", "loss"]
    shape = (2, 2, AZ + 2, RAD)
    scratch = {"t2": _OWN, "own1": shape, "beside1": shape, "t_lo": _END, "t_hi": _END}
    out = _call(_second_kernel, "second_sweep", V, names, {"blocks": (SEC, NG, RL, G * AZ)}, scratch)
    temperature = _temperature_take(lax.all_to_all(out["blocks"], "sec", 0, 0))
    return V["closing"], V["dissipation"], temperature


def solution(mesh):
    spec = P("ax", "sec", None)
    return jax.shard_map(
        shards,
        mesh=mesh,
        in_specs=(spec, P(None, "ax", "sec", None), spec, spec),
        out_specs=(spec, spec, spec),
        check_vma=False,
    )
```

```python
import functools
import math

import jax
import jax.numpy as jnp
from jax import lax
from jax.experimental import pallas as pl
from jax.experimental.pallas import tpu as pltpu
from jax.sharding import PartitionSpec as P

SAMPLES = 16
PERIOD = 32
SPAN = 8
DEPTH = SPAN // 2
FIRST_AT = (0, DEPTH, 2 * DEPTH, 3 * DEPTH, 4 * DEPTH)
NSEND = 5 * DEPTH
NLATEST = DEPTH + 1

F32 = jnp.float32
AX, AZ, RAD, ANG = 64, 16, 256, 512
SEC = 32
RL = RAD // SEC
G = 8
NG = AX // G
ENDS = (0, NG - 1)
HALF = RAD // 2


def _params(mib=16):
    return pltpu.CompilerParams(vmem_limit_bytes=mib * 2**20)


def _sds(*shape):
    return jax.ShapeDtypeStruct(shape, F32)


def _cost(flops, nbytes):
    return pl.CostEstimate(flops=flops, bytes_accessed=nbytes, transcendentals=0)


def _loop(n, body):
    def step(i, _):
        body(i)
        return 0

    lax.fori_loop(0, n, step, 0)


def _lockstep(chains):
    results = [None] * len(chains)
    going = dict(enumerate(chains))
    while going:
        for k in list(going):
            try:
                next(going[k])
            except StopIteration as end:
                results[k] = end.value
                del going[k]
    return results


def _pairs(body, count=2):
    _loop(NG // count, lambda i: body([count * i + k for k in range(count)]))


def _planes(g):
    return pl.ds(pl.multiple_of(g * G, G), G)


def _reluct(lab):
    return jnp.where(lab == 0, 0.05, jnp.where(lab == 3, 0.2, 0.24)).astype(F32)


def _sigma(lab):
    return jnp.where(lab == 0, 0.3, jnp.where(lab == 1, 1.0, jnp.where(lab == 2, 0.0, 0.6))).astype(F32)


def _driven(lab, x):
    return jnp.where((lab == 1) | (lab == 3), x, 0.0)


def _half_cond(lab, temp):
    half_k0 = jnp.where(lab == 0, 0.5, jnp.where(lab == 1, 0.75, jnp.where(lab == 2, 0.05, 0.2)))
    return half_k0 * (1.0 + 0.5 * jnp.tanh(temp))


def _capacity(lab):
    return jnp.where(lab == 1, 3.5, jnp.where(lab == 2, 0.5, 3.0)).astype(F32)


def _corner(first, latest_count, rows, consts, store, lane):
    top = 2 * DEPTH - 1 + latest_count - DEPTH
    level = {j: rows(j) for j in range(top + 1)}
    for t in range(latest_count):
        yield
        store(t, level[t])
        if t < DEPTH:
            store(latest_count + t, level[t + 1])
        level = {
            j: _step(first + t, level[j - 1], level[j], level[j + 1], *consts(j), lane)[0]
            for j in range(t + 1, top - t)
        }


def _edges_kernel(lab_hbm, exc_hbm, a_hbm, low_out, high_out, lab_v, exc_v, a_v, low_ref, high_ref, sems, out_sems):
    copies = []
    for g in range(NG):
        at = pl.ds(g * G, G)
        copies.append(
            [
                pltpu.make_async_copy(lab_hbm.at[at], lab_v.at[at], sems.at[g, 0]),
                pltpu.make_async_copy(exc_hbm.at[0, at], exc_v.at[0, at], sems.at[g, 1]),
                pltpu.make_async_copy(exc_hbm.at[1, at], exc_v.at[1, at], sems.at[g, 2]),
                pltpu.make_async_copy(a_hbm.at[at], a_v.at[at], sems.at[g, 3]),
            ]
        )
        for copy in copies[-1]:
            copy.start()

    lane, _ = _iotas()

    def sent(g):
        return [
            pltpu.make_async_copy(low_ref.at[:, g], low_out.at[:, g], out_sems.at[0, g]),
            pltpu.make_async_copy(high_ref.at[:, g], high_out.at[:, g], out_sems.at[1, g]),
        ]

    def corner(g, out, row, a, c, s, lab):
        kept = {}
        for j in range(2 * DEPTH - 1):
            r = row(j)
            kept[j] = _reluct(lab[r]), _driven(lab[r], c[r]), _driven(lab[r], s[r])
            if j < DEPTH:
                out[FIRST_AT[2] + j, g] = lab[r].astype(F32)
                out[FIRST_AT[3] + j, g] = kept[j][1]
                out[FIRST_AT[4] + j, g] = kept[j][2]

        def store(k, x):
            out[k, g] = x

        return _corner(0, DEPTH, lambda j: a[row(j)], lambda j: kept[j], store, lane)

    for pair in range(NG // 2):
        chains = []
        for g in (2 * pair, 2 * pair + 1):
            for copy in copies[g]:
                copy.wait()
            at = pl.ds(g * G, G)
            given = [jnp.swapaxes(x, 0, 1) for x in (a_v[at], exc_v[0, at], exc_v[1, at], lab_v[at])]
            chains.append(corner(g, low_ref, lambda j: j, *given))
            chains.append(corner(g, high_ref, lambda j: AZ - 1 - j, *given))
        _lockstep(chains)
        for g in (2 * pair, 2 * pair + 1):
            for copy in sent(g):
                copy.start()
    for g in range(NG):
        for copy in sent(g):
            copy.wait()


def _edges(labels, exc, a):
    return pl.pallas_call(
        _edges_kernel,
        in_specs=[pl.BlockSpec(memory_space=pl.ANY)] * 3,
        out_specs=[pl.BlockSpec(memory_space=pl.ANY)] * 2,
        out_shape=[_sds(NSEND, NG, G, RAD)] * 2,
        scratch_shapes=[
            pltpu.VMEM((AX, AZ, RAD), jnp.int32),
            pltpu.VMEM((2, AX, AZ, RAD), F32),
            pltpu.VMEM((AX, AZ, RAD), F32),
            pltpu.VMEM((NSEND, NG, G, RAD), F32),
            pltpu.VMEM((NSEND, NG, G, RAD), F32),
            pltpu.SemaphoreType.DMA((NG, 4)),
            pltpu.SemaphoreType.DMA((2, NG)),
        ],
        compiler_params=_params(56),
        cost_estimate=_cost(2**20, 6 * 2**20),
        name="edge_layers",
    )(labels, exc, a)


def _prepare_kernel(lab_ref, exc_ref, a_ref, latest, earlier, q, lab_out, nu_out, oc_out, os_out, bufs, a_v):
    lane, _ = _iotas()

    def group(g, k):
        at = _planes(g)
        lab = jnp.swapaxes(lab_ref[at], 0, 1)
        lab_out[:, g] = lab.astype(F32)
        nu_out[:, g] = _reluct(lab)
        oc_out[:, g] = _driven(lab, jnp.swapaxes(exc_ref[0, at], 0, 1))
        os_out[:, g] = _driven(lab, jnp.swapaxes(exc_ref[1, at], 0, 1))
        a_v[k] = jnp.swapaxes(a_ref[at], 0, 1)
        zero = jnp.zeros((G, RAD), F32)
        for r in (-1, 0, AZ - 1, AZ):
            q[r + 1, g] = zero

        def add_square(t, r, sq):
            q[r + 1, g] = sq if t == 0 else q[r + 1, g] + sq

        consts = [lambda r, ref=ref: ref[r, g] for ref in (nu_out, oc_out, os_out)]
        return _triangle(0, lambda r: a_v[k, r], consts, add_square, latest, earlier, g, bufs.at[k], lane)

    _pairs(lambda gs: _lockstep([group(g, k) for k, g in enumerate(gs)]))


def _prepare(labels, exc, a):
    return pl.pallas_call(
        _prepare_kernel,
        out_shape=[_sds(AZ, NG, G, RAD)] * 2 + [_sds(AZ + 2, NG, G, RAD)] + [_sds(AZ, NG, G, RAD)] * 4,
        scratch_shapes=[pltpu.VMEM((2, 2, AZ, G, RAD), F32), pltpu.VMEM((2, AZ, G, RAD), F32)],
        compiler_params=_params(),
        cost_estimate=_cost(2**22, 8 * 2**20),
        name="prepare",
    )(labels, exc, a)


PG = 16
NP = AX // PG


def _prior_send_kernel(prior_ref, out):
    for p in range(NP):
        x = prior_ref[p * PG : p * PG + PG]
        x = jnp.transpose(x.reshape(PG * RL, ANG)).reshape(SEC, AZ, PG * RL)
        out[:, p] = x
        for e, r in enumerate((AZ - 2, AZ - 1, 0, 1)):
            line = x[:, r : r + 1, :]
            at = slice(p * 4 + e, p * 4 + e + 1)
            if e < 2:
                out[1:, NP, at, :] = line[:-1]
                out[0:1, NP, at, :] = line[-1:]
            else:
                out[:-1, NP, at, :] = line[1:]
                out[SEC - 1 :, NP, at, :] = line[:1]


def _prior_send(prior):
    return pl.pallas_call(
        _prior_send_kernel,
        out_shape=_sds(SEC, NP + 1, AZ, PG * RL),
        compiler_params=_params(),
        cost_estimate=_cost(2**20, 3 * 2**20),
        name="prior_send",
    )(prior)


def _swap_blocks(x, lanes):
    count = 128 // lanes
    blk = lax.broadcasted_iota(jnp.int32, (8, 128), 1) // lanes
    x = list(x)
    b = count // 2
    while b:
        keep = (blk & b) == 0
        for j in range(count):
            if j & b == 0:
                p, q = x[j], x[j + b]
                x[j] = jnp.where(keep, p, pltpu.roll(q, b * lanes, 1))
                x[j + b] = jnp.where(keep, pltpu.roll(p, 128 - b * lanes, 1), q)
        b //= 2
    return x


def _prior_take_kernel(x_hbm, out, more, x_ref, nat, sems):
    copies = [pltpu.make_async_copy(x_hbm.at[:, p], x_ref.at[:, p], sems.at[p]) for p in range(NP + 1)]
    for copy in copies:
        copy.start()

    def fill(p):
        for tile in range(AZ // 8):
            rows = slice(tile * 8, tile * 8 + 8)
            for half in range(2):
                got = _swap_blocks([x_ref[half * PG + j, p, rows] for j in range(PG)], RL)
                for k in range(PG):
                    nat[k, rows, half * 128 : half * 128 + 128] = got[k]

    def block(p):
        pltpu.make_async_copy(x_hbm.at[:, p], x_ref.at[:, p], sems.at[p]).wait()
        fill(p)
        for k in range(PG // G):
            out[:, p * (PG // G) + k] = jnp.swapaxes(nat[k * G : k * G + G], 0, 1)

    _loop(NP, block)
    copies[NP].wait()
    fill(NP)
    for k in range(PG // G):
        x = jnp.swapaxes(nat[k * G : k * G + G], 0, 1)
        for p in range(NP):
            more[:, p * (PG // G) + k] = x[p * 4 : p * 4 + 4]


def _prior_take(x):
    return pl.pallas_call(
        _prior_take_kernel,
        in_specs=[pl.BlockSpec(memory_space=pl.ANY)],
        out_shape=[_sds(AZ, NG, G, RAD), _sds(4, NG, G, RAD)],
        scratch_shapes=[
            pltpu.VMEM((SEC, NP + 1, AZ, PG * RL), F32),
            pltpu.VMEM((PG, AZ, RAD), F32),
            pltpu.SemaphoreType.DMA((NP + 1,)),
        ],
        compiler_params=_params(),
        cost_estimate=_cost(2**24, 2**25),
        name="prior_take",
    )(x)


def _temperature_take_kernel(x_ref, out, planes, sems):
    def copy(g):
        at = _planes(g)
        return pltpu.make_async_copy(planes.at[at], out.at[at], sems.at[g])

    def groups(gs):
        for g in gs:
            for s in range(SEC // 8):
                got = _swap_blocks([x_ref[s * 8 + j, g] for j in range(8)], AZ)
                for q in range(G):
                    planes[g * G + q, :, s * 128 : s * 128 + 128] = got[q]
        for g in gs:
            copy(g).start()

    _pairs(groups)
    for g in range(NG):
        copy(g).wait()


def _temperature_take(x):
    return pl.pallas_call(
        _temperature_take_kernel,
        out_shape=_sds(AX, RL, ANG),
        out_specs=pl.BlockSpec(memory_space=pl.ANY),
        scratch_shapes=[pltpu.VMEM((AX, RL, ANG), F32), pltpu.SemaphoreType.DMA((NG,))],
        compiler_params=_params(),
        cost_estimate=_cost(2**22, 2**21),
        name="temperature_take",
    )(x)


def _sides(x, lane):
    x0, x1 = x[:, :HALF], x[:, HALF:]
    f0, f1 = pltpu.roll(x0, 1, 1), pltpu.roll(x1, 1, 1)
    b0, b1 = pltpu.roll(x0, HALF - 1, 1), pltpu.roll(x1, HALF - 1, 1)
    at_low, at_high = lane == 0, lane == HALF - 1
    inward = jnp.concatenate([jnp.where(at_low, 0.0, f0), jnp.where(at_low, f0, f1)], axis=1)
    outward = jnp.concatenate([jnp.where(at_high, b1, b0), jnp.where(at_high, 0.0, b1)], axis=1)
    return inward, outward


def _axial(row, first, last, i, g, x, sub):
    before = pltpu.roll(row(i, g - 1), 1, 0) if g else first
    after = pltpu.roll(row(i, g + 1), G - 1, 0) if g < NG - 1 else last
    lower = jnp.where(sub == 0, before, pltpu.roll(x, 1, 0))
    return lower, jnp.where(sub == G - 1, after, pltpu.roll(x, G - 1, 0))


def _faces(t_row, h_row, i, g, beside, lane, sub):
    t, h = t_row(i, g), h_row(i, g)
    pairs = [(t_row(i - 1, g), h_row(i - 1, g)), (t_row(i + 1, g), h_row(i + 1, g))]
    pairs += list(zip(_sides(t, lane), _sides(h, lane)))
    if beside is None:
        (t_lo, h_lo), (t_hi, h_hi) = (t, -h), (t, -h)
    else:
        (t_lo, h_lo), (t_hi, h_hi) = beside
    pairs += list(zip(_axial(t_row, t_lo, t_hi, i, g, t, sub), _axial(h_row, h_lo, h_hi, i, g, h, sub)))
    flux, total = None, None
    for tn, hn in pairs:
        kf = h + hn
        term = kf * (tn - t)
        flux = term if flux is None else flux + term
        total = kf if total is None else total + kf
    return t, flux, total


def _iotas():
    lane = lax.broadcasted_iota(jnp.int32, (G, HALF), 1)
    sub = lax.broadcasted_iota(jnp.int32, (G, RAD), 0)
    return lane, sub


def _step(sample, down, mid, up, nu, oc, os, lane):
    phase = 2.0 * math.pi / PERIOD * sample
    cc, ss = math.cos(phase), math.sin(phase)
    inward, outward = _sides(mid, lane)
    source = cc * oc if sample == 0 else cc * oc + ss * os
    change = nu * ((down + up) + (inward + outward) - 4.0 * mid) + source
    return mid + change, change


def _triangle(first, rows, consts, add_square, latest, earlier, g, bufs, lane):
    nu, oc, os = consts

    def get(t, r):
        return rows(r) if t == 0 else bufs[(t - 1) % 2, r]

    latest[0, g] = rows(0)
    latest[AZ - 1, g] = rows(AZ - 1)
    earlier[1, g] = rows(1)
    earlier[AZ - 2, g] = rows(AZ - 2)
    for t in range(SPAN - 1):
        yield
        down, mid = get(t, t), get(t, t + 1)
        for r in range(t + 1, AZ - 1 - t):
            up = get(t, r + 1)
            new, change = _step(first + t, down, mid, up, nu(r), oc(r), os(r), lane)
            add_square(t, r, change * change)
            bufs[t % 2, r] = new
            if r in (t + 1, AZ - 2 - t):
                latest[r, g] = new
            elif r in (t + 2, AZ - 3 - t):
                earlier[r, g] = new
            down, mid = mid, up


def _valley(first, limit, own, halo, consts, add_square, bufs, final, lane):
    nu, oc, os = consts

    def get(t, x):
        j = x if x >= 0 else -1 - x
        if j < t:
            return bufs[(t - 1) % 2, x + DEPTH]
        latest, earlier = own if x >= 0 else halo
        if j == t or j == SPAN:
            return latest(j)
        return earlier(j)

    for t in range(SPAN):
        yield
        lo = -1 - min(t, limit - 1 - t)
        down, mid = get(t, lo - 1), get(t, lo)
        for x in range(lo, t + 1):
            up = get(t, x + 1)
            new, change = _step(first + t, down, mid, up, nu(x), oc(x), os(x), lane)
            if x >= -1:
                add_square(x, change * change)
            if t == SPAN - 1 and x >= 0:
                final(x, new)
            else:
                bufs[t % 2, x + DEPTH] = new
            down, mid = mid, up
    return bufs[SPAN % 2, DEPTH - 1]


_CONSTS = ["nu", "oc", "os"]
_STATE = ["latest", "earlier", "q"]


def _label(R, g):
    def get(r):
        if 0 <= r < AZ:
            return R["lab"][r, g]
        return R["lab_more"][r + 2 if r < 0 else r - AZ + 2, g]

    return get


def _fill(second, R, g, q_slot, final, bufs, lane):
    chains = []
    for high in (False, True):
        name = "high" if high else "low"
        consts_from = R["f_" + name]
        halo_from = R[name] if second else consts_from
        n = NLATEST if second else DEPTH

        def row(x, high=high):
            return AZ - 1 - x if high else x

        def const(name, k, row=row, consts_from=consts_from):
            return lambda x: R[name][row(x), g] if x >= 0 else consts_from[FIRST_AT[k] - 1 - x, g]

        kept = {}

        def nu(x, row=row, consts_from=consts_from, kept=kept):
            if x >= 0:
                return R["nu"][row(x), g]
            if x not in kept:
                kept[x] = _reluct(consts_from[FIRST_AT[2] - 1 - x, g])
            return kept[x]

        own = (lambda j, row=row: R["latest"][row(j), g], lambda j, row=row: R["earlier"][row(j), g])
        halo = (
            lambda j, halo_from=halo_from: halo_from[j, g],
            lambda j, halo_from=halo_from, n=n: halo_from[n + j - 1, g],
        )
        seen = set()

        def add_square(x, sq, row=row, seen=seen, high=high, halo=halo):
            r = row(x)
            if r in seen:
                before = R["q_out"][q_slot(r)]
            else:
                seen.add(r)
                before = R["q"][r + 1, g]
                if second and x < 0:
                    missed = halo[0](0) - R["gone"][int(high), g]
                    before = before + missed * missed
            R["q_out"][q_slot(r)] = before + sq

        chains.append(
            _valley(
                SPAN if second else 0,
                SPAN if second else SPAN - 1,
                own,
                halo,
                (nu, const("oc", 3), const("os", 4)),
                add_square,
                bufs.at[int(high)],
                lambda x, v, row=row: final(row(x), v),
                lane,
            )
        )
    return chains


def _middle_kernel(names, *refs):
    R = dict(zip(names, refs))
    lane, _ = _iotas()
    for g in range(NG):
        for copy in _fetch(R, g):
            copy.start()

    def sent(g):
        return [
            pltpu.make_async_copy(R[name + "_v"].at[:, g], R[name].at[:, g], R["sems"].at[k, g])
            for k, name in enumerate(("e_low", "e_high"))
        ]

    def groups(gs):
        for g in gs:
            for copy in _fetch(R, g):
                copy.wait()
        chains = []
        for k, g in enumerate(gs):

            def final(r, v, g=g):
                R["rows8"][r, g] = v

            chains += _fill(False, R, g, lambda r, g=g: (r + 1, g), final, R["ends"].at[k], lane)
        gone = _lockstep(chains)
        chains = []
        for k, g in enumerate(gs):
            at = FIRST_AT[2]
            R["lab_more"][0, g], R["lab_more"][1, g] = R["f_low"][at + 1, g], R["f_low"][at, g]
            R["lab_more"][2, g], R["lab_more"][3, g] = R["f_high"][at, g], R["f_high"][at + 1, g]
            for end, (name, row) in enumerate((("e_low", lambda j: j), ("e_high", lambda j: AZ - 1 - j))):
                R["gone"][end, g] = gone[2 * k + end]

                def rows(j, g=g, row=row):
                    return R["rows8"][row(j), g]

                def consts(j, g=g, row=row):
                    return [R[c][row(j), g] for c in ("nu", "oc", "os")]

                def store(at, x, g=g, name=name):
                    R[name + "_v"][at, g] = x

                chains.append(_corner(SPAN, NLATEST, rows, consts, store, lane))
        _lockstep(chains)
        for g in gs:
            for copy in sent(g):
                copy.start()

    _pairs(groups, 4)
    for g in range(NG):
        for copy in sent(g):
            copy.wait()


def _triangle_kernel(names, *refs):
    R = dict(zip(names, refs))
    lane, _ = _iotas()

    def group(g, k):
        q, q_out = R["q"], R["q_out"]
        for r in (-1, 0, AZ - 1, AZ):
            q_out[r + 1, g] = q[r + 1, g]

        def add_square(t, r, sq):
            q_out[r + 1, g] = (q if t == 0 else q_out)[r + 1, g] + sq

        consts = [lambda r, name=name: R[name][r, g] for name in ("nu", "oc", "os")]
        latest, earlier = R["latest_out"], R["earlier_out"]
        start = lambda r: R["rows8"][r, g]
        return _triangle(SPAN, start, consts, add_square, latest, earlier, g, R["bufs"].at[k], lane)

    _pairs(lambda gs: _lockstep([group(g, k) for k, g in enumerate(gs)]))


def _losses(R, gs, lane, store, final):
    chains = []
    for k, g in enumerate(gs):
        chains += _fill(
            True, R, g, lambda r, k=k: (k, r + 1), lambda r, v, k=k: final(k, r, v), R["ends"].at[k], lane
        )
    _lockstep(chains)
    for k, g in enumerate(gs):
        label = _label(R, g)
        for r in range(-1, AZ + 1):
            lab = label(r)
            store(k, r, _sigma(lab) * R["q_out"][k, r + 1], lab)


_T, _H, _J, _N, _L = range(5)
_END = (5, AZ + 2, RAD)


def _last(R, gs, lane, rows, send=None):
    def final(k, r, v):
        rows[k, r] = v

    def store(k, r, d, lab):
        g = gs[k]
        t = R["base"][r + 1, g] + d * R["gain"][r + 1, g]
        R["t1_out"][r + 1, g] = t
        R["h1_out"][r + 1, g] = _half_cond(lab, t)
        if 0 <= r < AZ:
            R["loss_out"][r, g] = d
        if send is not None:
            send(k, r, d)

    _losses(R, gs, lane, store, final)


def _even():
    return lax.rem(lax.axis_index("ax"), 2) == 0


def _last_ends_kernel(names, *refs):
    R = dict(zip(names, refs))
    lane, _ = _iotas()
    outs, parts = (R["down"], R["up"]), (R["part_lo"], R["part_hi"])
    copies = [copy for g in ENDS for copy in _fetch(R, g, FIRST_AT[2])]
    for copy in copies:
        copy.start()
    for out, part in zip(outs, parts):
        out[...] = part[...]
    for copy in copies:
        copy.wait()

    def send(k, r, d):
        at, q = slice(r + 1, r + 2), (0, G - 1)[k]
        outs[k][_N, at, :] = parts[k][_N, at, :] + d[q : q + 1]

    _last(R, ENDS, lane, R["end_rows"], send)
    even = _even()
    R["swap_a"][...] = jnp.where(even, R["up"][...], R["down"][...])
    R["swap_b"][...] = jnp.where(even, R["down"][...], R["up"][...])


def _last_kernel(names, *refs):
    R = dict(zip(names, refs))
    lane, _ = _iotas()
    closing, dissipation = R["closing_v"], R["dissipation_v"]

    def copies(g):
        at = _planes(g)
        return [
            pltpu.make_async_copy(closing.at[at], R["closing"].at[at], R["sems"].at[0, g]),
            pltpu.make_async_copy(dissipation.at[at], R["dissipation"].at[at], R["sems"].at[1, g]),
        ]

    def natural(g, rows):
        closing[_planes(g)] = jnp.swapaxes(rows, 0, 1)
        dissipation[_planes(g)] = jnp.swapaxes(R["loss_out"][:, g], 0, 1)
        for copy in copies(g):
            copy.start()

    for g in range(1, NG - 1):
        for copy in _fetch(R, g, FIRST_AT[2]):
            copy.start()
    for k, g in enumerate(ENDS):
        natural(g, R["end_rows"][k])

    def groups(i):
        gs = [3 * i + k for k in (1, 2, 3)]
        for g in gs:
            for copy in _fetch(R, g, FIRST_AT[2]):
                copy.wait()
        _last(R, gs, lane, R["rows"])
        for k, g in enumerate(gs):
            natural(g, R["rows"][k])

    _loop((NG - 2) // 3, groups)
    for g in range(NG):
        for copy in copies(g):
            copy.wait()


def _second_kernel(names, *refs):
    R = dict(zip(names, refs))
    lane, sub = _iotas()
    ax = lax.axis_index("ax")
    exists = (ax > 0, ax < lax.axis_size("ax") - 1)
    even = _even()
    for k in range(5):
        a, b = R["got_a"][k], R["got_b"][k]
        R["t_lo"][k] = jnp.where(even, b, a)
        R["t_hi"][k] = jnp.where(even, a, b)
    for side, (own, other) in enumerate(((R["down"], R["t_lo"]), (R["up"], R["t_hi"]))):
        kf = own[_H] + other[_H]
        jump = kf * (other[_T] - own[_T])
        t = own[_T] + (own[_N] + jump) / (own[_J] + kf)
        R["own1"][side, 0] = t
        R["own1"][side, 1] = _half_cond(own[_L], t)
        t = other[_T] + (other[_N] - jump) / (other[_J] + kf)
        R["beside1"][side, 0] = jnp.where(exists[side], t, 0.0)
        R["beside1"][side, 1] = jnp.where(exists[side], _half_cond(other[_L], t), 0.0)

    def patched(name, k):
        def row(i, g):
            x = R[name][i, g]
            if g == ENDS[0]:
                x = jnp.where(sub == 0, R["own1"][0, k, pl.ds(i, 1), :], x)
            if g == ENDS[1]:
                x = jnp.where(sub == G - 1, R["own1"][1, k, pl.ds(i, 1), :], x)
            return x

        return row

    t_row, h_row = patched("t1", 0), patched("h1", 1)

    def row(r):
        at = pl.ds(r + 1, 1)
        beside = [[R["beside1"][side, k, at, :] for k in range(2)] for side in range(2)]
        for g in range(NG):
            t, flux, total = _faces(t_row, h_row, r + 1, g, beside, lane, sub)
            cap = _capacity(R["lab"][r, g])
            mismatch = cap * (t - R["prior"][r, g]) - flux - R["loss"][r, g]
            R["t2"][r, g] = t - mismatch / (cap + total)

    _loop(AZ, row)

    def turn(i):
        for g in [4 * i + k for k in range(4)]:
            nat = jnp.swapaxes(R["t2"][:, g], 0, 1).reshape(G * AZ, RAD)
            R["blocks"][:, g] = jnp.transpose(nat).reshape(SEC, RL, G * AZ)

    _loop(NG // 4, turn)


def _prior_row(R, g, r):
    if 0 <= r < AZ:
        return R["prior"][r, g]
    return R["prior_more"][r + 2 if r < 0 else r - AZ + 2, g]


def _warmth_kernel(names, *refs):
    R = dict(zip(names, refs))

    def fill(g):
        label = _label(R, g)
        for r in range(-2, AZ + 2):
            t, lab = _prior_row(R, g, r), label(r)
            R["t0"][r + 2, g] = t
            R["h0"][r + 2, g] = _half_cond(lab, t)
            R["cap"][r + 2, g] = _capacity(lab)

    _loop(NG, fill)


def _ready_kernel(names, *refs):
    R = dict(zip(names, refs))
    lane, sub = _iotas()

    def row(k):
        for g in range(NG):
            t, flux, total = _faces(
                lambda i, g: R["t0"][i, g], lambda i, g: R["h0"][i, g], k + 1, g, None, lane, sub
            )
            jac = R["cap"][k + 1, g] + total
            gain = 1.0 / jac
            R["base"][k, g] = t + flux * gain
            R["gain"][k, g] = gain
            if g in ENDS:
                end = 0 if g == ENDS[0] else 1
                R["jac"][end, k] = jac
                R["flux"][end, k] = flux

    _loop(AZ + 2, row)
    for end, (out, g, q) in enumerate(((R["part_lo"], ENDS[0], 0), (R["part_hi"], ENDS[1], G - 1))):
        label = _label(R, g)
        plane = slice(q, q + 1)
        for k in range(AZ + 2):
            at = slice(k, k + 1)
            out[_T, at, :] = R["t0"][k + 1, g, plane, :]
            out[_H, at, :] = R["h0"][k + 1, g, plane, :]
            out[_J, at, :] = R["jac"][end, k, plane, :]
            out[_N, at, :] = R["flux"][end, k, plane, :]
            out[_L, at, :] = label(k - 1)[plane]


def _fetch(R, g, skip=0):
    copies = []
    for k, name in enumerate(sorted(key for key in R if "apart " + key in R)):
        lo = skip if name.startswith("f_") else 0
        at = pl.ds(lo, R[name].shape[0] - lo)
        copies.append(pltpu.make_async_copy(R["apart " + name].at[at, g], R[name].at[at, g], R["in_sems"].at[k, g]))
    return copies


def _call(kernel, name, given, names, outs, scratch, alias=(), apart=(), fetch=()):
    given = {**given, **{"apart " + key: given[key] for key in fetch}}
    names = names + ["apart " + key for key in fetch]
    shapes = {key: pltpu.VMEM(shape, F32) for key, shape in scratch.items()}
    shapes.update({key: pltpu.VMEM(given[key].shape, F32) for key in fetch})
    if fetch:
        shapes["in_sems"] = pltpu.SemaphoreType.DMA((len(fetch), NG))
    if apart:
        shapes["sems"] = pltpu.SemaphoreType.DMA((len(apart), NG))
    space = {True: pl.ANY, False: pltpu.VMEM}
    results = pl.pallas_call(
        functools.partial(kernel, names + list(outs) + list(shapes)),
        out_shape=[_sds(*shape) for shape in outs.values()],
        in_specs=[pl.BlockSpec(memory_space=space[key.startswith("apart ")]) for key in names],
        out_specs=[pl.BlockSpec(memory_space=space[key in apart]) for key in outs],
        scratch_shapes=list(shapes.values()),
        input_output_aliases={names.index(key): list(outs).index(key + "_out") for key in alias},
        compiler_params=_params(),
        cost_estimate=_cost(2**24, 2**25),
        name=name,
    )(*[given[key] for key in names])
    return dict(zip(outs, results))


_OWN = (AZ, NG, G, RAD)
_MORE = (AZ + 2, NG, G, RAD)
_ENDS = (2, 2, 2, SPAN + DEPTH, G, RAD)
_LAST = _CONSTS + _STATE + ["lab", "lab_more", "gone", "base", "gain"]
_FETCH = ["f_low", "f_high", "low", "high"]
_PRIOR = ["lab", "lab_more", "prior", "prior_more"]


def _ring(axis, x, step, closed):
    count = lax.axis_size(axis)
    pairs = [(i, (i + 1) % count) for i in range(count if closed else count - 1)]
    return lax.ppermute(x, axis, pairs if step > 0 else [(b, a) for a, b in pairs])


def _swap(axis, x, start):
    pairs = [(i, i + 1) for i in range(start, lax.axis_size(axis) - 1, 2)]
    return lax.ppermute(x, axis, pairs + [(b, a) for a, b in pairs])


def _around(low_edge, high_edge):
    return _ring("sec", high_edge, 1, True), _ring("sec", low_edge, -1, True)


def shards(labels, exc, a0, prior):
    V = {}
    V["f_low"], V["f_high"] = _around(*_edges(labels, exc, a0))
    got = lax.all_to_all(_prior_send(prior), "sec", 0, 0)
    V.update(zip(_STATE + ["lab"] + _CONSTS, _prepare(labels, exc, a0)))
    edge = (NLATEST + DEPTH, NG, G, RAD)
    outs = {"rows8": _OWN, "q_out": _MORE, "gone": (2, NG, G, RAD), "lab_more": (4, NG, G, RAD)}
    outs.update(e_low=edge, e_high=edge)
    scratch = {"ends": (4, *_ENDS[1:]), "e_low_v": edge, "e_high_v": edge}
    out = _call(_middle_kernel, "field_middle", V, _CONSTS + _STATE, outs, scratch, (), ["e_low", "e_high"], ["f_low", "f_high"])
    V["low"], V["high"] = _around(out["e_low"], out["e_high"])
    V.update(rows8=out["rows8"], q=out["q_out"], gone=out["gone"], lab_more=out["lab_more"])
    outs = {"latest_out": _OWN, "earlier_out": _OWN, "q_out": _MORE}
    names = ["rows8", "q", "nu", "oc", "os"]
    out = _call(_triangle_kernel, "field_triangle", V, names, outs, {"bufs": (2, 2, AZ, G, RAD)})
    for name in _STATE:
        V[name] = out[name + "_out"]
    got, V["latest"] = lax.optimization_barrier((got, V["latest"]))
    V["prior"], V["prior_more"] = _prior_take(got)
    warmth = {name: (AZ + 4, NG, G, RAD) for name in ("t0", "h0", "cap")}
    V.update(_call(_warmth_kernel, "prior_warmth", V, _PRIOR, warmth, {}))
    scratch = {"jac": (2, AZ + 2, G, RAD), "flux": (2, AZ + 2, G, RAD)}
    outs = {"base": _MORE, "gain": _MORE, "part_lo": _END, "part_hi": _END}
    V.update(_call(_ready_kernel, "first_ready", V, ["lab", "lab_more", *warmth], outs, scratch))
    scratch = {"q_out": (3, AZ + 2, G, RAD), "ends": (3, *_ENDS[1:])}
    state = {"t1_out": _MORE, "h1_out": _MORE, "loss_out": _OWN}
    names = _LAST + ["part_lo", "part_hi"]
    outs = {**state, "down": _END, "up": _END, "swap_a": _END, "swap_b": _END, "end_rows": (2, AZ, G, RAD)}
    V.update(_call(_last_ends_kernel, "last_ends", V, names, outs, scratch, fetch=_FETCH))
    V["got_a"], V["got_b"] = _swap("ax", V["swap_a"], 0), _swap("ax", V["swap_b"], 1)
    V.update(t1=V["t1_out"], h1=V["h1_out"], loss=V["loss_out"])
    results = {"closing": (AX, AZ, RAD), "dissipation": (AX, AZ, RAD)}
    scratch.update(rows=(3, AZ, G, RAD), closing_v=(AX, AZ, RAD), dissipation_v=(AX, AZ, RAD))
    names = _LAST + ["end_rows", "t1", "h1", "loss"]
    outs = {**results, **state}
    V.update(
        _call(_last_kernel, "field_last", V, names, outs, scratch, ["t1", "h1", "loss"], list(results), _FETCH)
    )
    V.update(t1=V["t1_out"], h1=V["h1_out"], loss=V["loss_out"])
    names = ["t1", "h1", "down", "up", "got_a", "got_b", "lab", "prior", "loss"]
    shape = (2, 2, AZ + 2, RAD)
    scratch = {"t2": _OWN, "own1": shape, "beside1": shape, "t_lo": _END, "t_hi": _END}
    out = _call(_second_kernel, "second_sweep", V, names, {"blocks": (SEC, NG, RL, G * AZ)}, scratch)
    temperature = _temperature_take(lax.all_to_all(out["blocks"], "sec", 0, 0))
    return V["closing"], V["dissipation"], temperature


def solution(mesh):
    spec = P("ax", "sec", None)
    return jax.shard_map(
        shards,
        mesh=mesh,
        in_specs=(spec, P(None, "ax", "sec", None), spec, spec),
        out_specs=(spec, spec, spec),
        check_vma=False,
    )
```
